32 devices in a mesh: batch: 4 (over x, core), frame: 8 (over z, y).
Axes of the slice: x: 2, y: 2, z: 4, core: 2. Of those that a mesh axis runs over, the one named last changes fastest.
Arguments:
- latents: bfloat16 [4, 4096, 384], P('batch', 'frame'), may hold values from -6 to 6
- time_embed: bfloat16 [4, 4, 384], P('batch'), may hold values from -6 to 6
- text_states: bfloat16 [4, 4, 128, 512], P('batch'), may hold values from -6 to 6
- text_len: int32 [4, 4], P('batch'), may hold values from 4 to 128
- clip_len: int32 [4, 4], P('batch'), may hold values from 1 to 4093, as said below
- cotangent: bfloat16 [4, 4096, 384], P('batch', 'frame'), may hold values from -6 to 6
- w_ada: bfloat16 [384, 2304], replicated, may hold values from -0.3125 to 0.3125
- b_ada: float32 [2304], replicated, may hold values from -3 to 3
- w_qkv: bfloat16 [384, 1152], replicated, may hold values from -0.3125 to 0.3125
- w_ao: bfloat16 [384, 384], replicated, may hold values from -1.25 to 1.25
- gain_cross: float32 [384], replicated, may hold values from 0.1 to 1.9
- w_cq: bfloat16 [384, 384], replicated, may hold values from -0.3125 to 0.3125
- w_ckv: bfloat16 [512, 768], replicated, may hold values from -0.25 to 0.25
- w_co: bfloat16 [384, 384], replicated, may hold values from -0.875 to 0.875
- w_up: bfloat16 [384, 1536], replicated, may hold values from -0.3125 to 0.3125
- w_down: bfloat16 [1536, 384], replicated, may hold values from -0.15625 to 0.15625
Outputs:
- mixed: bfloat16 [4, 4096, 384], P('batch', 'frame')
- grad_latents: bfloat16 [4, 4096, 384], P('batch', 'frame')
- grad_w_ada: float32 [384, 2304], replicated
- grad_b_ada: float32 [2304], replicated
- grad_w_qkv: float32 [384, 1152], replicated
- grad_w_ao: float32 [384, 384], replicated
- grad_gain_cross: float32 [384], replicated
- grad_w_cq: float32 [384, 384], replicated
- grad_w_ckv: float32 [512, 768], replicated
- grad_w_co: float32 [384, 384], replicated
- grad_w_up: float32 [384, 1536], replicated
- grad_w_down: float32 [1536, 384], replicated
The draws below stay inside these ranges and needn't reach their ends.
Inputs may be any that keep to these rules, and one draw needn't show every extreme that they name: `clip_len`: in each group the 4 lengths sum to at most 4096; one clip, at a place drawn from the seed, begins within the first 512 frames and ends within the last 512; the frames after the clips are padding. In one group, drawn from the seed, there is no padding and the other clips have one frame each.
All inputs are finite; a program needn't handle non-finite values.
Results may differ from the reference program's by a relative error of at most 0.025.
Values may be sent and summed in bfloat16 or wider, within the bound.
A program may use at most 320 MiB of HBM per device.

```python
import math
import jax
import jax.numpy as jnp
from jax import lax

D = 384
HEADS = 6
DH = 64
FF = 1536
TD = 512
CLIPS = 4
TXT = 128
F_DEV = 512
GROUPS = 4
TG = 4096


def draw_clip_len(key, part):
    key = jax.random.fold_in(key, 11)
    short_key, pad_key, place_key, group_key = jax.random.split(key, 4)
    full_group = jax.random.randint(group_key, (), 0, GROUPS, dtype=jnp.int32)
    group_index = jnp.arange(GROUPS, dtype=jnp.int32)[:, None]
    is_full = group_index == full_group
    shorts = jax.random.randint(short_key, (GROUPS, CLIPS), 1, F_DEV // 8 + 1, dtype=jnp.int32)
    shorts = jnp.where(is_full, 1, shorts).astype(jnp.int32)
    padding = jax.random.randint(pad_key, (GROUPS, 1), 0, F_DEV // 2 + 1, dtype=jnp.int32)
    padding = jnp.where(is_full, 0, padding).astype(jnp.int32)
    place = jax.random.randint(place_key, (GROUPS, 1), 0, CLIPS, dtype=jnp.int32)
    slot_index = jnp.arange(CLIPS, dtype=jnp.int32)[None, :]
    at_place = slot_index == place
    others = jnp.sum(jnp.where(at_place, 0, shorts), axis=1, keepdims=True).astype(jnp.int32)
    longest = (TG - padding - others).astype(jnp.int32)
    return jnp.where(at_place, longest, shorts).astype(jnp.int32)


def place_ends(entries, key, low, largest):
    longest = entries.shape.index(max(entries.shape))
    spots = []
    for shift in (0, 1):
        where = [jax.random.randint(jax.random.fold_in(key, axis), (), 0, length) for axis, length in enumerate(entries.shape)]
        where[longest] = (where[longest] + shift) % entries.shape[longest]
        spots.append(tuple(where))
    return entries.at[spots[0]].set(low).at[spots[1]].set(largest)


def level_of(own_key, dims, cuts, least, top_value):
    level, own = 1.0, jax.random.fold_in(own_key, 6)
    for dim, shards_of in cuts:
        draws = jnp.exp(jax.random.uniform(jax.random.fold_in(own, dim), (shards_of,), jnp.float32, least / len(cuts), top_value / len(cuts)))
        level = level * jnp.repeat(draws, dims[dim] // shards_of).reshape([-1 if axis == dim else 1 for axis in range(len(dims))])
    return level


def scatter_about(rng, shape, spread, most, shards=(), held_as=jnp.bfloat16):
    factor_of = level_of(rng, shape, shards, -0.22, 0.18) if shards else 1.0
    values = jax.random.normal(rng, shape, jnp.float32) * spread * factor_of
    return jnp.minimum(jnp.maximum(values, -most), most).astype(held_as)


def setup_inputs(seed: int = 0) -> dict:
    seeds = jax.random.split(jax.random.key(seed), 17)
    latents = scatter_about(seeds[0], (GROUPS, TG, D), 1.0, 6.0, ((0, 4), (1, 8)))
    time_embed = scatter_about(seeds[1], (GROUPS, CLIPS, D), 1.0, 6.0, ((0, 4),))
    text_states = scatter_about(seeds[2], (GROUPS, CLIPS, TXT, TD), 1.0, 6.0, ((0, 4),))
    text_len = place_ends(jax.random.randint(seeds[3], (GROUPS, CLIPS), 4, TXT + 1), jax.random.fold_in(seeds[3], 1), 4, TXT).astype(jnp.int32)
    clip_len = draw_clip_len(jax.random.fold_in(seeds[16], 71), 0)
    cotangent = scatter_about(seeds[5], (GROUPS, TG, D), 1.0, 6.0, ((0, 4), (1, 8)))
    w_ada = scatter_about(seeds[6], (D, 6 * D), D ** -0.5, 0.3125)
    b_ada = scatter_about(seeds[7], (6 * D,), 0.5, 3.0, (), jnp.float32)
    w_qkv = scatter_about(seeds[8], (D, 3 * D), D ** -0.5, 0.3125)
    w_ao = scatter_about(seeds[9], (D, D), (D // 16) ** -0.5, 1.25)
    gain_cross = jnp.clip(1.0 + 0.18 * jax.random.normal(seeds[10], (D,), jnp.float32), 0.1, 1.9)
    w_cq = scatter_about(seeds[11], (D, D), D ** -0.5, 0.3125)
    w_ckv = scatter_about(seeds[12], (TD, 2 * D), TD ** -0.5, 0.25)
    w_co = scatter_about(seeds[13], (D, D), (D // 8) ** -0.5, 0.875)
    w_up = scatter_about(seeds[14], (D, FF), D ** -0.5, 0.3125)
    w_down = scatter_about(seeds[15], (FF, D), FF ** -0.5, 0.15625)
    return {"latents": latents, "time_embed": time_embed, "text_states": text_states, "text_len": text_len, "clip_len": clip_len, "cotangent": cotangent, "w_ada": w_ada, "b_ada": b_ada, "w_qkv": w_qkv, "w_ao": w_ao, "gain_cross": gain_cross, "w_cq": w_cq, "w_ckv": w_ckv, "w_co": w_co, "w_up": w_up, "w_down": w_down}


highest = lax.Precision.HIGHEST
eps_norm = 1e-06
neg_fill = -1e+30

@jax.custom_vjp
def low(v):
    return lax.optimization_barrier(v.astype(jnp.bfloat16)).astype(jnp.float32)

@jax.custom_vjp
def low_back(v):
    return v

def low_keep(v):
    return (low(v), None)

def low_pass(kept, grad):
    return (grad,)

def back_keep(v):
    return (v, None)

def back_low(kept, grad):
    return (low(grad),)
low.defvjp(low_keep, low_pass)
low_back.defvjp(back_keep, back_low)

def layer_norm(values):
    center = values - lax.optimization_barrier(jnp.mean(values, axis=-1, keepdims=True))
    return center * lax.rsqrt(lax.optimization_barrier(jnp.mean(center * center, axis=-1, keepdims=True)) + eps_norm)

def clip_index(lengths, positions):
    clip_ends = jnp.cumsum(lengths).astype(jnp.int32)
    return lax.optimization_barrier(jnp.sum((positions[:, None] >= clip_ends[None, :]).astype(jnp.int32), axis=1)).astype(jnp.int32)

def split_heads(matrix):
    return matrix.reshape(matrix.shape[0], HEADS, DH).transpose(1, 0, 2)

def join_heads(stacked):
    return stacked.transpose(1, 0, 2).reshape(stacked.shape[1], HEADS * DH)

def attend(queries, keys, values, query_ids, key_ids, key_live):
    row_total = queries.shape[0]
    block_size = math.gcd(row_total, 512)
    blocks = row_total // block_size
    keys_h = split_heads(keys)
    values_h = split_heads(values)
    queries_b = split_heads(queries).reshape(HEADS, blocks, block_size, DH).transpose(1, 0, 2, 3)
    ids_b = query_ids.reshape(blocks, block_size)

    def per_block(element):
        queries_h, ids_here = element
        scores = jnp.einsum('hqd,hkd->hqk', queries_h, keys_h, precision=highest) * DH ** (-0.5)
        scores = low_back(scores)
        allowed = (ids_here[:, None] == key_ids[None, :]) & key_live[None, :]
        scores = jnp.where(allowed[None], scores, neg_fill)
        probs = jax.nn.softmax(scores, axis=-1)
        return jnp.einsum('hqk,hkd->hqd', low(probs), values_h, precision=highest)
    result = lax.map(jax.checkpoint(per_block), (queries_b, ids_b))
    return join_heads(result.transpose(1, 0, 2, 3).reshape(HEADS, row_total, DH))

def block_forward(latents, time_embed, text_rows, text_len, clip_len, weights):
    w_ada, b_ada, w_qkv, w_ao, gain_cross, w_cq, w_ckv, w_co, w_up, w_down = weights
    positions = jnp.arange(TG, dtype=jnp.int32)
    frame_clip = clip_index(clip_len, positions)
    frame_valid = (frame_clip < CLIPS).astype(jnp.float32)[:, None]
    onehot = (frame_clip[:, None] == jnp.arange(CLIPS, dtype=jnp.int32)[None, :]).astype(jnp.float32)
    modulation = jnp.dot(low(jax.nn.silu(time_embed)), w_ada, precision=highest) + b_ada
    frame_mod = jnp.dot(onehot, modulation, precision=highest)
    shift_attn, scale_attn, gate_attn, shift_mlp, scale_mlp, gate_mlp = jnp.split(frame_mod, 6, axis=1)
    modulated = low(layer_norm(latents) * (1.0 + scale_attn) + shift_attn)
    projected = low(low_back(jnp.dot(modulated, w_qkv, precision=highest)))
    queries, keys, values = jnp.split(projected, 3, axis=1)
    attention = low(low_back(attend(queries, keys, values, frame_clip, frame_clip, frame_clip < CLIPS)))
    branch_attn = low_back(jnp.dot(attention, w_ao, precision=highest))
    after_attn = latents + gate_attn * branch_attn * frame_valid
    cross_in = low(layer_norm(after_attn) * gain_cross)
    cross_queries = low(low_back(jnp.dot(cross_in, w_cq, precision=highest)))
    text_kv = low(jnp.dot(text_rows, w_ckv, precision=highest))
    text_keys, text_values = jnp.split(text_kv, 2, axis=1)
    rows = jnp.arange(CLIPS * TXT, dtype=jnp.int32)
    text_clip = (rows // TXT).astype(jnp.int32)
    text_live = rows % TXT < jnp.repeat(text_len, TXT)
    cross = low(low_back(attend(cross_queries, text_keys, text_values, frame_clip, text_clip, text_live)))
    branch_cross = low_back(jnp.dot(cross, w_co, precision=highest))
    after_cross = after_attn + branch_cross * frame_valid
    mlp_in = low(layer_norm(after_cross) * (1.0 + scale_mlp) + shift_mlp)
    hidden = low_back(jnp.dot(mlp_in, w_up, precision=highest))
    activated = low(jax.nn.gelu(hidden, approximate=True))
    branch_mlp = low_back(jnp.dot(activated, w_down, precision=highest))
    return after_cross + gate_mlp * branch_mlp * frame_valid

def reference(latents, time_embed, text_states, text_len, clip_len, cotangent, w_ada, b_ada, w_qkv, w_ao, gain_cross, w_cq, w_ckv, w_co, w_up, w_down):
    weights = tuple((weight.astype(jnp.float32) for weight in (w_ada, b_ada, w_qkv, w_ao, gain_cross, w_cq, w_ckv, w_co, w_up, w_down)))
    text_flat = text_states.astype(jnp.float32).reshape(GROUPS, CLIPS * TXT, TD)

    def per_group(summed, element):
        group_latents, group_time, group_text, group_tlen, group_clen, group_cot = element

        def forward(latent_in, weight_in):
            return block_forward(latent_in, group_time, group_text, group_tlen, group_clen, weight_in)
        output, pull = jax.vjp(forward, group_latents, weights)
        grad_input, grad_weights = pull(group_cot)
        summed = jax.tree.map(lambda before, added: before + added, summed, grad_weights)
        return (summed, (output.astype(jnp.bfloat16), grad_input.astype(jnp.bfloat16)))
    zeros = tuple((jnp.zeros_like(weight) for weight in weights))
    summed, (outputs, grad_inputs) = lax.scan(per_group, zeros, (latents.astype(jnp.float32), time_embed.astype(jnp.float32), text_flat, text_len, clip_len, cotangent.astype(jnp.float32)))
    return (outputs, grad_inputs, summed[0], summed[1], summed[2], summed[3], summed[4], summed[5], summed[6], summed[7], summed[8], summed[9])
```

```python
import functools

import jax
import jax.numpy as jnp
from jax import lax
from jax.experimental import pallas as pl
from jax.experimental.pallas import tpu as pltpu
from jax.sharding import PartitionSpec as P

HEADS = 6
LANES = 128
MASKED = -1e30

f32 = jnp.float32
bf16 = jnp.bfloat16
highest = lax.Precision.HIGHEST
eps_norm = 1e-06
MESH = pl.DeviceIdType.MESH

NT = (((1,), (1,)), ((), ()))
NN = (((1,), (0,)), ((), ()))
TN = (((0,), (0,)), ((), ()))


def dg(left, right, dims):
    return lax.dot_general(left, right, dims, preferred_element_type=f32)


def layer_norm(values):
    center = values - jnp.mean(values, axis=-1, keepdims=True)
    inverse = lax.rsqrt(jnp.mean(center * center, axis=-1, keepdims=True) + eps_norm)
    return (center * inverse, inverse)


def norm_back(grad, normed, inverse):
    mean_grad = jnp.mean(grad, axis=-1, keepdims=True)
    mean_prod = jnp.mean(grad * normed, axis=-1, keepdims=True)
    return (grad - mean_grad - normed * mean_prod) * inverse


def pieces(value):
    high = value.astype(bf16)
    rest = value - high.astype(f32)
    middle = rest.astype(bf16)
    low = (rest - middle.astype(f32)).astype(bf16)
    return high, middle, low


def nearest(step, me, count):
    lower = me < count // 2
    mine = jnp.where(lower, me, count - 1 - me)
    index = jnp.where(step - 1 < mine, step - 1, step)
    return jnp.where(lower, index, count - 1 - index)


def place():
    batch = lax.axis_index("batch")
    frame = lax.axis_index("frame")
    side = lax.rem(frame, 2)
    column = lax.div(frame, 2)
    return batch, frame, side, column, frame + 1 - 2 * side


def greet(batch, side, column, count, peer):
    barrier = pltpu.get_barrier_semaphore()
    pl.semaphore_signal(barrier, inc=1, device_id=(batch, peer), device_id_type=MESH)
    for step in range(1, count):
        other = nearest(step, column, count)
        pl.semaphore_signal(
            barrier, inc=1, device_id=(batch, 2 * other + side), device_id_type=MESH
        )
    pl.semaphore_wait(barrier, count)


def forward_kernel(
    frames,
    count,
    mod_own,
    w_qp,
    w_kp,
    w_vp,
    key_aug,
    query_aug,
    attention,
    stats,
    mod_all,
    mod_peer,
    pairs,
    queries,
    total,
    tops,
    part_out,
    part_in,
    stat_out,
    stat_in,
    send_sem,
    recv_sem,
):
    batch, frame, side, column, peer = place()
    head_size = mod_own.shape[1] // HEADS
    greet(batch, side, column, count, peer)

    def to_peer(source, target, slot):
        return pltpu.make_async_remote_copy(
            src_ref=source,
            dst_ref=target,
            send_sem=send_sem.at[slot],
            recv_sem=recv_sem.at[slot],
            device_id=(batch, peer),
            device_id_type=MESH,
        )

    def to_column(step, other, slot):
        return pltpu.make_async_remote_copy(
            src_ref=mod_own,
            dst_ref=mod_all.at[slot],
            send_sem=send_sem.at[2 + step],
            recv_sem=recv_sem.at[3 + slot],
            device_id=(batch, 2 * other + side),
            device_id_type=MESH,
        )

    swap = to_peer(mod_own, mod_peer, 0)
    sends = [
        to_column(step, nearest(step, column, count), column) for step in range(1, count)
    ]
    for index, send in enumerate(sends):
        send.start()
        if index == 0:
            swap.start()
    mod_all[column] = mod_own[...]
    total[...] = jnp.zeros_like(total)
    tops[...] = jnp.full_like(tops, -1e38)
    ones = (lax.broadcasted_iota(jnp.int32, (frames, LANES), 1) >= head_size).astype(bf16)

    def make_queries(half, source):
        rows = pl.ds(half * frames, frames)
        flat = dg(source, w_qp[...], NN).astype(bf16)
        extra = query_aug[rows, :]
        for head in range(HEADS):
            queries[head, rows, :] = flat[:, head * LANES : (head + 1) * LANES] * 0.125 + extra

    def make_keys(block):
        source = mod_all[block]
        flat = dg(source, w_kp[...], NN).astype(bf16)
        extra = key_aug[block]
        for head in range(HEADS):
            pairs[block, 0, head] = flat[:, head * LANES : (head + 1) * LANES] + extra
        flat = dg(source, w_vp[...], NN).astype(bf16)
        for head in range(HEADS):
            pairs[block, 1, head] = flat[:, head * LANES : (head + 1) * LANES] + ones

    def attend(half, block):
        rows = pl.ds(half * frames, frames)

        def scores(head):
            now = dg(pairs[block, 0, head], queries[head, rows, :], NT)
            return now, jnp.max(now, axis=0, keepdims=True)

        ahead = scores(0)
        for head in range(HEADS):
            now, top = ahead
            if head + 1 < HEADS:
                ahead = scores(head + 1)
            before = tops[head, :1, rows]
            new = jnp.maximum(before, top)
            probs = jnp.exp(now - new).astype(bf16)
            total[head, :, rows] = total[head, :, rows] * jnp.exp(before - new) + dg(
                pairs[block, 1, head], probs, TN
            )
            tops[head, :, rows] = jnp.broadcast_to(new, (8, frames))

    def arrive(step):
        block = nearest(step, column, count)
        to_column(step, block, block).wait_recv()
        make_keys(block)
        return block

    make_queries(0, mod_own[...])
    make_keys(column)
    attend(0, column)
    swap.wait()
    make_queries(1, mod_peer[...])
    attend(1, column)

    def per_block(step, unused):
        block = arrive(step)
        attend(0, block)
        attend(1, block)
        return unused

    lax.fori_loop(1, count - 1, per_block, 0)
    block = arrive(count - 1)
    attend(1, block)
    there = pl.ds(frames, frames)
    for head in range(HEADS):
        part_out[head * head_size : (head + 1) * head_size, :] = total[
            head, :head_size, there
        ].astype(bf16)
        stat_out[head : head + 1, :] = tops[head, :1, there]
        stat_out[8 + head : 9 + head, :] = total[head, head_size : head_size + 1, there]
    parts = to_peer(part_out, part_in, 1)
    numbers = to_peer(stat_out, stat_in, 2)
    numbers.start()
    parts.start()
    attend(0, block)
    numbers.wait()
    parts.wait()
    here = pl.ds(0, frames)
    joined = []
    logs = []
    for head in range(HEADS):
        mine, theirs = tops[head, :1, here], stat_in[head : head + 1, :]
        new = jnp.maximum(mine, theirs)
        left, right = jnp.exp(mine - new), jnp.exp(theirs - new)
        row_sum = (
            total[head, head_size : head_size + 1, here] * left
            + stat_in[8 + head : 9 + head, :] * right
        )
        logs.append(new + jnp.log(row_sum))
        scale = 1.0 / row_sum
        joined.append(
            total[head, :head_size, here] * (left * scale)
            + part_in[head * head_size : (head + 1) * head_size, :].astype(f32) * (right * scale)
        )
    attention[...] = jnp.concatenate(joined, axis=0).T.astype(bf16)
    rows = [piece for log in logs for piece in log_pieces(log)]
    rows.append(jnp.zeros((LANES - len(rows), frames), f32))
    stats[...] = jnp.concatenate(rows, axis=0).T.astype(bf16)
    for send in sends:
        send.wait_send()


def log_pieces(log):
    high, middle, low = pieces(-log)
    return [high.astype(f32), middle.astype(f32), low.astype(f32)]


def forward_attention(modulated, w_q, w_k, w_v, key_aug, query_aug):
    frames, width = modulated.shape
    count = key_aug.shape[0]
    head_size = width // HEADS
    vmem = pl.BlockSpec(memory_space=pltpu.VMEM)
    shapes = (
        jax.ShapeDtypeStruct((frames, width), bf16),
        jax.ShapeDtypeStruct((frames, LANES), bf16),
        jax.ShapeDtypeStruct((count, frames, width), bf16),
        jax.ShapeDtypeStruct((frames, width), bf16),
        jax.ShapeDtypeStruct((count, 2, HEADS, frames, LANES), bf16),
        jax.ShapeDtypeStruct((HEADS, 2 * frames, LANES), bf16),
    )
    return pl.pallas_call(
        functools.partial(forward_kernel, frames, count),
        name="attention_forward",
        out_shape=shapes,
        in_specs=[vmem] * 6,
        out_specs=(vmem,) * 6,
        scratch_shapes=[
            pltpu.VMEM((HEADS, LANES, 2 * frames), f32),
            pltpu.VMEM((HEADS, 8, 2 * frames), f32),
            pltpu.VMEM((width, frames), bf16),
            pltpu.VMEM((width, frames), bf16),
            pltpu.VMEM((16, frames), f32),
            pltpu.VMEM((16, frames), f32),
            pltpu.SemaphoreType.DMA((2 + count,)),
            pltpu.SemaphoreType.DMA((3 + count,)),
        ],
        compiler_params=pltpu.CompilerParams(
            collective_id=1, has_side_effects=True, vmem_limit_bytes=62 * 2**20
        ),
    )(modulated, w_q, w_k, w_v, key_aug, query_aug)


def backward_kernel(
    frames,
    count,
    grad_att,
    attention,
    stats,
    mod_all,
    mod_peer,
    pairs,
    queries_in,
    w_qkv,
    spread_q,
    spread_o,
    sum_heads,
    grad_mod,
    grad_w,
    pack_out,
    pack_in,
    queries,
    grads,
    query_grad,
    key_grad,
    value_grad,
    flat_kv,
    part_out,
    part_in,
    peer_out,
    peer_in,
    held,
    held_sem,
    send_sem,
    recv_sem,
):
    batch, frame, side, column, peer = place()
    width = grad_att.shape[1]
    head_size = width // HEADS

    def block_at(step):
        return jnp.where(step == count, column, nearest(count - step, column, count))

    def fetch(step):
        slot = lax.rem(step - 1, 2)
        return pltpu.make_async_copy(
            pairs.at[block_at(step)], held.at[slot], held_sem.at[slot]
        )

    fetch(1).start()
    fetch(2).start()
    greet(batch, side, column, count, peer)

    def to_peer(source, target, slot):
        return pltpu.make_async_remote_copy(
            src_ref=source,
            dst_ref=target,
            send_sem=send_sem.at[slot],
            recv_sem=recv_sem.at[slot],
            device_id=(batch, peer),
            device_id_type=MESH,
        )

    def to_owner(step, owner, slot):
        return pltpu.make_async_remote_copy(
            src_ref=part_out.at[step],
            dst_ref=part_in.at[slot],
            send_sem=send_sem.at[2 + step],
            recv_sem=recv_sem.at[2 + slot],
            device_id=(batch, 2 * owner + side),
            device_id_type=MESH,
        )

    grad_now = grad_att[...]
    product = grad_now.astype(f32) * attention[...].astype(f32)
    high, middle, low = pieces(product)
    delta = (
        dg(high, sum_heads[...], NN) + dg(middle, sum_heads[...], NN) + dg(low, sum_heads[...], NN)
    )
    high, middle, low = pieces(-delta)
    pack_out[:, :width] = grad_now
    pack_out[:, width : width + LANES] = stats[...]
    pack_out[:, width + LANES : width + 2 * LANES] = high
    pack_out[:, width + 2 * LANES : width + 3 * LANES] = middle
    pack_out[:, width + 3 * LANES :] = low
    swap = to_peer(pack_out, pack_in, 0)
    swap.start()
    query_grad[...] = jnp.zeros_like(query_grad)

    def prepare(half, source):
        rows = pl.ds(half * frames, frames)
        wide = dg(source[:, :width], spread_o[:width, :], NN)
        wide += dg(source[:, width + LANES :], spread_o[width:, :], NN)
        extra = dg(source[:, width : width + LANES], spread_q[...], NN).astype(bf16)
        wide = wide.astype(bf16)
        for head in range(HEADS):
            lanes = slice(head * LANES, (head + 1) * LANES)
            grads[head, rows, :] = wide[:, lanes]
            queries[head, rows, :] = queries_in[head, rows, :] + extra[:, lanes]

    def differentiate(half, slot, first):
        rows = pl.ds(half * frames, frames)
        for head in range(HEADS):
            key, value = held[slot, 0, head], held[slot, 1, head]
            query, grad = queries[head, rows, :], grads[head, rows, :]
            probs = jnp.exp(dg(key, query, NT))
            dscore = (probs * dg(value, grad, NT)).astype(bf16)
            probs = probs.astype(bf16)
            more_k, more_v = dg(dscore, query, NN), dg(probs, grad, NN)
            if first:
                key_grad[slot, head] = more_k
                value_grad[slot, head] = more_v
            else:
                key_grad[slot, head] += more_k
                value_grad[slot, head] += more_v
            query_grad[head, :, rows] += dg(key, dscore, TN)

    def finish_keys(block, slot):
        for kind, source in enumerate((key_grad, value_grad)):
            for pair in range(HEADS // 2):
                start = kind * width + pair * LANES
                flat_kv[:, start : start + LANES] = jnp.concatenate(
                    [
                        source[slot, 2 * pair][:, :head_size],
                        source[slot, 2 * pair + 1][:, :head_size],
                    ],
                    axis=1,
                ).astype(bf16)
        flat = flat_kv[...]
        return dg(flat, w_qkv[:, width:], NT), dg(mod_all[block], flat, TN)

    def finish_queries(half, source):
        rows = pl.ds(half * frames, frames)
        flat = jnp.concatenate(
            [query_grad[head, :head_size, rows] for head in range(HEADS)], axis=0
        )
        flat = (flat * 0.125).T.astype(bf16)
        return dg(flat, w_qkv[:, :width], NT), dg(source, flat, TN)

    def send_block(step, slot, first):
        block = block_at(step)
        part, weight = finish_keys(block, slot)
        part_out[step] = part.astype(bf16)
        to_owner(step, block, column).start()
        if first:
            grad_w[:, width:] = weight
        else:
            grad_w[:, width:] += weight

        @pl.when(step + 2 <= count)
        def _():
            fetch(step + 2).start()

    prepare(0, pack_out[...])
    fetch(1).wait()
    differentiate(0, 0, True)
    fetch(2).wait()
    differentiate(0, 1, True)
    swap.wait()
    prepare(1, pack_in[...])
    differentiate(1, 0, False)
    send_block(1, 0, True)
    differentiate(1, 1, False)
    send_block(2, 1, False)

    def per_block(step, unused):
        slot = lax.rem(step - 1, 2)
        fetch(step).wait()
        differentiate(0, slot, True)
        differentiate(1, slot, False)
        send_block(step, slot, False)
        return unused

    lax.fori_loop(3, count, per_block, 0)
    slot = (count - 1) % 2
    fetch(count).wait()
    differentiate(1, slot, True)
    part, weight = finish_queries(1, mod_peer[...])
    peer_out[...] = part.astype(bf16)
    back = to_peer(peer_out, peer_in, 1)
    back.start()
    grad_w[:, :width] = weight
    differentiate(0, slot, False)
    part, weight = finish_keys(column, slot)
    grad_w[:, width:] += weight
    mine, weight = finish_queries(0, mod_all[column])
    grad_w[:, :width] += weight
    grad_mod[...] = part + mine

    def receive(step, unused):
        other = nearest(step, column, count)
        to_owner(step, other, other).wait_recv()
        grad_mod[...] += part_in[other].astype(f32)
        return unused

    lax.fori_loop(1, count, receive, 0)
    back.wait()
    grad_mod[...] += peer_in[...].astype(f32)

    def sent(step, unused):
        to_owner(step, column, column).wait_send()
        return unused

    lax.fori_loop(1, count, sent, 0)


def backward_attention(
    grad_att, attention, stats, mod_all, mod_peer, pairs, queries, w_qkv, spreads
):
    frames, width = grad_att.shape
    count = pairs.shape[0]
    vmem = pl.BlockSpec(memory_space=pltpu.VMEM)
    return pl.pallas_call(
        functools.partial(backward_kernel, frames, count),
        name="attention_backward",
        out_shape=(
            jax.ShapeDtypeStruct((frames, width), f32),
            jax.ShapeDtypeStruct((width, 3 * width), f32),
        ),
        in_specs=[vmem] * 5 + [pl.BlockSpec(memory_space=pl.ANY)] + [vmem] * 5,
        out_specs=(vmem,) * 2,
        scratch_shapes=[
            pltpu.VMEM((frames, width + 4 * LANES), bf16),
            pltpu.VMEM((frames, width + 4 * LANES), bf16),
            pltpu.VMEM((HEADS, 2 * frames, LANES), bf16),
            pltpu.VMEM((HEADS, 2 * frames, LANES), bf16),
            pltpu.VMEM((HEADS, LANES, 2 * frames), f32),
            pltpu.VMEM((2, HEADS, frames, LANES), f32),
            pltpu.VMEM((2, HEADS, frames, LANES), f32),
            pltpu.VMEM((frames, 2 * width), bf16),
            pltpu.VMEM((count, frames, width), bf16),
            pltpu.VMEM((count, frames, width), bf16),
            pltpu.VMEM((frames, width), bf16),
            pltpu.VMEM((frames, width), bf16),
            pltpu.VMEM((2, 2, HEADS, frames, LANES), bf16),
            pltpu.SemaphoreType.DMA((2,)),
            pltpu.SemaphoreType.DMA((2 + count,)),
            pltpu.SemaphoreType.DMA((2 + count,)),
        ],
        compiler_params=pltpu.CompilerParams(
            collective_id=2, has_side_effects=True, vmem_limit_bytes=62 * 2**20
        ),
    )(grad_att, attention, stats, mod_all, mod_peer, pairs, queries, w_qkv, *spreads)


def ids_at(positions, clip_ends):
    return jnp.sum((positions[..., None] >= clip_ends).astype(jnp.int32), axis=-1)


def split_heads(matrix, head_count):
    return matrix.reshape(matrix.shape[0], head_count, matrix.shape[1] // head_count).transpose(
        1, 0, 2
    )


def join_heads(stacked):
    return stacked.transpose(1, 0, 2).reshape(stacked.shape[1], stacked.shape[0] * stacked.shape[2])


def masked_scores(queries_h, keys_h, key_ids, query_ids, clip_count):
    head_size = queries_h.shape[2]
    scores = jnp.einsum(
        "hqd,hkd->hqk", queries_h, keys_h, preferred_element_type=jnp.float32
    ) * head_size ** (-0.5)
    allowed = (query_ids[:, None] == key_ids[None, :]) & (key_ids[None, :] < clip_count)
    return jnp.where(allowed[None], scores, MASKED)


def head_pad(weight):
    width = weight.shape[0]
    heads = weight.reshape(width, HEADS, -1)
    return jnp.pad(heads, ((0, 0), (0, 0), (0, LANES - heads.shape[2]))).reshape(
        width, HEADS * LANES
    )


def spread_matrices(width):
    head_size = width // HEADS
    lane = jnp.arange(HEADS * LANES, dtype=jnp.int32)[None, :]
    head, inner = lane // LANES, lane % LANES
    row = jnp.arange(LANES, dtype=jnp.int32)[:, None]
    spread_q = (row < 3 * HEADS) & (head == row // 3) & (inner == head_size + 4 + row % 3)
    row = jnp.arange(width, dtype=jnp.int32)[:, None]
    spread_o = [(head == row // head_size) & (inner == row % head_size)]
    row = jnp.arange(LANES, dtype=jnp.int32)[:, None]
    for piece in range(3):
        spread_o.append((row == head) & (inner == head_size + piece))
    column = jnp.arange(LANES, dtype=jnp.int32)[None, :]
    sum_heads = jnp.arange(width, dtype=jnp.int32)[:, None] // head_size == column
    return (
        spread_q.astype(bf16),
        jnp.concatenate(spread_o, axis=0).astype(bf16),
        sum_heads.astype(bf16),
    )


def per_device(
    latents,
    time_embed,
    text_states,
    text_len,
    clip_len,
    cotangent,
    w_ada,
    b_ada,
    w_qkv,
    w_ao,
    gain_cross,
    w_cq,
    w_ckv,
    w_co,
    w_up,
    w_down,
):
    frames = latents.shape[1]
    width = latents.shape[2]
    clip_count = time_embed.shape[1]
    text_slots = text_states.shape[2]
    head_size = width // HEADS
    score_scale = head_size ** (-0.5)
    frame = lax.axis_index("frame")
    count = lax.axis_size("frame") // 2
    side = frame % 2
    clip_ends = jnp.cumsum(clip_len[0])
    clips = jnp.arange(clip_count, dtype=jnp.int32)
    inner = jnp.arange(frames, dtype=jnp.int32)
    local_ids = ids_at(frame * frames + inner, clip_ends)
    peer_ids = ids_at((frame + 1 - 2 * side) * frames + inner, clip_ends)
    frame_valid = (local_ids < clip_count).astype(f32)[:, None]
    onehot = (local_ids[:, None] == clips[None, :]).astype(f32)

    lane = jnp.arange(LANES, dtype=jnp.int32)
    starts = (2 * jnp.arange(count, dtype=jnp.int32) + side) * frames
    key_ids = ids_at(starts[:, None] + inner[None, :], clip_ends)[..., None]
    masks = (lane >= head_size) & (lane < head_size + clip_count)
    key_aug = jnp.where(
        masks,
        jnp.where(key_ids == lane - head_size, 0.0, MASKED),
        jnp.where((lane >= head_size + 4) & (lane < head_size + 7), 1.0, 0.0),
    ).astype(bf16)
    query_ids = jnp.concatenate([local_ids, peer_ids])[:, None]
    query_aug = (masks & (query_ids == lane - head_size)).astype(bf16)

    inputs = latents[0].astype(f32)
    time_low = jax.nn.silu(time_embed[0].astype(f32)).astype(bf16)
    modulation = jnp.dot(time_low, w_ada, preferred_element_type=f32) + b_ada
    frame_mod = jnp.dot(onehot, modulation, precision=highest)
    shift_attn, scale_attn, gate_attn, shift_mlp, scale_mlp, gate_mlp = jnp.split(
        frame_mod, 6, axis=1
    )
    normed_attn, inverse_attn = layer_norm(inputs)
    modulated = (normed_attn * (1.0 + scale_attn) + shift_attn).astype(bf16)
    attention, stats, mod_all, mod_peer, pairs, queries = forward_attention(
        modulated,
        head_pad(w_qkv[:, :width]),
        head_pad(w_qkv[:, width : 2 * width]),
        head_pad(w_qkv[:, 2 * width :]),
        key_aug,
        query_aug,
    )

    branch_attn = jnp.dot(attention, w_ao, preferred_element_type=f32)
    after_attn = inputs + gate_attn * branch_attn * frame_valid
    normed_cross, inverse_cross = layer_norm(after_attn)
    cross_in = (normed_cross * gain_cross).astype(bf16)
    cross_queries = jnp.dot(cross_in, w_cq, preferred_element_type=f32).astype(bf16)
    text_rows = text_states[0].reshape(clip_count * text_slots, text_states.shape[3])
    text_kv = jnp.dot(text_rows, w_ckv, preferred_element_type=f32).astype(bf16)
    text_keys_h = split_heads(text_kv[:, :width], HEADS)
    text_values_h = split_heads(text_kv[:, width:], HEADS)
    slot_rows = jnp.arange(clip_count * text_slots, dtype=jnp.int32)
    text_clip = slot_rows // text_slots
    text_live = slot_rows % text_slots < jnp.repeat(text_len[0], text_slots)
    text_clip = jnp.where(text_live, text_clip, clip_count)
    cross_queries_h = split_heads(cross_queries, HEADS)
    cross_scores = masked_scores(cross_queries_h, text_keys_h, text_clip, local_ids, clip_count)
    cross_probs = jax.nn.softmax(cross_scores, axis=-1)
    cross_low = cross_probs.astype(bf16)
    cross = join_heads(
        jnp.einsum("hqk,hkd->hqd", cross_low, text_values_h, preferred_element_type=f32)
    ).astype(bf16)
    branch_cross = jnp.dot(cross, w_co, preferred_element_type=f32)
    after_cross = after_attn + branch_cross * frame_valid
    normed_mlp, inverse_mlp = layer_norm(after_cross)
    mlp_in = (normed_mlp * (1.0 + scale_mlp) + shift_mlp).astype(bf16)
    hidden = jnp.dot(mlp_in, w_up, preferred_element_type=f32)
    activated, gelu_pull = jax.vjp(lambda value: jax.nn.gelu(value, approximate=True), hidden)
    activated = activated.astype(bf16)
    branch_mlp = jnp.dot(activated, w_down, preferred_element_type=f32)
    mixed = after_cross + gate_mlp * branch_mlp * frame_valid
    grad_out = cotangent[0].astype(f32)
    grad_mlp = (grad_out * gate_mlp * frame_valid).astype(bf16)
    grad_gate_mlp = grad_out * branch_mlp * frame_valid
    grad_w_down = jnp.dot(activated.T, grad_mlp, preferred_element_type=f32)
    grad_act = jnp.dot(grad_mlp, w_down.T, preferred_element_type=f32)
    grad_hidden = gelu_pull(grad_act)[0].astype(bf16)
    grad_w_up = jnp.dot(mlp_in.T, grad_hidden, preferred_element_type=f32)
    grad_mlp_in = jnp.dot(grad_hidden, w_up.T, preferred_element_type=f32)
    grad_cross_out = grad_out + norm_back(grad_mlp_in * (1.0 + scale_mlp), normed_mlp, inverse_mlp)
    grad_branch_cross = (grad_cross_out * frame_valid).astype(bf16)
    grad_w_co = jnp.dot(cross.T, grad_branch_cross, preferred_element_type=f32)
    grad_cross_h = split_heads(
        jnp.dot(grad_branch_cross, w_co.T, preferred_element_type=f32).astype(bf16), HEADS
    )
    cross_dprob = jnp.einsum(
        "hqd,hkd->hqk", grad_cross_h, text_values_h, preferred_element_type=f32
    )
    cross_dscore = (
        cross_probs * (cross_dprob - jnp.sum(cross_probs * cross_dprob, axis=-1, keepdims=True))
    ).astype(bf16)
    grad_cross_queries = (
        join_heads(
            jnp.einsum("hqk,hkd->hqd", cross_dscore, text_keys_h, preferred_element_type=f32)
        )
        * score_scale
    ).astype(bf16)
    grad_text_keys = (
        join_heads(
            jnp.einsum("hqk,hqd->hkd", cross_dscore, cross_queries_h, preferred_element_type=f32)
        )
        * score_scale
    )
    grad_text_values = join_heads(
        jnp.einsum("hqk,hqd->hkd", cross_low, grad_cross_h, preferred_element_type=f32)
    )
    grad_text = jnp.concatenate([grad_text_keys, grad_text_values], axis=1).astype(bf16)
    grad_w_ckv = jnp.dot(text_rows.T, grad_text, preferred_element_type=f32)
    grad_w_cq = jnp.dot(cross_in.T, grad_cross_queries, preferred_element_type=f32)
    grad_cross_in = jnp.dot(grad_cross_queries, w_cq.T, preferred_element_type=f32)
    grad_gain_cross = jnp.sum(grad_cross_in * normed_cross, axis=0)
    grad_attn_out = grad_cross_out + norm_back(
        grad_cross_in * gain_cross, normed_cross, inverse_cross
    )
    grad_branch_attn = (grad_attn_out * gate_attn * frame_valid).astype(bf16)
    grad_gate_attn = grad_attn_out * branch_attn * frame_valid
    grad_w_ao = jnp.dot(attention.T, grad_branch_attn, preferred_element_type=f32)
    grad_attention = jnp.dot(grad_branch_attn, w_ao.T, preferred_element_type=f32).astype(bf16)

    both = ("batch", "frame")
    middle = (grad_w_ao, grad_w_cq, grad_w_ckv, grad_w_co, grad_w_up, grad_w_down)
    middle = lax.psum(tuple(grad.astype(bf16) for grad in middle), both)

    grad_mod_in, grad_w_qkv = backward_attention(
        grad_attention,
        attention,
        stats,
        mod_all,
        mod_peer,
        pairs,
        queries,
        w_qkv,
        spread_matrices(width),
    )
    middle, grad_w_qkv = lax.optimization_barrier((middle, grad_w_qkv))
    grad_inputs = grad_attn_out + norm_back(
        grad_mod_in * (1.0 + scale_attn), normed_attn, inverse_attn
    )
    grad_frame_mod = jnp.concatenate(
        [
            grad_mod_in,
            grad_mod_in * normed_attn,
            grad_gate_attn,
            grad_mlp_in,
            grad_mlp_in * normed_mlp,
            grad_gate_mlp,
        ],
        axis=1,
    )
    grad_modulation = jnp.dot(onehot.T, grad_frame_mod, precision=highest)
    time_all = lax.all_gather(time_low, "batch", axis=0, tiled=True)
    own_rows = (jnp.arange(lax.axis_size("batch")) == lax.axis_index("batch")).astype(f32)
    spread_rows = (own_rows[:, None, None] * grad_modulation[None]).reshape(-1, 6 * width)
    grad_w_qkv = lax.psum(grad_w_qkv.astype(bf16), both)
    spread_rows, grad_gain_cross = lax.psum((spread_rows, grad_gain_cross), both)
    grad_w_ada = jnp.dot(time_all.astype(f32).T, spread_rows, precision=highest)
    grad_b_ada = jnp.sum(spread_rows, axis=0)
    grad_w_ao, grad_w_cq, grad_w_ckv, grad_w_co, grad_w_up, grad_w_down = (
        grad.astype(f32) for grad in middle
    )
    return (
        mixed.astype(bf16)[None],
        grad_inputs.astype(bf16)[None],
        grad_w_ada,
        grad_b_ada,
        grad_w_qkv.astype(f32),
        grad_w_ao,
        grad_gain_cross,
        grad_w_cq,
        grad_w_ckv,
        grad_w_co,
        grad_w_up,
        grad_w_down,
    )


def solution(mesh):
    placed = (
        P("batch", "frame", None),
        P("batch", None, None),
        P("batch", None, None, None),
        P("batch", None),
        P("batch", None),
        P("batch", "frame", None),
    ) + (P(),) * 10
    return jax.shard_map(
        per_device,
        mesh=mesh,
        in_specs=placed,
        out_specs=(P("batch", "frame", None), P("batch", "frame", None)) + (P(),) * 10,
        check_vma=False,
    )
```

```python
import functools
import math

import jax
import jax.numpy as jnp
import numpy as np
from jax import lax
from jax.experimental import pallas as pl
from jax.experimental.pallas import tpu as pltpu
from jax.sharding import PartitionSpec as P

HEADS = 6
LANES = 128
MASKED = -1e30

f32 = jnp.float32
bf16 = jnp.bfloat16
highest = lax.Precision.HIGHEST
eps_norm = 1e-06
MESH = pl.DeviceIdType.MESH

NT = (((1,), (1,)), ((), ()))
NN = (((1,), (0,)), ((), ()))
TN = (((0,), (0,)), ((), ()))


def dg(left, right, dims):
    return lax.dot_general(left, right, dims, preferred_element_type=f32)


def layer_norm(values):
    center = values - jnp.mean(values, axis=-1, keepdims=True)
    inverse = lax.rsqrt(jnp.mean(center * center, axis=-1, keepdims=True) + eps_norm)
    return (center * inverse, inverse)


def norm_back(grad, normed, inverse):
    mean_grad = jnp.mean(grad, axis=-1, keepdims=True)
    mean_prod = jnp.mean(grad * normed, axis=-1, keepdims=True)
    return (grad - mean_grad - normed * mean_prod) * inverse


def pieces(value):
    high = value.astype(bf16)
    rest = value - high.astype(f32)
    middle = rest.astype(bf16)
    low = (rest - middle.astype(f32)).astype(bf16)
    return high, middle, low


def nearest(step, me, count):
    lower = me < count // 2
    mine = jnp.where(lower, me, count - 1 - me)
    index = jnp.where(step - 1 < mine, step - 1, step)
    return jnp.where(lower, index, count - 1 - index)


def place():
    batch = lax.axis_index("batch")
    frame = lax.axis_index("frame")
    side = lax.rem(frame, 2)
    column = lax.div(frame, 2)
    return batch, frame, side, column, frame + 1 - 2 * side


def greet(batch, side, column, count, peer):
    barrier = pltpu.get_barrier_semaphore()
    pl.semaphore_signal(barrier, inc=1, device_id=(batch, peer), device_id_type=MESH)
    for step in range(1, count):
        other = nearest(step, column, count)
        pl.semaphore_signal(
            barrier, inc=1, device_id=(batch, 2 * other + side), device_id_type=MESH
        )
    pl.semaphore_wait(barrier, count)


def clip_ids(clip_len, clip_count, first, shape):
    position = first + lax.broadcasted_iota(jnp.int32, shape, 0)
    ids = jnp.zeros(shape, jnp.int32)
    end = 0
    for clip in range(clip_count):
        end = end + clip_len[0, clip]
        ids += (position >= end).astype(jnp.int32)
    return ids


def row_choice(ids, clip_count):
    lane = lax.broadcasted_iota(jnp.int32, ids.shape, 1)
    return ((lax.rem(lane, clip_count) == ids) & (lane < 3 * clip_count)).astype(bf16)


def head_tile(flat, head, tail):
    size = LANES - tail.shape[1]
    return jnp.concatenate([flat[:, head * size : (head + 1) * size], tail], axis=1)


def forward_kernel(
    frames,
    count,
    clip_count,
    clip_len,
    latents,
    time_embed,
    w_ada,
    b_ada,
    w_qkv,
    attention,
    stats,
    mod_rows,
    mod_all,
    mod_peer,
    pairs,
    queries,
    total,
    tops,
    part_out,
    part_in,
    stat_out,
    stat_in,
    send_sem,
    recv_sem,
):
    batch, frame, side, column, peer = place()
    width = latents.shape[1]
    head_size = width // HEADS
    greet(batch, side, column, count, peer)

    def to_peer(source, target, slot):
        return pltpu.make_async_remote_copy(
            src_ref=source,
            dst_ref=target,
            send_sem=send_sem.at[slot],
            recv_sem=recv_sem.at[slot],
            device_id=(batch, peer),
            device_id_type=MESH,
        )

    def to_column(step, other, slot):
        return pltpu.make_async_remote_copy(
            src_ref=mod_all.at[slot],
            dst_ref=mod_all.at[slot],
            send_sem=send_sem.at[2 + step],
            recv_sem=recv_sem.at[3 + slot],
            device_id=(batch, 2 * other + side),
            device_id_type=MESH,
        )

    time_low = time_embed[...].astype(f32)
    time_low = (time_low / (1.0 + jnp.exp(-time_low))).astype(bf16)
    modulation = dg(time_low, w_ada[...], NN) + b_ada[...]
    parts = [piece.astype(f32) for piece in pieces(modulation)]
    parts.append(jnp.zeros((16 - 3 * clip_count, modulation.shape[1]), f32))
    mod_rows[...] = jnp.concatenate(parts, axis=0).astype(bf16)
    choice = row_choice(clip_ids(clip_len, clip_count, frame * frames, (frames, 16)), clip_count)
    normed, inverse = layer_norm(latents[...].astype(f32))
    shift, scale = (
        dg(choice, mod_rows[:, part * width : (part + 1) * width], NN) for part in range(2)
    )
    mod_all[column] = (normed * (1.0 + scale) + shift).astype(bf16)
    swap = to_peer(mod_all.at[column], mod_peer, 0)
    sends = [
        to_column(step, nearest(step, column, count), column) for step in range(1, count)
    ]
    for index, send in enumerate(sends):
        send.start()
        if index == 0:
            swap.start()
    total[...] = jnp.zeros_like(total)
    tops[...] = jnp.full_like(tops, -1e38)
    tail = (frames, LANES - head_size)
    lane = lax.broadcasted_iota(jnp.int32, tail, 1)
    ones = jnp.ones(tail, bf16)

    def make_queries(half, owner, source):
        rows = pl.ds(half * frames, frames)
        flat = dg(source, w_qkv[:, :width], NN).astype(bf16) * 0.125
        ids = clip_ids(clip_len, clip_count, owner * frames, tail)
        extra = (ids == lane).astype(f32).astype(bf16)
        for head in range(HEADS):
            queries[head, rows, :] = head_tile(flat, head, extra)

    def make_keys(block):
        source = mod_all[block]
        ids = clip_ids(clip_len, clip_count, (2 * block + side) * frames, tail)
        masks = jnp.where((ids == lane) | (lane > clip_count), 0.0, MASKED)
        extra = jnp.where(
            lane < clip_count, masks, jnp.where(lane < clip_count + 3, 1.0, 0.0)
        ).astype(bf16)
        flat = dg(source, w_qkv[:, width : 2 * width], NN).astype(bf16)
        for head in range(HEADS):
            pairs[block, 0, head] = head_tile(flat, head, extra)
        flat = dg(source, w_qkv[:, 2 * width :], NN).astype(bf16)
        for head in range(HEADS):
            pairs[block, 1, head] = head_tile(flat, head, ones)

    def attend(half, block):
        rows = pl.ds(half * frames, frames)

        def scores(head):
            now = dg(pairs[block, 0, head], queries[head, rows, :], NT)
            return now, jnp.max(now, axis=0, keepdims=True)

        ahead = scores(0)
        for head in range(HEADS):
            now, top = ahead
            if head + 1 < HEADS:
                ahead = scores(head + 1)
            before = tops[head, :1, rows]
            new = jnp.maximum(before, top)
            probs = jnp.exp(now - new).astype(bf16)
            total[head, :, rows] = total[head, :, rows] * jnp.exp(before - new) + dg(
                pairs[block, 1, head], probs, TN
            )
            tops[head, :, rows] = jnp.broadcast_to(new, (8, frames))

    def arrive(step):
        block = nearest(step, column, count)
        to_column(step, block, block).wait_recv()
        make_keys(block)
        return block

    make_queries(0, frame, mod_all[column])
    make_keys(column)
    attend(0, column)
    swap.wait()
    make_queries(1, peer, mod_peer[...])
    attend(1, column)

    def per_block(step, unused):
        block = arrive(step)
        attend(0, block)
        attend(1, block)
        return unused

    lax.fori_loop(1, count - 1, per_block, 0)
    block = arrive(count - 1)
    attend(1, block)
    there = pl.ds(frames, frames)
    for head in range(HEADS):
        part_out[head * head_size : (head + 1) * head_size, :] = total[
            head, :head_size, there
        ].astype(bf16)
        stat_out[head : head + 1, :] = tops[head, :1, there]
        stat_out[8 + head : 9 + head, :] = total[head, head_size : head_size + 1, there]
    parts = to_peer(part_out, part_in, 1)
    numbers = to_peer(stat_out, stat_in, 2)
    numbers.start()
    parts.start()
    attend(0, block)
    numbers.wait()
    parts.wait()
    here = pl.ds(0, frames)
    joined = []
    logs = []
    for head in range(HEADS):
        mine, theirs = tops[head, :1, here], stat_in[head : head + 1, :]
        new = jnp.maximum(mine, theirs)
        left, right = jnp.exp(mine - new), jnp.exp(theirs - new)
        row_sum = (
            total[head, head_size : head_size + 1, here] * left
            + stat_in[8 + head : 9 + head, :] * right
        )
        logs.append(new + jnp.log(row_sum))
        scale = 1.0 / row_sum
        joined.append(
            total[head, :head_size, here] * (left * scale)
            + part_in[head * head_size : (head + 1) * head_size, :].astype(f32) * (right * scale)
        )
    attention[...] = jnp.concatenate(joined, axis=0).T.astype(bf16)
    rows = [piece for log in logs for piece in log_pieces(log)]
    rows.append(jnp.zeros((LANES - len(rows), frames), f32))
    stats[...] = jnp.concatenate(rows, axis=0).T.astype(bf16)
    for send in sends:
        send.wait_send()


def log_pieces(log):
    high, middle, low = pieces(-log)
    return [high.astype(f32), middle.astype(f32), low.astype(f32)]


def forward_attention(clip_len, latents, time_embed, w_ada, b_ada, w_qkv, count):
    frames, width = latents.shape
    clip_count = clip_len.shape[1]
    vmem = pl.BlockSpec(memory_space=pltpu.VMEM)
    shapes = (
        jax.ShapeDtypeStruct((frames, width), bf16),
        jax.ShapeDtypeStruct((frames, LANES), bf16),
        jax.ShapeDtypeStruct((16, w_ada.shape[1]), bf16),
        jax.ShapeDtypeStruct((count, frames, width), bf16),
        jax.ShapeDtypeStruct((frames, width), bf16),
        jax.ShapeDtypeStruct((count, 2, HEADS, frames, LANES), bf16),
        jax.ShapeDtypeStruct((HEADS, 2 * frames, LANES), bf16),
    )
    return pl.pallas_call(
        functools.partial(forward_kernel, frames, count, clip_count),
        name="attention_forward",
        out_shape=shapes,
        in_specs=[pl.BlockSpec(memory_space=pltpu.SMEM)] + [vmem] * 5,
        out_specs=(vmem,) * 7,
        scratch_shapes=[
            pltpu.VMEM((HEADS, LANES, 2 * frames), f32),
            pltpu.VMEM((HEADS, 8, 2 * frames), f32),
            pltpu.VMEM((width, frames), bf16),
            pltpu.VMEM((width, frames), bf16),
            pltpu.VMEM((16, frames), f32),
            pltpu.VMEM((16, frames), f32),
            pltpu.SemaphoreType.DMA((2 + count,)),
            pltpu.SemaphoreType.DMA((3 + count,)),
        ],
        compiler_params=pltpu.CompilerParams(
            collective_id=1, has_side_effects=True, vmem_limit_bytes=62 * 2**20
        ),
    )(clip_len, latents, time_embed, w_ada, b_ada, w_qkv)


def clip_sums(choice, value):
    high = value.astype(bf16)
    low = (value - high.astype(f32)).astype(bf16)
    return dg(choice, high, TN) + dg(choice, low, TN)


def middle_kernel(
    frames,
    clip_count,
    clip_len,
    text_len,
    latents,
    cotangent,
    attention,
    mod_rows,
    text_rows,
    gain_cross,
    w_ao,
    w_cq,
    w_ckv,
    w_co,
    w_up,
    w_down,
    mixed,
    grad_att,
    grad_attn_out,
    sums,
    weights,
    key_tiles,
    query_tiles,
    grad_tiles,
    probs_kept,
    flat_kv,
):
    batch, frame, side, column, peer = place()
    width = latents.shape[1]
    head_size = width // HEADS
    slots = text_rows.shape[0]
    per_clip = slots // clip_count
    tail = (frames, LANES - head_size)

    wide_ids = clip_ids(clip_len, clip_count, frame * frames, (frames, 16))
    choice = row_choice(wide_ids, clip_count)
    group_lane = lax.broadcasted_iota(jnp.int32, (frames, 16), 1)
    members = ((group_lane == batch * clip_count + wide_ids) & (wide_ids < clip_count)).astype(f32)
    members = members.astype(bf16)
    ids = clip_ids(clip_len, clip_count, frame * frames, (frames, width))
    valid = (ids < clip_count).astype(f32)

    def mod_part(part):
        return dg(choice, mod_rows[:, part * width : (part + 1) * width], NN)

    gate_attn = mod_part(2) * valid
    branch_attn = dg(attention[...], w_ao[...], NN)
    after_attn = latents[...].astype(f32) + gate_attn * branch_attn
    normed_cross, inverse_cross = layer_norm(after_attn)
    gain = gain_cross[...]
    cross_in = (normed_cross * gain).astype(bf16)

    flat = dg(cross_in, w_cq[...], NN).astype(bf16) * 0.125
    lane = lax.broadcasted_iota(jnp.int32, tail, 1)
    extra = (clip_ids(clip_len, clip_count, frame * frames, tail) == lane).astype(f32).astype(bf16)
    for head in range(HEADS):
        query_tiles[head] = head_tile(flat, head, extra)
    slot = lax.broadcasted_iota(jnp.int32, (slots, LANES - head_size), 0)
    lane = lax.broadcasted_iota(jnp.int32, (slots, LANES - head_size), 1)
    live = jnp.zeros(lane.shape, jnp.bool_)
    for clip in range(clip_count):
        inside = (slot >= clip * per_clip) & (slot < clip * per_clip + text_len[0, clip])
        live = live | (inside & (lane == clip))
    extra = jnp.where(live | (lane >= clip_count), 0.0, MASKED).astype(bf16)
    flat = dg(text_rows[...], w_ckv[:, :width], NN).astype(bf16)
    for head in range(HEADS):
        key_tiles[0, head] = head_tile(flat, head, extra)
    extra = (lane < 3).astype(f32).astype(bf16)
    flat = dg(text_rows[...], w_ckv[:, width:], NN).astype(bf16)
    for head in range(HEADS):
        key_tiles[1, head] = head_tile(flat, head, extra)

    def scores(head):
        now = dg(key_tiles[0, head], query_tiles[head], NT)
        return now, jnp.max(now, axis=0, keepdims=True)

    joined = []
    ahead = scores(0)
    for head in range(HEADS):
        now, top = ahead
        if head + 1 < HEADS:
            ahead = scores(head + 1)
        probs = jnp.exp(now - top)
        probs = (probs * (1.0 / jnp.sum(probs, axis=0, keepdims=True))).astype(bf16)
        probs_kept[head] = probs
        joined.append(dg(key_tiles[1, head], probs, TN)[:head_size])
    cross_exact = jnp.concatenate(joined, axis=0).T
    cross = cross_exact.astype(bf16)
    after_cross = after_attn + dg(cross, w_co[...], NN) * valid
    normed_mlp, inverse_mlp = layer_norm(after_cross)
    scale_mlp = 1.0 + mod_part(4)
    mlp_in = (normed_mlp * scale_mlp + mod_part(3)).astype(bf16)
    gate_mlp = mod_part(5) * valid
    grad_out = cotangent[...].astype(f32)
    grad_mlp = (grad_out * gate_mlp).astype(bf16)
    root = math.sqrt(2.0 / math.pi)
    branch_mlp = jnp.zeros((frames, width), f32)
    grad_mlp_in = jnp.zeros((frames, width), f32)
    hidden_width = w_up.shape[1]
    first = 0
    for part in range(hidden_width // width):
        here = slice(part * width, (part + 1) * width)
        hidden = dg(mlp_in, w_up[:, here], NN)
        square = hidden * hidden
        bend = jnp.tanh(root * hidden * (1.0 + 0.044715 * square))
        half = 0.5 * (1.0 + bend)
        activated = (hidden * half).astype(bf16)
        slope = half + (0.5 * root) * hidden * (1.0 - bend * bend) * (1.0 + 0.134145 * square)
        grad_hidden = (dg(grad_mlp, w_down[here, :], NT) * slope).astype(bf16)
        branch_mlp += dg(activated, w_down[here, :], NN)
        grad_mlp_in += dg(grad_hidden, w_up[:, here], NT)
        weights[first : first + width, :] = dg(activated, grad_mlp, TN).astype(bf16)
        first += width
        weights[first : first + width, :] = dg(mlp_in, grad_hidden, TN).astype(bf16)
        first += width
    mixed[...] = (after_cross + gate_mlp * branch_mlp).astype(bf16)
    sums[3] = clip_sums(members, grad_out * branch_mlp)
    sums[1] = clip_sums(members, grad_mlp_in)
    sums[2] = clip_sums(members, grad_mlp_in * normed_mlp)
    grad_cross_out = grad_out + norm_back(grad_mlp_in * scale_mlp, normed_mlp, inverse_mlp)
    grad_branch = (grad_cross_out * valid).astype(bf16)
    weights[first : first + width, :] = dg(cross, grad_branch, TN).astype(bf16)
    first += width

    flat = dg(grad_branch, w_co[...], NT).astype(bf16)
    product = flat.astype(f32) * cross_exact
    lane = lax.broadcasted_iota(jnp.int32, tail, 1)
    for head in range(HEADS):
        part = product[:, head * head_size : (head + 1) * head_size]
        high, middle, low = pieces(-jnp.sum(part, axis=1, keepdims=True))
        extra = jnp.where(
            lane == 0,
            high.astype(f32),
            jnp.where(lane == 1, middle.astype(f32), jnp.where(lane == 2, low.astype(f32), 0.0)),
        ).astype(bf16)
        grad_tiles[head] = head_tile(flat, head, extra)
    joined = []
    for pair in range(HEADS // 2):
        kept = []
        for head in (2 * pair, 2 * pair + 1):
            probs = probs_kept[head]
            dscore = dg(key_tiles[1, head], grad_tiles[head], NT) * probs.astype(f32)
            dscore = dscore.astype(bf16)
            joined.append(dg(key_tiles[0, head], dscore, TN)[:head_size])
            kept.append(
                (
                    dg(dscore, query_tiles[head], NN)[:, :head_size],
                    dg(probs, grad_tiles[head], NN)[:, :head_size],
                )
            )
        for kind in range(2):
            start = kind * width + pair * LANES
            flat_kv[:, start : start + LANES] = jnp.concatenate(
                [kept[0][kind], kept[1][kind]], axis=1
            ).astype(bf16)
    for kind in range(2):
        grad = dg(text_rows[...], flat_kv[:, kind * width : (kind + 1) * width], TN)
        weights[first : first + grad.shape[0], :] = grad.astype(bf16)
        first += grad.shape[0]
    grad_queries = (jnp.concatenate(joined, axis=0) * 0.125).T.astype(bf16)
    weights[first : first + width, :] = dg(cross_in, grad_queries, TN).astype(bf16)
    first += width
    grad_cross_in = dg(grad_queries, w_cq[...], NT)
    grad_gain = jnp.sum(grad_cross_in * normed_cross, axis=0, keepdims=True)
    top_row = lax.broadcasted_iota(jnp.int32, (16, width), 0) == 0
    sums[4] = jnp.where(top_row, grad_gain, 0.0)
    grad_attn = grad_cross_out + norm_back(grad_cross_in * gain, normed_cross, inverse_cross)
    grad_attn_out[...] = grad_attn
    sums[0] = clip_sums(members, grad_attn * branch_attn)
    grad_branch = (grad_attn * gate_attn).astype(bf16)
    weights[first : first + width, :] = dg(attention[...], grad_branch, TN).astype(bf16)
    first += width
    grad_att[...] = dg(grad_branch, w_ao[...], NT).astype(bf16)
    weights[first:, :] = jnp.zeros((weights.shape[0] - first, width), bf16)


def middle_lengths(width, text_width, hidden_width):
    return [width] * (2 * hidden_width // width + 1) + [text_width] * 2 + [width] * 2


def middle_part(clip_len, text_len, latents, *others, count):
    frames, width = latents.shape
    text_rows, w_up = others[3], others[9]
    slots, text_width = text_rows.shape
    rows = round_up(sum(middle_lengths(width, text_width, w_up.shape[1])), count)
    vmem = pl.BlockSpec(memory_space=pltpu.VMEM)
    smem = pl.BlockSpec(memory_space=pltpu.SMEM)
    return pl.pallas_call(
        functools.partial(middle_kernel, frames, clip_len.shape[1]),
        name="middle",
        out_shape=(
            jax.ShapeDtypeStruct((frames, width), bf16),
            jax.ShapeDtypeStruct((frames, width), bf16),
            jax.ShapeDtypeStruct((frames, width), f32),
            jax.ShapeDtypeStruct((5, 16, width), f32),
            jax.ShapeDtypeStruct((rows, width), bf16),
        ),
        in_specs=[smem] * 2 + [vmem] * 12,
        out_specs=(vmem,) * 5,
        scratch_shapes=[
            pltpu.VMEM((2, HEADS, slots, LANES), bf16),
            pltpu.VMEM((HEADS, frames, LANES), bf16),
            pltpu.VMEM((HEADS, frames, LANES), bf16),
            pltpu.VMEM((HEADS, slots, frames), bf16),
            pltpu.VMEM((slots, 2 * width), bf16),
        ],
        compiler_params=pltpu.CompilerParams(vmem_limit_bytes=62 * 2**20),
    )(clip_len, text_len, latents, *others)


def tile_of(rows):
    return max(tile for tile in range(16, 129, 16) if rows % tile == 0)


def level_size(kind, count):
    return {"core": 2, "x": 2, "y": 2, "square": 4, "z": count}[kind]


def level_place(kind):
    batch, frame, side, column, peer = place()
    core, across = lax.rem(batch, 2), lax.div(batch, 2)
    if kind == "core":
        return core, lambda member: (2 * across + member, frame)
    if kind == "x":
        return across, lambda member: (core + 2 * member, frame)
    if kind == "y":
        return side, lambda member: (batch, 2 * column + member)
    if kind == "square":
        return 2 * across + side, lambda member: (
            core + 2 * lax.div(member, 2),
            2 * column + lax.rem(member, 2),
        )
    return column, lambda member: (batch, 2 * member + side)


class Summing:
    def __init__(self, kinds, data, result, landings, send_sem, recv_sem, chunk, first, rows, count):
        self.data, self.result = data, result
        self.landings, self.send_sem, self.recv_sem, self.chunk = landings, send_sem, recv_sem, chunk
        self.sizes = [level_size(kind, count) for kind in kinds]
        self.places, self.devices = zip(*(level_place(kind) for kind in kinds))
        self.starts, self.lengths = [first], [rows]
        for size, mine in zip(self.sizes, self.places):
            self.lengths.append(self.lengths[-1] // size)
            self.starts.append(self.starts[-1] + mine * self.lengths[-1])
        self.sent = []

    def others(self, level):
        size = self.sizes[level]
        return [lax.rem(self.places[level] + step, size) for step in range(1, size)]

    def rows(self, start, length):
        return pl.ds(pl.multiple_of(start, 16), length)

    def copy(self, way, level, source, target, member, slot):
        base = way * sum(self.sizes) + sum(self.sizes[:level])
        return pltpu.make_async_remote_copy(
            src_ref=source,
            dst_ref=target,
            send_sem=self.send_sem.at[self.chunk, base + member],
            recv_sem=self.recv_sem.at[self.chunk, base + slot],
            device_id=self.devices[level](member),
            device_id_type=MESH,
        )

    def scatter(self, level):
        length = self.lengths[level + 1]
        for member in self.others(level):
            rows = self.rows(self.starts[level] + member * length, length)
            mine = self.places[level]
            copy = self.copy(
                0, level, self.data.at[rows], self.landings[level].at[mine], member, mine
            )
            copy.start()
            self.sent.append(copy)

    def add(self, level):
        length, start = self.lengths[level + 1], self.starts[level + 1]
        others = self.others(level)
        landing = self.landings[level]
        for member in others:
            rows = self.rows(start, length)
            self.copy(0, level, self.data.at[rows], landing.at[member], member, member).wait_recv()
        tile = tile_of(length)
        target = self.result if level == len(self.sizes) - 1 else self.data

        def body(index, unused):
            inner = self.rows(index * tile, tile)
            outer = self.rows(start + index * tile, tile)
            value = self.data[outer, :].astype(f32)
            for member in others:
                value += landing[member, inner, :].astype(f32)
            target[outer, :] = value.astype(bf16)
            return unused

        lax.fori_loop(0, length // tile, body, 0)

    def gather(self, level):
        rows = self.rows(self.starts[level + 1], self.lengths[level + 1])
        mine = self.places[level]
        for member in self.others(level):
            copy = self.copy(1, level, self.result.at[rows], self.result.at[rows], member, mine)
            copy.start()
            self.sent.append(copy)

    def gathered(self, level):
        length = self.lengths[level + 1]
        for member in self.others(level):
            rows = self.rows(self.starts[level] + member * length, length)
            self.copy(
                1, level, self.result.at[rows], self.result.at[rows], member, member
            ).wait_recv()

    def steps(self):
        def step(*calls):
            def run():
                for call, level in calls:
                    call(level)

            return run

        last = len(self.sizes) - 1
        runs = [step((self.scatter, 0))]
        for level in range(last):
            runs.append(step((self.add, level), (self.scatter, level + 1)))
        runs.append(step((self.add, last), (self.gather, last)))
        for level in range(last, 0, -1):
            runs.append(step((self.gathered, level), (self.gather, level - 1)))
        runs.append(step((self.gathered, 0)))
        return runs

    def finish(self):
        for copy in self.sent:
            copy.wait_send()


def chunk_rows(rows, chunks, count):
    unit = 128 * count
    units = rows // unit
    chunks = min(chunks, units)
    return [(units // chunks + (index < units % chunks)) * unit for index in range(chunks)]


def round_up(rows, count):
    unit = 128 * count
    return -(-rows // unit) * unit


def summing_scratch(kinds, rows, chunks, count):
    shapes, sizes = [], [level_size(kind, count) for kind in kinds]
    for length in chunk_rows(rows, chunks, count):
        for size in sizes:
            length //= size
            shapes.append(pltpu.VMEM((size, length, 384), bf16))
    slots = 2 * sum(sizes)
    return shapes + [pltpu.SemaphoreType.DMA((chunks, slots))] * 2


def make_summing(kinds, data, result, scratch, chunks, count):
    send_sem, recv_sem = scratch[-2:]
    sums, first = [], 0
    for chunk, length in enumerate(chunk_rows(data.shape[0], chunks, count)):
        landings = scratch[len(kinds) * chunk : len(kinds) * (chunk + 1)]
        sums.append(
            Summing(kinds, data, result, landings, send_sem, recv_sem, chunk, first, length, count)
        )
        first += length
    return sums


def greet_all(count):
    batch, frame, side, column, peer = place()
    core, across = lax.rem(batch, 2), lax.div(batch, 2)
    barrier = pltpu.get_barrier_semaphore()
    targets = [
        (batch + 1 - 2 * core, frame),
        (batch, peer),
        (core + 2 - 2 * across, frame),
        (core + 2 - 2 * across, peer),
    ]
    for step in range(1, count):
        targets.append((batch, 2 * lax.rem(column + step, count) + side))
    for target in targets:
        pl.semaphore_signal(barrier, inc=1, device_id=target, device_id_type=MESH)
    pl.semaphore_wait(barrier, len(targets))


TAIL_KINDS = ("core", "square", "z")
MIDDLE_KINDS = ("core", "x", "y", "z")


def sum_kernel(chunks, count, given, result, data, load_sem, *scratch):
    load = pltpu.make_async_copy(given, data, load_sem)
    load.start()
    greet_all(count)
    load.wait()
    sums = make_summing(TAIL_KINDS, data, result, scratch, chunks, count)
    for group in zip(*(item.steps() for item in sums)):
        for run in group:
            run()
    for item in sums:
        item.finish()


def sum_devices(given, count, chunks):
    rows, width = given.shape
    return pl.pallas_call(
        functools.partial(sum_kernel, chunks, count),
        name="sum_devices",
        out_shape=jax.ShapeDtypeStruct((rows, width), bf16),
        in_specs=[pl.BlockSpec(memory_space=pl.ANY)],
        out_specs=pl.BlockSpec(memory_space=pltpu.VMEM),
        scratch_shapes=[pltpu.VMEM(given.shape, bf16), pltpu.SemaphoreType.DMA]
        + summing_scratch(TAIL_KINDS, rows, chunks, count),
        compiler_params=pltpu.CompilerParams(
            collective_id=3, has_side_effects=True, vmem_limit_bytes=62 * 2**20
        ),
    )(given)


def backward_kernel(
    frames,
    count,
    clip_count,
    clip_len,
    latents,
    time_embed,
    mod_rows,
    grad_attn_out,
    sums,
    weights,
    grad_att,
    attention,
    stats,
    mod_all,
    mod_peer,
    pairs,
    queries_in,
    w_qkv,
    spread_q,
    spread_o,
    sum_heads,
    grad_latents,
    tail,
    result,
    data,
    grad_mod,
    grad_w,
    pack_out,
    pack_in,
    queries,
    grads,
    query_grad,
    key_grad,
    value_grad,
    flat_kv,
    part_out,
    part_in,
    peer_out,
    peer_in,
    held,
    held_sem,
    load_sem,
    query_sem,
    send_sem,
    recv_sem,
    *scratch,
):
    batch, frame, side, column, peer = place()
    width = grad_att.shape[1]
    slots = part_out.shape[0]
    load = pltpu.make_async_copy(weights, data, load_sem)
    load.start()
    load_queries = pltpu.make_async_copy(queries_in, queries, query_sem)
    load_queries.start()
    head_size = width // HEADS

    def block_at(step):
        return jnp.where(step == count, column, nearest(count - step, column, count))

    def fetch(step):
        slot = lax.rem(step - 1, 2)
        return pltpu.make_async_copy(
            pairs.at[block_at(step)], held.at[slot], held_sem.at[slot]
        )

    fetch(1).start()
    fetch(2).start()
    greet_all(count)
    load.wait()
    items = make_summing(MIDDLE_KINDS, data, result, scratch, MIDDLE_CHUNKS, count)
    waiting = [run for group in zip(*(item.steps() for item in items)) for run in group]

    def advance(runs=1):
        for run in waiting[:runs]:
            run()
        del waiting[:runs]

    advance(MIDDLE_CHUNKS)

    def to_peer(source, target, slot):
        return pltpu.make_async_remote_copy(
            src_ref=source,
            dst_ref=target,
            send_sem=send_sem.at[slot],
            recv_sem=recv_sem.at[slot],
            device_id=(batch, peer),
            device_id_type=MESH,
        )

    def to_owner(step, owner, slot):
        return pltpu.make_async_remote_copy(
            src_ref=part_out.at[lax.rem(step, slots)],
            dst_ref=part_in.at[slot],
            send_sem=send_sem.at[2 + step],
            recv_sem=recv_sem.at[2 + slot],
            device_id=(batch, 2 * owner + side),
            device_id_type=MESH,
        )

    grad_now = grad_att[...]
    product = grad_now.astype(f32) * attention[...].astype(f32)
    high, middle, low = pieces(product)
    delta = (
        dg(high, sum_heads[...], NN) + dg(middle, sum_heads[...], NN) + dg(low, sum_heads[...], NN)
    )
    high, middle, low = pieces(-delta)
    pack_out[:, :width] = grad_now
    pack_out[:, width : width + LANES] = stats[...]
    pack_out[:, width + LANES : width + 2 * LANES] = high
    pack_out[:, width + 2 * LANES : width + 3 * LANES] = middle
    pack_out[:, width + 3 * LANES :] = low
    swap = to_peer(pack_out, pack_in, 0)
    swap.start()
    query_grad[...] = jnp.zeros_like(query_grad)

    def prepare(half, source):
        rows = pl.ds(half * frames, frames)
        wide = dg(source[:, :width], spread_o[:width, :], NN)
        wide += dg(source[:, width + LANES :], spread_o[width:, :], NN)
        extra = dg(source[:, width : width + LANES], spread_q[...], NN).astype(bf16)
        wide = wide.astype(bf16)
        for head in range(HEADS):
            lanes = slice(head * LANES, (head + 1) * LANES)
            grads[head, rows, :] = wide[:, lanes]
            queries[head, rows, :] += extra[:, lanes]

    def differentiate(half, slot, first, moving=True):
        rows = pl.ds(half * frames, frames)
        for head in range(HEADS):
            if moving and head % 3 == 2:
                advance()
            key, value = held[slot, 0, head], held[slot, 1, head]
            query, grad = queries[head, rows, :], grads[head, rows, :]
            probs = jnp.exp(dg(key, query, NT))
            dscore = (probs * dg(value, grad, NT)).astype(bf16)
            probs = probs.astype(bf16)
            more_k, more_v = dg(dscore, query, NN), dg(probs, grad, NN)
            if first:
                key_grad[slot, head] = more_k
                value_grad[slot, head] = more_v
            else:
                key_grad[slot, head] += more_k
                value_grad[slot, head] += more_v
            query_grad[head, :, rows] += dg(key, dscore, TN)

    def finish_keys(block, slot):
        for kind, source in enumerate((key_grad, value_grad)):
            for pair in range(HEADS // 2):
                start = kind * width + pair * LANES
                flat_kv[:, start : start + LANES] = jnp.concatenate(
                    [
                        source[slot, 2 * pair][:, :head_size],
                        source[slot, 2 * pair + 1][:, :head_size],
                    ],
                    axis=1,
                ).astype(bf16)
        flat = flat_kv[...]
        return dg(flat, w_qkv[:, width:], NT), dg(mod_all[block], flat, TN)

    def finish_queries(half, source):
        rows = pl.ds(half * frames, frames)
        flat = jnp.concatenate(
            [query_grad[head, :head_size, rows] for head in range(HEADS)], axis=0
        )
        flat = (flat * 0.125).T.astype(bf16)
        return dg(flat, w_qkv[:, :width], NT), dg(source, flat, TN)

    def send_block(step, slot, first):
        block = block_at(step)
        part, weight = finish_keys(block, slot)
        if not isinstance(step, int):

            @pl.when(step > slots)
            def _():
                to_owner(step - slots, column, column).wait_send()

        part_out[lax.rem(step, slots)] = part.astype(bf16)
        to_owner(step, block, column).start()
        if first:
            grad_w[:, width:] = weight
        else:
            grad_w[:, width:] += weight

        @pl.when(step + 2 <= count)
        def _():
            fetch(step + 2).start()

    load_queries.wait()
    prepare(0, pack_out[...])
    fetch(1).wait()
    differentiate(0, 0, True)
    fetch(2).wait()
    differentiate(0, 1, True)
    swap.wait()
    prepare(1, pack_in[...])
    differentiate(1, 0, False)
    send_block(1, 0, True)
    differentiate(1, 1, False)
    send_block(2, 1, False)

    def per_block(step, moving):
        slot = (step - 1) % 2 if isinstance(step, int) else lax.rem(step - 1, 2)
        fetch(step).wait()
        differentiate(0, slot, True, moving)
        differentiate(1, slot, False, moving)
        send_block(step, slot, False)

    if count <= 4:
        for step in range(3, count):
            per_block(step, True)
    else:

        def looped(step, unused):
            per_block(step, False)
            return unused

        lax.fori_loop(3, count, looped, 0)
    slot = (count - 1) % 2
    fetch(count).wait()
    differentiate(1, slot, True)
    part, weight = finish_queries(1, mod_peer[...])
    peer_out[...] = part.astype(bf16)
    back = to_peer(peer_out, peer_in, 1)
    back.start()
    grad_w[:, :width] = weight
    differentiate(0, slot, False)
    part, weight = finish_keys(column, slot)
    grad_w[:, width:] += weight
    mine, weight = finish_queries(0, mod_all[column])
    grad_w[:, :width] += weight
    grad_mod[...] = part + mine

    choice = row_choice(clip_ids(clip_len, clip_count, frame * frames, (frames, 16)), clip_count)
    ids = clip_ids(clip_len, clip_count, frame * frames, (frames, 16))
    lane = lax.broadcasted_iota(jnp.int32, (frames, 16), 1)
    members = ((lane == batch * clip_count + ids) & (ids < clip_count)).astype(f32).astype(bf16)
    normed, inverse = layer_norm(latents[...].astype(f32))
    scale = 1.0 + dg(choice, mod_rows[:, width : 2 * width], NN)
    first = 0
    for part in range(3):
        tail[first : first + width, :] = grad_w[:, part * width : (part + 1) * width].astype(bf16)
        first += width
    first += 32
    for part in range(5):
        tail[first : first + 16, :] = sums[part].astype(bf16)
        first += 16
    time_low = time_embed[...].astype(f32)
    time_low = time_low / (1.0 + jnp.exp(-time_low))
    repeated = jnp.concatenate([time_low] * (16 // clip_count), axis=0)
    row = lax.broadcasted_iota(jnp.int32, (16, width), 0)
    mine = (lax.div(row, clip_count) == batch) & (frame == 0)
    tail[first : first + 16, :] = jnp.where(mine, repeated, 0.0).astype(bf16)
    first += 16
    tail[first:, :] = jnp.zeros((tail.shape[0] - first, width), bf16)

    def receive(step, unused):
        other = nearest(step, column, count)
        to_owner(step, other, other).wait_recv()
        grad_mod[...] += part_in[other].astype(f32)
        return unused

    lax.fori_loop(1, count, receive, 0)
    back.wait()
    total = grad_mod[...] + peer_in[...].astype(f32)
    grad_latents[...] = (
        grad_attn_out[...] + norm_back(total * scale, normed, inverse)
    ).astype(bf16)
    first = 3 * width
    tail[first : first + 16, :] = clip_sums(members, total).astype(bf16)
    tail[first + 16 : first + 32, :] = clip_sums(members, total * normed).astype(bf16)

    def sent(step, unused):
        to_owner(step, column, column).wait_send()
        return unused

    lax.fori_loop(max(1, count - slots), count, sent, 0)
    advance(len(waiting))
    for item in items:
        item.finish()


MIDDLE_CHUNKS = 2


def backward_attention(clip_len, *given, count):
    latents, weights = given[0], given[5]
    frames, width = latents.shape
    slots = min(count, 4)
    tail_rows = round_up(3 * width + 8 * 16, count)
    vmem = pl.BlockSpec(memory_space=pltpu.VMEM)
    anywhere = pl.BlockSpec(memory_space=pl.ANY)
    specs = [vmem] * 5 + [anywhere] + [vmem] * 5 + [anywhere] * 2 + [vmem] * 4
    return pl.pallas_call(
        functools.partial(backward_kernel, frames, count, clip_len.shape[1]),
        name="attention_backward",
        out_shape=(
            jax.ShapeDtypeStruct((frames, width), bf16),
            jax.ShapeDtypeStruct((tail_rows, width), bf16),
            jax.ShapeDtypeStruct(weights.shape, bf16),
        ),
        in_specs=[pl.BlockSpec(memory_space=pltpu.SMEM)] + specs,
        out_specs=(vmem,) * 3,
        scratch_shapes=[
            pltpu.VMEM(weights.shape, bf16),
            pltpu.VMEM((frames, width), f32),
            pltpu.VMEM((width, 3 * width), f32),
            pltpu.VMEM((frames, width + 4 * LANES), bf16),
            pltpu.VMEM((frames, width + 4 * LANES), bf16),
            pltpu.VMEM((HEADS, 2 * frames, LANES), bf16),
            pltpu.VMEM((HEADS, 2 * frames, LANES), bf16),
            pltpu.VMEM((HEADS, LANES, 2 * frames), f32),
            pltpu.VMEM((2, HEADS, frames, LANES), f32),
            pltpu.VMEM((2, HEADS, frames, LANES), f32),
            pltpu.VMEM((frames, 2 * width), bf16),
            pltpu.VMEM((slots, frames, width), bf16),
            pltpu.VMEM((count, frames, width), bf16),
            pltpu.VMEM((frames, width), bf16),
            pltpu.VMEM((frames, width), bf16),
            pltpu.VMEM((2, 2, HEADS, frames, LANES), bf16),
            pltpu.SemaphoreType.DMA((2,)),
            pltpu.SemaphoreType.DMA,
            pltpu.SemaphoreType.DMA,
            pltpu.SemaphoreType.DMA((2 + count,)),
            pltpu.SemaphoreType.DMA((2 + count,)),
        ]
        + summing_scratch(MIDDLE_KINDS, weights.shape[0], MIDDLE_CHUNKS, count),
        compiler_params=pltpu.CompilerParams(
            collective_id=2, has_side_effects=True, vmem_limit_bytes=63 * 2**20
        ),
    )(clip_len, *given)


def spread_matrices(width):
    head_size = width // HEADS
    lane = np.arange(HEADS * LANES, dtype=np.int32)[None, :]
    head, inner = lane // LANES, lane % LANES
    row = np.arange(LANES, dtype=np.int32)[:, None]
    spread_q = (row < 3 * HEADS) & (head == row // 3) & (inner == head_size + 4 + row % 3)
    row = np.arange(width, dtype=np.int32)[:, None]
    spread_o = [(head == row // head_size) & (inner == row % head_size)]
    row = np.arange(LANES, dtype=np.int32)[:, None]
    for piece in range(3):
        spread_o.append((row == head) & (inner == head_size + piece))
    column = np.arange(LANES, dtype=np.int32)[None, :]
    sum_heads = np.arange(width, dtype=np.int32)[:, None] // head_size == column
    return (
        spread_q.astype(bf16),
        np.concatenate(spread_o, axis=0).astype(bf16),
        sum_heads.astype(bf16),
    )


def per_device(
    latents,
    time_embed,
    text_states,
    text_len,
    clip_len,
    cotangent,
    w_ada,
    b_ada,
    w_qkv,
    w_ao,
    gain_cross,
    w_cq,
    w_ckv,
    w_co,
    w_up,
    w_down,
):
    frames = latents.shape[1]
    width = latents.shape[2]
    clip_count = time_embed.shape[1]
    text_slots = text_states.shape[2]
    count = lax.axis_size("frame") // 2
    attention, stats, mod_rows, mod_all, mod_peer, pairs, queries = forward_attention(
        clip_len, latents[0], time_embed[0], w_ada, b_ada[None], w_qkv, count
    )
    text_rows = text_states[0].reshape(clip_count * text_slots, text_states.shape[3])
    mixed, grad_attention, grad_attn_out, sums, weights = middle_part(
        clip_len,
        text_len,
        latents[0],
        cotangent[0],
        attention,
        mod_rows,
        text_rows,
        gain_cross[None],
        w_ao,
        w_cq,
        w_ckv,
        w_co,
        w_up,
        w_down,
        count=count,
    )

    grad_latents, tail, weights = backward_attention(
        clip_len,
        latents[0],
        time_embed[0],
        mod_rows,
        grad_attn_out,
        sums,
        weights,
        grad_attention,
        attention,
        stats,
        mod_all,
        mod_peer,
        pairs,
        queries,
        w_qkv,
        *spread_matrices(width),
        count=count,
    )
    tail = sum_devices(tail, count, 2)
    middle, first = [], 0
    for length in middle_lengths(width, text_rows.shape[1], w_up.shape[1]):
        middle.append(weights[first : first + length].astype(f32))
        first += length
    tail = tail.astype(f32)
    parts = [tail[first : first + width] for first in (0, width, 2 * width)]
    rows = tail[3 * width : 3 * width + 8 * 16].reshape(8, 16, width)
    spread_rows = jnp.concatenate([rows[part] for part in range(6)], axis=1)
    grad_w_ada = jnp.dot(rows[7].T, spread_rows, precision=highest)
    parted = 2 * (w_up.shape[1] // width)
    grad_w_down = jnp.concatenate(middle[0:parted:2], axis=0)
    grad_w_up = jnp.concatenate(middle[1:parted:2], axis=1)
    grad_w_co, text_keys, text_values, grad_w_cq, grad_w_ao = middle[parted:]
    return (
        mixed[None],
        grad_latents[None],
        grad_w_ada,
        jnp.sum(spread_rows, axis=0),
        jnp.concatenate(parts, axis=1),
        grad_w_ao,
        rows[6, 0],
        grad_w_cq,
        jnp.concatenate([text_keys, text_values], axis=1),
        grad_w_co,
        grad_w_up,
        grad_w_down,
    )


def solution(mesh):
    placed = (
        P("batch", "frame", None),
        P("batch", None, None),
        P("batch", None, None, None),
        P("batch", None),
        P("batch", None),
        P("batch", "frame", None),
    ) + (P(),) * 10
    return jax.shard_map(
        per_device,
        mesh=mesh,
        in_specs=placed,
        out_specs=(P("batch", "frame", None), P("batch", "frame", None)) + (P(),) * 10,
        check_vma=False,
    )
```

```python
import functools
import math

import jax
import jax.numpy as jnp
import numpy as np
from jax import lax
from jax.experimental import pallas as pl
from jax.experimental.pallas import tpu as pltpu
from jax.sharding import PartitionSpec as P

HEADS = 6
LANES = 128
MASKED = -1e30

f32 = jnp.float32
bf16 = jnp.bfloat16
highest = lax.Precision.HIGHEST
eps_norm = 1e-06
MESH = pl.DeviceIdType.MESH

NT = (((1,), (1,)), ((), ()))
NN = (((1,), (0,)), ((), ()))
TN = (((0,), (0,)), ((), ()))


def dg(left, right, dims):
    return lax.dot_general(left, right, dims, preferred_element_type=f32)


def layer_norm(values):
    center = values - jnp.mean(values, axis=-1, keepdims=True)
    inverse = lax.rsqrt(jnp.mean(center * center, axis=-1, keepdims=True) + eps_norm)
    return (center * inverse, inverse)


def norm_back(grad, normed, inverse):
    mean_grad = jnp.mean(grad, axis=-1, keepdims=True)
    mean_prod = jnp.mean(grad * normed, axis=-1, keepdims=True)
    return (grad - mean_grad - normed * mean_prod) * inverse


def pieces(value):
    high = value.astype(bf16)
    rest = value - high.astype(f32)
    middle = rest.astype(bf16)
    low = (rest - middle.astype(f32)).astype(bf16)
    return high, middle, low


def nearest(step, me, count):
    lower = me < count // 2
    mine = jnp.where(lower, me, count - 1 - me)
    index = jnp.where(step - 1 < mine, step - 1, step)
    return jnp.where(lower, index, count - 1 - index)


def place():
    batch = lax.axis_index("batch")
    frame = lax.axis_index("frame")
    side = lax.rem(frame, 2)
    column = lax.div(frame, 2)
    return batch, frame, side, column, frame + 1 - 2 * side


def greet(batch, side, column, count, peer):
    barrier = pltpu.get_barrier_semaphore()
    pl.semaphore_signal(barrier, inc=1, device_id=(batch, peer), device_id_type=MESH)
    for step in range(1, count):
        other = nearest(step, column, count)
        pl.semaphore_signal(
            barrier, inc=1, device_id=(batch, 2 * other + side), device_id_type=MESH
        )
    pl.semaphore_wait(barrier, count)


def clip_ids(clip_len, clip_count, first, shape):
    position = first + lax.broadcasted_iota(jnp.int32, shape, 0)
    ids = jnp.zeros(shape, jnp.int32)
    end = 0
    for clip in range(clip_count):
        end = end + clip_len[0, clip]
        ids += (position >= end).astype(jnp.int32)
    return ids


def row_choice(ids, clip_count):
    lane = lax.broadcasted_iota(jnp.int32, ids.shape, 1)
    return ((lax.rem(lane, clip_count) == ids) & (lane < 3 * clip_count)).astype(bf16)


def head_tile(flat, head, tail):
    size = LANES - tail.shape[1]
    return jnp.concatenate([flat[:, head * size : (head + 1) * size], tail], axis=1)


def forward_kernel(
    frames,
    count,
    clip_count,
    clip_len,
    latents,
    time_embed,
    w_ada,
    b_ada,
    w_qkv,
    attention,
    stats,
    mod_rows,
    mod_all,
    mod_peer,
    pairs,
    queries,
    total,
    tops,
    part_out,
    part_in,
    stat_out,
    stat_in,
    send_sem,
    recv_sem,
):
    batch, frame, side, column, peer = place()
    width = latents.shape[1]
    head_size = width // HEADS
    greet(batch, side, column, count, peer)

    def to_peer(source, target, slot):
        return pltpu.make_async_remote_copy(
            src_ref=source,
            dst_ref=target,
            send_sem=send_sem.at[slot],
            recv_sem=recv_sem.at[slot],
            device_id=(batch, peer),
            device_id_type=MESH,
        )

    def to_column(step, other, slot):
        return pltpu.make_async_remote_copy(
            src_ref=mod_all.at[slot],
            dst_ref=mod_all.at[slot],
            send_sem=send_sem.at[2 + step],
            recv_sem=recv_sem.at[3 + slot],
            device_id=(batch, 2 * other + side),
            device_id_type=MESH,
        )

    time_low = time_embed[...].astype(f32)
    time_low = (time_low / (1.0 + jnp.exp(-time_low))).astype(bf16)
    modulation = dg(time_low, w_ada[...], NN) + b_ada[...]
    parts = [piece.astype(f32) for piece in pieces(modulation)]
    parts.append(jnp.zeros((16 - 3 * clip_count, modulation.shape[1]), f32))
    mod_rows[...] = jnp.concatenate(parts, axis=0).astype(bf16)
    choice = row_choice(clip_ids(clip_len, clip_count, frame * frames, (frames, 16)), clip_count)
    normed, inverse = layer_norm(latents[...].astype(f32))
    shift, scale = (
        dg(choice, mod_rows[:, part * width : (part + 1) * width], NN) for part in range(2)
    )
    mod_all[column] = (normed * (1.0 + scale) + shift).astype(bf16)
    swap = to_peer(mod_all.at[column], mod_peer, 0)
    relayed = count == 4

    def hop(block, up):
        other = column + 1 if up else column - 1
        return pltpu.make_async_remote_copy(
            src_ref=mod_all.at[block],
            dst_ref=mod_all.at[block],
            send_sem=send_sem.at[2 + block + (0 if up else count)],
            recv_sem=recv_sem.at[3 + block],
            device_id=(batch, 2 * other + side),
            device_id_type=MESH,
        )

    def each_hop(distance, act):
        for up in (True, False):
            block = column - distance if up else column + distance
            here = block >= 0 if up else block < count
            further = column < count - 1 if up else column > 0
            act(block, up, here, further)

    def begin(block, up, here, further):
        @pl.when(here & further)
        def _():
            hop(block, up).start()

    def take(block, up, here, further):
        @pl.when(here)
        def _():
            hop(block, up).wait_recv()

        begin(block, up, here, further)

    def end(block, up, here, further):
        @pl.when(here & further)
        def _():
            hop(block, up).wait_send()

    if relayed:
        each_hop(0, begin)
        swap.start()
    else:
        sends = [
            to_column(step, nearest(step, column, count), column) for step in range(1, count)
        ]
        for index, send in enumerate(sends):
            send.start()
            if index == 0:
                swap.start()
    total[...] = jnp.zeros_like(total)
    tops[...] = jnp.full_like(tops, -1e38)
    tail = (frames, LANES - head_size)
    lane = lax.broadcasted_iota(jnp.int32, tail, 1)
    ones = jnp.ones(tail, bf16)

    def make_queries(half, owner, source):
        rows = pl.ds(half * frames, frames)
        flat = dg(source, w_qkv[:, :width], NN).astype(bf16) * 0.125
        ids = clip_ids(clip_len, clip_count, owner * frames, tail)
        extra = (ids == lane).astype(f32).astype(bf16)
        for head in range(HEADS):
            queries[head, rows, :] = head_tile(flat, head, extra)

    def make_keys(block):
        source = mod_all[block]
        ids = clip_ids(clip_len, clip_count, (2 * block + side) * frames, tail)
        masks = jnp.where((ids == lane) | (lane > clip_count), 0.0, MASKED)
        extra = jnp.where(
            lane < clip_count, masks, jnp.where(lane < clip_count + 3, 1.0, 0.0)
        ).astype(bf16)
        flat = dg(source, w_qkv[:, width : 2 * width], NN).astype(bf16)
        for head in range(HEADS):
            pairs[block, 0, head] = head_tile(flat, head, extra)
        flat = dg(source, w_qkv[:, 2 * width :], NN).astype(bf16)
        for head in range(HEADS):
            pairs[block, 1, head] = head_tile(flat, head, ones)

    def attend(half, block):
        rows = pl.ds(half * frames, frames)

        def scores(head):
            now = dg(pairs[block, 0, head], queries[head, rows, :], NT)
            return now, jnp.max(now, axis=0, keepdims=True)

        ahead = scores(0)
        for head in range(HEADS):
            now, top = ahead
            if head + 1 < HEADS:
                ahead = scores(head + 1)
            before = tops[head, :1, rows]
            new = jnp.maximum(before, top)
            probs = jnp.exp(now - new).astype(bf16)
            total[head, :, rows] = total[head, :, rows] * jnp.exp(before - new) + dg(
                pairs[block, 1, head], probs, TN
            )
            tops[head, :, rows] = jnp.broadcast_to(new, (8, frames))

    def arrive(step):
        block = nearest(step, column, count)
        if not relayed:
            to_column(step, block, block).wait_recv()
        make_keys(block)
        return block

    make_queries(0, frame, mod_all[column])
    make_keys(column)
    attend(0, column)
    swap.wait()
    make_queries(1, peer, mod_peer[...])
    attend(1, column)

    if relayed:
        outer = (column == 0) | (column == count - 1)
        each_hop(1, take)
        block = arrive(1)
        attend(0, block)
        attend(1, block)

        @pl.when(outer)
        def _():
            each_hop(2, take)

        block = arrive(2)
        attend(0, block)

        @pl.when(jnp.logical_not(outer))
        def _():
            each_hop(2, take)

        attend(1, block)
        each_hop(3, take)
    else:

        def per_block(step, unused):
            block = arrive(step)
            attend(0, block)
            attend(1, block)
            return unused

        lax.fori_loop(1, count - 1, per_block, 0)
    block = arrive(count - 1)
    attend(1, block)
    there = pl.ds(frames, frames)
    for head in range(HEADS):
        part_out[head * head_size : (head + 1) * head_size, :] = total[
            head, :head_size, there
        ].astype(bf16)
        stat_out[head : head + 1, :] = tops[head, :1, there]
        stat_out[8 + head : 9 + head, :] = total[head, head_size : head_size + 1, there]
    parts = to_peer(part_out, part_in, 1)
    numbers = to_peer(stat_out, stat_in, 2)
    numbers.start()
    parts.start()
    attend(0, block)
    numbers.wait()
    parts.wait()
    here = pl.ds(0, frames)
    joined = []
    logs = []
    for head in range(HEADS):
        mine, theirs = tops[head, :1, here], stat_in[head : head + 1, :]
        new = jnp.maximum(mine, theirs)
        left, right = jnp.exp(mine - new), jnp.exp(theirs - new)
        row_sum = (
            total[head, head_size : head_size + 1, here] * left
            + stat_in[8 + head : 9 + head, :] * right
        )
        logs.append(new + jnp.log(row_sum))
        scale = 1.0 / row_sum
        joined.append(
            total[head, :head_size, here] * (left * scale)
            + part_in[head * head_size : (head + 1) * head_size, :].astype(f32) * (right * scale)
        )
    attention[...] = jnp.concatenate(joined, axis=0).T.astype(bf16)
    rows = [piece for log in logs for piece in log_pieces(log)]
    rows.append(jnp.zeros((LANES - len(rows), frames), f32))
    stats[...] = jnp.concatenate(rows, axis=0).T.astype(bf16)
    if relayed:
        for distance in range(count - 1):
            each_hop(distance, end)
    else:
        for send in sends:
            send.wait_send()


def log_pieces(log):
    high, middle, low = pieces(-log)
    return [high.astype(f32), middle.astype(f32), low.astype(f32)]


def forward_attention(clip_len, latents, time_embed, w_ada, b_ada, w_qkv, count):
    frames, width = latents.shape
    clip_count = clip_len.shape[1]
    vmem = pl.BlockSpec(memory_space=pltpu.VMEM)
    shapes = (
        jax.ShapeDtypeStruct((frames, width), bf16),
        jax.ShapeDtypeStruct((frames, LANES), bf16),
        jax.ShapeDtypeStruct((16, w_ada.shape[1]), bf16),
        jax.ShapeDtypeStruct((count, frames, width), bf16),
        jax.ShapeDtypeStruct((frames, width), bf16),
        jax.ShapeDtypeStruct((count, 2, HEADS, frames, LANES), bf16),
        jax.ShapeDtypeStruct((HEADS, 2 * frames, LANES), bf16),
    )
    return pl.pallas_call(
        functools.partial(forward_kernel, frames, count, clip_count),
        name="attention_forward",
        out_shape=shapes,
        in_specs=[pl.BlockSpec(memory_space=pltpu.SMEM)] + [vmem] * 5,
        out_specs=(vmem,) * 7,
        scratch_shapes=[
            pltpu.VMEM((HEADS, LANES, 2 * frames), f32),
            pltpu.VMEM((HEADS, 8, 2 * frames), f32),
            pltpu.VMEM((width, frames), bf16),
            pltpu.VMEM((width, frames), bf16),
            pltpu.VMEM((16, frames), f32),
            pltpu.VMEM((16, frames), f32),
            pltpu.SemaphoreType.DMA((2 + 2 * count,)),
            pltpu.SemaphoreType.DMA((3 + count,)),
        ],
        compiler_params=pltpu.CompilerParams(
            collective_id=1, has_side_effects=True, vmem_limit_bytes=62 * 2**20
        ),
    )(clip_len, latents, time_embed, w_ada, b_ada, w_qkv)


def clip_sums(choice, value):
    high = value.astype(bf16)
    low = (value - high.astype(f32)).astype(bf16)
    return dg(choice, high, TN) + dg(choice, low, TN)


def middle_kernel(
    frames,
    clip_count,
    clip_len,
    text_len,
    latents,
    cotangent,
    attention,
    mod_rows,
    text_rows,
    gain_cross,
    w_ao,
    w_cq,
    w_ckv,
    w_co,
    w_up,
    w_down,
    mixed,
    grad_att,
    grad_attn_out,
    sums,
    weights,
    key_tiles,
    query_tiles,
    grad_tiles,
    probs_kept,
    flat_kv,
):
    batch, frame, side, column, peer = place()
    width = latents.shape[1]
    head_size = width // HEADS
    slots = text_rows.shape[0]
    per_clip = slots // clip_count
    tail = (frames, LANES - head_size)

    wide_ids = clip_ids(clip_len, clip_count, frame * frames, (frames, 16))
    choice = row_choice(wide_ids, clip_count)
    group_lane = lax.broadcasted_iota(jnp.int32, (frames, 16), 1)
    members = ((group_lane == batch * clip_count + wide_ids) & (wide_ids < clip_count)).astype(f32)
    members = members.astype(bf16)
    ids = clip_ids(clip_len, clip_count, frame * frames, (frames, width))
    valid = (ids < clip_count).astype(f32)

    def mod_part(part):
        return dg(choice, mod_rows[:, part * width : (part + 1) * width], NN)

    gate_attn = mod_part(2) * valid
    branch_attn = dg(attention[...], w_ao[...], NN)
    after_attn = latents[...].astype(f32) + gate_attn * branch_attn
    normed_cross, inverse_cross = layer_norm(after_attn)
    gain = gain_cross[...]
    cross_in = (normed_cross * gain).astype(bf16)

    flat = dg(cross_in, w_cq[...], NN).astype(bf16) * 0.125
    lane = lax.broadcasted_iota(jnp.int32, tail, 1)
    extra = (clip_ids(clip_len, clip_count, frame * frames, tail) == lane).astype(f32).astype(bf16)
    for head in range(HEADS):
        query_tiles[head] = head_tile(flat, head, extra)
    slot = lax.broadcasted_iota(jnp.int32, (slots, LANES - head_size), 0)
    lane = lax.broadcasted_iota(jnp.int32, (slots, LANES - head_size), 1)
    live = jnp.zeros(lane.shape, jnp.bool_)
    for clip in range(clip_count):
        inside = (slot >= clip * per_clip) & (slot < clip * per_clip + text_len[0, clip])
        live = live | (inside & (lane == clip))
    extra = jnp.where(live | (lane >= clip_count), 0.0, MASKED).astype(bf16)
    flat = dg(text_rows[...], w_ckv[:, :width], NN).astype(bf16)
    for head in range(HEADS):
        key_tiles[0, head] = head_tile(flat, head, extra)
    extra = (lane < 3).astype(f32).astype(bf16)
    flat = dg(text_rows[...], w_ckv[:, width:], NN).astype(bf16)
    for head in range(HEADS):
        key_tiles[1, head] = head_tile(flat, head, extra)

    def scores(head):
        now = dg(key_tiles[0, head], query_tiles[head], NT)
        return now, jnp.max(now, axis=0, keepdims=True)

    joined = []
    ahead = scores(0)
    for head in range(HEADS):
        now, top = ahead
        if head + 1 < HEADS:
            ahead = scores(head + 1)
        probs = jnp.exp(now - top)
        probs = (probs * (1.0 / jnp.sum(probs, axis=0, keepdims=True))).astype(bf16)
        probs_kept[head] = probs
        joined.append(dg(key_tiles[1, head], probs, TN)[:head_size])
    cross_exact = jnp.concatenate(joined, axis=0).T
    cross = cross_exact.astype(bf16)
    after_cross = after_attn + dg(cross, w_co[...], NN) * valid
    normed_mlp, inverse_mlp = layer_norm(after_cross)
    scale_mlp = 1.0 + mod_part(4)
    mlp_in = (normed_mlp * scale_mlp + mod_part(3)).astype(bf16)
    gate_mlp = mod_part(5) * valid
    grad_out = cotangent[...].astype(f32)
    grad_mlp = (grad_out * gate_mlp).astype(bf16)
    root = math.sqrt(2.0 / math.pi)
    branch_mlp = jnp.zeros((frames, width), f32)
    grad_mlp_in = jnp.zeros((frames, width), f32)
    hidden_width = w_up.shape[1]
    first = 0
    for part in range(hidden_width // width):
        here = slice(part * width, (part + 1) * width)
        hidden = dg(mlp_in, w_up[:, here], NN)
        square = hidden * hidden
        bend = jnp.tanh(root * hidden * (1.0 + 0.044715 * square))
        half = 0.5 * (1.0 + bend)
        activated = (hidden * half).astype(bf16)
        slope = half + (0.5 * root) * hidden * (1.0 - bend * bend) * (1.0 + 0.134145 * square)
        grad_hidden = (dg(grad_mlp, w_down[here, :], NT) * slope).astype(bf16)
        branch_mlp += dg(activated, w_down[here, :], NN)
        grad_mlp_in += dg(grad_hidden, w_up[:, here], NT)
        weights[first : first + width, :] = dg(activated, grad_mlp, TN).astype(bf16)
        first += width
        weights[first : first + width, :] = dg(mlp_in, grad_hidden, TN).astype(bf16)
        first += width
    mixed[...] = (after_cross + gate_mlp * branch_mlp).astype(bf16)
    sums[3] = clip_sums(members, grad_out * branch_mlp)
    sums[1] = clip_sums(members, grad_mlp_in)
    sums[2] = clip_sums(members, grad_mlp_in * normed_mlp)
    grad_cross_out = grad_out + norm_back(grad_mlp_in * scale_mlp, normed_mlp, inverse_mlp)
    grad_branch = (grad_cross_out * valid).astype(bf16)
    weights[first : first + width, :] = dg(cross, grad_branch, TN).astype(bf16)
    first += width

    flat = dg(grad_branch, w_co[...], NT).astype(bf16)
    product = flat.astype(f32) * cross_exact
    lane = lax.broadcasted_iota(jnp.int32, tail, 1)
    for head in range(HEADS):
        part = product[:, head * head_size : (head + 1) * head_size]
        high, middle, low = pieces(-jnp.sum(part, axis=1, keepdims=True))
        extra = jnp.where(
            lane == 0,
            high.astype(f32),
            jnp.where(lane == 1, middle.astype(f32), jnp.where(lane == 2, low.astype(f32), 0.0)),
        ).astype(bf16)
        grad_tiles[head] = head_tile(flat, head, extra)
    joined = []
    for pair in range(HEADS // 2):
        kept = []
        for head in (2 * pair, 2 * pair + 1):
            probs = probs_kept[head]
            dscore = dg(key_tiles[1, head], grad_tiles[head], NT) * probs.astype(f32)
            dscore = dscore.astype(bf16)
            joined.append(dg(key_tiles[0, head], dscore, TN)[:head_size])
            kept.append(
                (
                    dg(dscore, query_tiles[head], NN)[:, :head_size],
                    dg(probs, grad_tiles[head], NN)[:, :head_size],
                )
            )
        for kind in range(2):
            start = kind * width + pair * LANES
            flat_kv[:, start : start + LANES] = jnp.concatenate(
                [kept[0][kind], kept[1][kind]], axis=1
            ).astype(bf16)
    for kind in range(2):
        grad = dg(text_rows[...], flat_kv[:, kind * width : (kind + 1) * width], TN)
        weights[first : first + grad.shape[0], :] = grad.astype(bf16)
        first += grad.shape[0]
    grad_queries = (jnp.concatenate(joined, axis=0) * 0.125).T.astype(bf16)
    weights[first : first + width, :] = dg(cross_in, grad_queries, TN).astype(bf16)
    first += width
    grad_cross_in = dg(grad_queries, w_cq[...], NT)
    grad_gain = jnp.sum(grad_cross_in * normed_cross, axis=0, keepdims=True)
    top_row = lax.broadcasted_iota(jnp.int32, (16, width), 0) == 0
    sums[4] = jnp.where(top_row, grad_gain, 0.0)
    grad_attn = grad_cross_out + norm_back(grad_cross_in * gain, normed_cross, inverse_cross)
    grad_attn_out[...] = grad_attn
    sums[0] = clip_sums(members, grad_attn * branch_attn)
    grad_branch = (grad_attn * gate_attn).astype(bf16)
    weights[first : first + width, :] = dg(attention[...], grad_branch, TN).astype(bf16)
    first += width
    grad_att[...] = dg(grad_branch, w_ao[...], NT).astype(bf16)
    weights[first:, :] = jnp.zeros((weights.shape[0] - first, width), bf16)


def middle_lengths(width, text_width, hidden_width):
    return [width] * (2 * hidden_width // width + 1) + [text_width] * 2 + [width] * 2


def middle_part(clip_len, text_len, latents, *others, count):
    frames, width = latents.shape
    text_rows, w_up = others[3], others[9]
    slots, text_width = text_rows.shape
    rows = round_up(sum(middle_lengths(width, text_width, w_up.shape[1])), count)
    vmem = pl.BlockSpec(memory_space=pltpu.VMEM)
    smem = pl.BlockSpec(memory_space=pltpu.SMEM)
    return pl.pallas_call(
        functools.partial(middle_kernel, frames, clip_len.shape[1]),
        name="middle",
        out_shape=(
            jax.ShapeDtypeStruct((frames, width), bf16),
            jax.ShapeDtypeStruct((frames, width), bf16),
            jax.ShapeDtypeStruct((frames, width), f32),
            jax.ShapeDtypeStruct((5, 16, width), f32),
            jax.ShapeDtypeStruct((rows, width), bf16),
        ),
        in_specs=[smem] * 2 + [vmem] * 12,
        out_specs=(vmem,) * 5,
        scratch_shapes=[
            pltpu.VMEM((2, HEADS, slots, LANES), bf16),
            pltpu.VMEM((HEADS, frames, LANES), bf16),
            pltpu.VMEM((HEADS, frames, LANES), bf16),
            pltpu.VMEM((HEADS, slots, frames), bf16),
            pltpu.VMEM((slots, 2 * width), bf16),
        ],
        compiler_params=pltpu.CompilerParams(vmem_limit_bytes=62 * 2**20),
    )(clip_len, text_len, latents, *others)


def tile_of(rows):
    return max(tile for tile in range(16, 129, 16) if rows % tile == 0)


def level_size(kind, count):
    return {"square": 4, "z": count}.get(kind, 2)


def level_place(kind):
    batch, frame, side, column, peer = place()
    core, across = lax.rem(batch, 2), lax.div(batch, 2)
    if kind == "core":
        return core, lambda member: (2 * across + member, frame)
    if kind == "x":
        return across, lambda member: (core + 2 * member, frame)
    if kind == "y":
        return side, lambda member: (batch, 2 * column + member)
    if kind == "square":
        return 2 * across + side, lambda member: (
            core + 2 * lax.div(member, 2),
            2 * column + lax.rem(member, 2),
        )
    if kind == "z":
        return column, lambda member: (batch, 2 * member + side)
    bit = int(kind)
    mine = lax.rem(lax.div(column, bit), 2)
    return mine, lambda member: (batch, 2 * (column + bit * (member - mine)) + side)


class Summing:
    def __init__(self, kinds, data, result, landings, send_sem, recv_sem, chunk, first, rows, count):
        self.data, self.result = data, result
        self.landings, self.send_sem, self.recv_sem, self.chunk = landings, send_sem, recv_sem, chunk
        self.sizes = [level_size(kind, count) for kind in kinds]
        self.places, self.devices = zip(*(level_place(kind) for kind in kinds))
        self.starts, self.lengths = [first], [rows]
        for size, mine in zip(self.sizes, self.places):
            self.lengths.append(self.lengths[-1] // size)
            self.starts.append(self.starts[-1] + mine * self.lengths[-1])
        self.sent = []

    def others(self, level):
        size = self.sizes[level]
        return [lax.rem(self.places[level] + step, size) for step in range(1, size)]

    def rows(self, start, length):
        return pl.ds(pl.multiple_of(start, 16), length)

    def copy(self, way, level, source, target, member, slot):
        base = way * sum(self.sizes) + sum(self.sizes[:level])
        return pltpu.make_async_remote_copy(
            src_ref=source,
            dst_ref=target,
            send_sem=self.send_sem.at[self.chunk, base + member],
            recv_sem=self.recv_sem.at[self.chunk, base + slot],
            device_id=self.devices[level](member),
            device_id_type=MESH,
        )

    def scatter(self, level):
        length = self.lengths[level + 1]
        for member in self.others(level):
            rows = self.rows(self.starts[level] + member * length, length)
            mine = self.places[level]
            copy = self.copy(
                0, level, self.data.at[rows], self.landings[level].at[mine], member, mine
            )
            copy.start()
            self.sent.append(copy)

    def add(self, level):
        length, start = self.lengths[level + 1], self.starts[level + 1]
        others = self.others(level)
        landing = self.landings[level]
        for member in others:
            rows = self.rows(start, length)
            self.copy(0, level, self.data.at[rows], landing.at[member], member, member).wait_recv()
        tile = tile_of(length)
        target = self.result if level == len(self.sizes) - 1 else self.data

        def body(index, unused):
            inner = self.rows(index * tile, tile)
            outer = self.rows(start + index * tile, tile)
            value = self.data[outer, :].astype(f32)
            for member in others:
                value += landing[member, inner, :].astype(f32)
            target[outer, :] = value.astype(bf16)
            return unused

        lax.fori_loop(0, length // tile, body, 0)

    def gather(self, level):
        rows = self.rows(self.starts[level + 1], self.lengths[level + 1])
        mine = self.places[level]
        for member in self.others(level):
            copy = self.copy(1, level, self.result.at[rows], self.result.at[rows], member, mine)
            copy.start()
            self.sent.append(copy)

    def gathered(self, level):
        length = self.lengths[level + 1]
        for member in self.others(level):
            rows = self.rows(self.starts[level] + member * length, length)
            self.copy(
                1, level, self.result.at[rows], self.result.at[rows], member, member
            ).wait_recv()

    def steps(self):
        def step(*calls):
            def run():
                for call, level in calls:
                    call(level)

            return run

        last = len(self.sizes) - 1
        runs = [step((self.scatter, 0))]
        for level in range(last):
            runs.append(step((self.add, level), (self.scatter, level + 1)))
        runs.append(step((self.add, last), (self.gather, last)))
        for level in range(last, 0, -1):
            runs.append(step((self.gathered, level), (self.gather, level - 1)))
        runs.append(step((self.gathered, 0)))
        return runs

    def finish(self):
        for copy in self.sent:
            copy.wait_send()


def middle_kinds(count):
    bits, bit = [], 1
    while bit < count:
        bits.append(str(bit))
        bit *= 2
    return tuple(start + tuple(bits) for start in MIDDLE_STARTS)


def chunk_rows(rows, chunks, count):
    unit = 128 * count
    units = rows // unit
    chunks = min(chunks, units)
    return [(units // chunks + (index < units % chunks)) * unit for index in range(chunks)]


def round_up(rows, count):
    unit = 128 * count
    return -(-rows // unit) * unit


def summing_scratch(kinds, rows, chunks, count):
    shapes, sizes = [], [level_size(kind, count) for kind in kinds[0]]
    for length in chunk_rows(rows, chunks, count):
        for size in sizes:
            length //= size
            shapes.append(pltpu.VMEM((size, length, 384), bf16))
    slots = 2 * sum(sizes)
    return shapes + [pltpu.SemaphoreType.DMA((chunks, slots))] * 2


def make_summing(kinds, data, result, scratch, chunks, count):
    send_sem, recv_sem = scratch[-2:]
    levels = len(kinds[0])
    sums, first = [], 0
    for chunk, length in enumerate(chunk_rows(data.shape[0], chunks, count)):
        landings = scratch[levels * chunk : levels * (chunk + 1)]
        order = kinds[chunk % len(kinds)]
        sums.append(
            Summing(order, data, result, landings, send_sem, recv_sem, chunk, first, length, count)
        )
        first += length
    return sums


def greet_all(count):
    batch, frame, side, column, peer = place()
    core, across = lax.rem(batch, 2), lax.div(batch, 2)
    barrier = pltpu.get_barrier_semaphore()
    targets = [
        (batch + 1 - 2 * core, frame),
        (batch, peer),
        (core + 2 - 2 * across, frame),
        (core + 2 - 2 * across, peer),
    ]
    for step in range(1, count):
        targets.append((batch, 2 * lax.rem(column + step, count) + side))
    for target in targets:
        pl.semaphore_signal(barrier, inc=1, device_id=target, device_id_type=MESH)
    pl.semaphore_wait(barrier, len(targets))


TAIL_KINDS = (("core", "square", "z"),)
TAIL_CHUNKS = 2
MIDDLE_STARTS = (("core", "x", "y"), ("core", "y", "x"))
MIDDLE_CHUNKS = 2
MIDDLE_TIMES = (1, 5, 7)


def backward_kernel(
    frames,
    count,
    clip_count,
    clip_len,
    latents,
    time_embed,
    mod_rows,
    grad_attn_out,
    sums,
    weights,
    grad_att,
    attention,
    stats,
    mod_all,
    mod_peer,
    pairs,
    queries_in,
    w_qkv,
    spread_q,
    spread_o,
    sum_heads,
    grad_latents,
    tail_result,
    result,
    data,
    tail,
    grad_mod,
    grad_w,
    pack_out,
    pack_in,
    queries,
    grads,
    query_grad,
    key_grad,
    value_grad,
    flat_kv,
    part_out,
    part_in,
    peer_out,
    peer_in,
    held,
    held_mod,
    held_sem,
    load_sem,
    query_sem,
    send_sem,
    recv_sem,
    *scratch,
):
    batch, frame, side, column, peer = place()
    width = grad_att.shape[1]
    slots = part_out.shape[0]
    load = pltpu.make_async_copy(weights, data, load_sem)
    load.start()
    load_queries = pltpu.make_async_copy(queries_in, queries, query_sem)
    load_queries.start()
    head_size = width // HEADS

    def block_at(step):
        return jnp.where(step == count, column, nearest(count - step, column, count))

    def fetches(step):
        slot = lax.rem(step - 1, 2)
        block = block_at(step)
        return (
            pltpu.make_async_copy(pairs.at[block], held.at[slot], held_sem.at[slot]),
            pltpu.make_async_copy(mod_all.at[block], held_mod.at[slot], held_sem.at[2 + slot]),
        )

    def fetch(step):
        for copy in fetches(step):
            copy.start()

    def fetched(step):
        for copy in fetches(step):
            copy.wait()

    fetch(1)
    fetch(2)
    greet_all(count)
    load.wait()
    kinds = middle_kinds(count)
    levels = len(kinds[0])
    chunks = len(chunk_rows(data.shape[0], MIDDLE_CHUNKS, count))
    own = scratch[: levels * chunks + 2]
    items = make_summing(kinds, data, result, own, MIDDLE_CHUNKS, count)
    waiting = [list(group) for group in zip(*(item.steps() for item in items))]
    tail_items = make_summing(TAIL_KINDS, tail, tail_result, scratch[len(own) :], TAIL_CHUNKS, count)
    tail_waiting = [list(group) for group in zip(*(item.steps() for item in tail_items))]

    def advance(queue):
        if queue:
            for run in queue.pop(0):
                run()

    done = []

    def part_done():
        done.append(0)
        if len(done) in MIDDLE_TIMES:
            advance(waiting)

    advance(waiting)

    def to_peer(source, target, slot):
        return pltpu.make_async_remote_copy(
            src_ref=source,
            dst_ref=target,
            send_sem=send_sem.at[slot],
            recv_sem=recv_sem.at[slot],
            device_id=(batch, peer),
            device_id_type=MESH,
        )

    def toward(step, owner):
        up = owner > column
        other = jnp.where(up, column + 1, column - 1)
        slot = jnp.where((other == owner) & jnp.logical_not(up), count, owner)
        return pltpu.make_async_remote_copy(
            src_ref=part_out.at[lax.rem(step, slots)],
            dst_ref=part_in.at[slot],
            send_sem=send_sem.at[2 + step],
            recv_sem=recv_sem.at[2 + slot],
            device_id=(batch, 2 * other + side),
            device_id_type=MESH,
        )

    def arrived(slot):
        pltpu.make_async_remote_copy(
            src_ref=part_out.at[0],
            dst_ref=part_in.at[slot],
            send_sem=send_sem.at[2],
            recv_sem=recv_sem.at[2 + slot],
            device_id=(batch, peer),
            device_id_type=MESH,
        ).wait_recv()

    def pass_on(step):
        block = block_at(step)
        arrived(block)
        slot = lax.rem(step, slots)
        part_out[slot] = (part_out[slot].astype(f32) + part_in[block].astype(f32)).astype(bf16)
        toward(step, block).start()

    def chain_kind(step):
        block = block_at(step)
        up = block > column
        begins = jnp.where(up, column == 0, column == count - 1)
        late = jnp.where(column < count // 2, up, jnp.logical_not(up))
        return begins, late

    def pass_late(step):
        begins, late = chain_kind(step)

        @pl.when(jnp.logical_not(begins) & late)
        def _():
            pass_on(step)

    grad_now = grad_att[...]
    product = grad_now.astype(f32) * attention[...].astype(f32)
    high, middle, low = pieces(product)
    delta = (
        dg(high, sum_heads[...], NN) + dg(middle, sum_heads[...], NN) + dg(low, sum_heads[...], NN)
    )
    high, middle, low = (piece.astype(f32) for piece in pieces(-delta))
    which = lax.rem(lax.broadcasted_iota(jnp.int32, delta.shape, 1), 3)
    extra = jnp.where(which == 0, high, jnp.where(which == 1, middle, low))
    pack_out[:, :width] = grad_now
    pack_out[:, width:] = stats[...] + extra.astype(bf16)
    swap = to_peer(pack_out, pack_in, 0)
    swap.start()
    query_grad[...] = jnp.zeros_like(query_grad)

    def prepare(half, source):
        rows = pl.ds(half * frames, frames)
        wide = dg(source, spread_o[...], NN)
        extra = dg(source[:, width:], spread_q[...], NN).astype(bf16)
        wide = wide.astype(bf16)
        for head in range(HEADS):
            lanes = slice(head * LANES, (head + 1) * LANES)
            grads[head, rows, :] = wide[:, lanes]
            queries[head, rows, :] += extra[:, lanes]

    def differentiate(half, slot, first, moving=True):
        rows = pl.ds(half * frames, frames)
        for head in range(HEADS):
            key, value = held[slot, 0, head], held[slot, 1, head]
            query, grad = queries[head, rows, :], grads[head, rows, :]
            probs = jnp.exp(dg(key, query, NT))
            dscore = (probs * dg(value, grad, NT)).astype(bf16)
            probs = probs.astype(bf16)
            more_k, more_v = dg(dscore, query, NN), dg(probs, grad, NN)
            if first:
                key_grad[slot, head] = more_k
                value_grad[slot, head] = more_v
            else:
                key_grad[slot, head] += more_k
                value_grad[slot, head] += more_v
            query_grad[head, :, rows] += dg(key, dscore, TN)
        if moving:
            part_done()

    def finish_keys(slot):
        for kind, source in enumerate((key_grad, value_grad)):
            for pair in range(HEADS // 2):
                start = kind * width + pair * LANES
                flat_kv[:, start : start + LANES] = jnp.concatenate(
                    [
                        source[slot, 2 * pair][:, :head_size],
                        source[slot, 2 * pair + 1][:, :head_size],
                    ],
                    axis=1,
                ).astype(bf16)
        flat = flat_kv[...]
        return dg(flat, w_qkv[:, width:], NT), dg(held_mod[slot], flat, TN)

    def finish_queries(half, source):
        rows = pl.ds(half * frames, frames)
        flat = jnp.concatenate(
            [query_grad[head, :head_size, rows] for head in range(HEADS)], axis=0
        )
        flat = (flat * 0.125).T.astype(bf16)
        return dg(flat, w_qkv[:, :width], NT), dg(source, flat, TN)

    def send_block(step, slot, first):
        block = block_at(step)
        part, weight = finish_keys(slot)
        if not isinstance(step, int):

            @pl.when(step > slots)
            def _():
                toward(step - slots, block_at(step - slots)).wait_send()

        part_out[lax.rem(step, slots)] = part.astype(bf16)
        if first is False:
            pass_late(step - 1)
        begins, late = chain_kind(step)

        @pl.when(begins)
        def _():
            toward(step, block).start()

        @pl.when(jnp.logical_not(begins) & jnp.logical_not(late))
        def _():
            pass_on(step)

        if first:
            grad_w[:, width:] = weight
        else:
            grad_w[:, width:] += weight

        @pl.when(step + 2 <= count)
        def _():
            fetch(step + 2)

    load_queries.wait()
    prepare(0, pack_out[...])
    fetched(1)
    differentiate(0, 0, True)
    fetched(2)
    differentiate(0, 1, True)
    swap.wait()
    prepare(1, pack_in[...])
    differentiate(1, 0, False)
    send_block(1, 0, True)
    differentiate(1, 1, False)
    send_block(2, 1, False)

    def per_block(step, moving):
        slot = (step - 1) % 2 if isinstance(step, int) else lax.rem(step - 1, 2)
        fetched(step)
        differentiate(0, slot, True, moving)
        differentiate(1, slot, False, moving)
        send_block(step, slot, False)

    if count <= 4:
        for step in range(3, count):
            per_block(step, True)
    else:

        def looped(step, unused):
            per_block(step, False)
            return unused

        lax.fori_loop(3, count, looped, 0)
    slot = (count - 1) % 2
    fetched(count)
    differentiate(1, slot, True)
    pass_late(count - 1)
    part, weight = finish_queries(1, mod_peer[...])
    peer_out[...] = part.astype(bf16)
    back = to_peer(peer_out, peer_in, 1)
    back.start()
    grad_w[:, :width] = weight
    differentiate(0, slot, False)
    part, weight = finish_keys(slot)
    grad_w[:, width:] += weight
    mine, weight = finish_queries(0, held_mod[slot])
    grad_w[:, :width] += weight
    first = 0
    for part_index in range(3):
        tail[first : first + width, :] = grad_w[
            :, part_index * width : (part_index + 1) * width
        ].astype(bf16)
        first += width
    tail_waiting[0].pop(0)()
    grad_mod[...] = part + mine

    choice = row_choice(clip_ids(clip_len, clip_count, frame * frames, (frames, 16)), clip_count)
    ids = clip_ids(clip_len, clip_count, frame * frames, (frames, 16))
    lane = lax.broadcasted_iota(jnp.int32, (frames, 16), 1)
    members = ((lane == batch * clip_count + ids) & (ids < clip_count)).astype(f32).astype(bf16)
    normed, inverse = layer_norm(latents[...].astype(f32))
    scale = 1.0 + dg(choice, mod_rows[:, width : 2 * width], NN)
    first += 32
    for part in range(5):
        tail[first : first + 16, :] = sums[part].astype(bf16)
        first += 16
    time_low = time_embed[...].astype(f32)
    time_low = time_low / (1.0 + jnp.exp(-time_low))
    repeated = jnp.concatenate([time_low] * (16 // clip_count), axis=0)
    row = lax.broadcasted_iota(jnp.int32, (16, width), 0)
    mine = (lax.div(row, clip_count) == batch) & (frame == 0)
    tail[first : first + 16, :] = jnp.where(mine, repeated, 0.0).astype(bf16)
    first += 16
    tail[first:, :] = jnp.zeros((tail.shape[0] - first, width), bf16)

    @pl.when(column > 0)
    def _():
        arrived(column)
        grad_mod[...] += part_in[column].astype(f32)

    @pl.when(column < count - 1)
    def _():
        arrived(count)
        grad_mod[...] += part_in[count].astype(f32)

    back.wait()
    total = grad_mod[...] + peer_in[...].astype(f32)
    grad_latents[...] = (
        grad_attn_out[...] + norm_back(total * scale, normed, inverse)
    ).astype(bf16)
    first = 3 * width
    tail[first : first + 16, :] = clip_sums(members, total).astype(bf16)
    tail[first + 16 : first + 32, :] = clip_sums(members, total * normed).astype(bf16)

    advance(tail_waiting)
    while waiting or tail_waiting:
        advance(tail_waiting)
        advance(waiting)

    def sent(step, unused):
        toward(step, block_at(step)).wait_send()
        return unused

    lax.fori_loop(max(1, count - slots), count, sent, 0)
    for item in items + tail_items:
        item.finish()


def backward_attention(clip_len, *given, count):
    latents, weights = given[0], given[5]
    frames, width = latents.shape
    slots = min(count, 4)
    tail_rows = round_up(3 * width + 8 * 16, count)
    vmem = pl.BlockSpec(memory_space=pltpu.VMEM)
    anywhere = pl.BlockSpec(memory_space=pl.ANY)
    specs = [vmem] * 5 + [anywhere] + [vmem] * 3 + [anywhere, vmem] + [anywhere] * 2 + [vmem] * 4
    return pl.pallas_call(
        functools.partial(backward_kernel, frames, count, clip_len.shape[1]),
        name="attention_backward",
        out_shape=(
            jax.ShapeDtypeStruct((frames, width), bf16),
            jax.ShapeDtypeStruct((tail_rows, width), bf16),
            jax.ShapeDtypeStruct(weights.shape, bf16),
        ),
        in_specs=[pl.BlockSpec(memory_space=pltpu.SMEM)] + specs,
        out_specs=(vmem,) * 3,
        scratch_shapes=[
            pltpu.VMEM(weights.shape, bf16),
            pltpu.VMEM((tail_rows, width), bf16),
            pltpu.VMEM((frames, width), f32),
            pltpu.VMEM((width, 3 * width), f32),
            pltpu.VMEM((frames, width + LANES), bf16),
            pltpu.VMEM((frames, width + LANES), bf16),
            pltpu.VMEM((HEADS, 2 * frames, LANES), bf16),
            pltpu.VMEM((HEADS, 2 * frames, LANES), bf16),
            pltpu.VMEM((HEADS, LANES, 2 * frames), f32),
            pltpu.VMEM((2, HEADS, frames, LANES), f32),
            pltpu.VMEM((2, HEADS, frames, LANES), f32),
            pltpu.VMEM((frames, 2 * width), bf16),
            pltpu.VMEM((slots, frames, width), bf16),
            pltpu.VMEM((count + 1, frames, width), bf16),
            pltpu.VMEM((frames, width), bf16),
            pltpu.VMEM((frames, width), bf16),
            pltpu.VMEM((2, 2, HEADS, frames, LANES), bf16),
            pltpu.VMEM((2, frames, width), bf16),
            pltpu.SemaphoreType.DMA((4,)),
            pltpu.SemaphoreType.DMA,
            pltpu.SemaphoreType.DMA,
            pltpu.SemaphoreType.DMA((2 + count,)),
            pltpu.SemaphoreType.DMA((3 + count,)),
        ]
        + summing_scratch(middle_kinds(count), weights.shape[0], MIDDLE_CHUNKS, count)
        + summing_scratch(TAIL_KINDS, tail_rows, TAIL_CHUNKS, count),
        compiler_params=pltpu.CompilerParams(
            collective_id=2, has_side_effects=True, vmem_limit_bytes=63 * 2**20
        ),
    )(clip_len, *given)


def spread_matrices(width):
    head_size = width // HEADS
    lane = np.arange(HEADS * LANES, dtype=np.int32)[None, :]
    head, inner = lane // LANES, lane % LANES
    row = np.arange(LANES, dtype=np.int32)[:, None]
    spread_q = (row < 3 * HEADS) & (head == row // 3) & (inner == head_size + 4 + row % 3)
    row = np.arange(width, dtype=np.int32)[:, None]
    spread_o = [(head == row // head_size) & (inner == row % head_size)]
    row = np.arange(LANES, dtype=np.int32)[:, None] - 3 * HEADS
    spread_o.append((row >= 0) & (head == row // 3) & (inner == head_size + row % 3))
    column = np.arange(LANES, dtype=np.int32)[None, :] - 3 * HEADS
    sum_heads = np.arange(width, dtype=np.int32)[:, None] // head_size == column // 3
    return (
        spread_q.astype(bf16),
        np.concatenate(spread_o, axis=0).astype(bf16),
        sum_heads.astype(bf16),
    )


def per_device(
    latents,
    time_embed,
    text_states,
    text_len,
    clip_len,
    cotangent,
    w_ada,
    b_ada,
    w_qkv,
    w_ao,
    gain_cross,
    w_cq,
    w_ckv,
    w_co,
    w_up,
    w_down,
):
    frames = latents.shape[1]
    width = latents.shape[2]
    clip_count = time_embed.shape[1]
    text_slots = text_states.shape[2]
    count = lax.axis_size("frame") // 2
    attention, stats, mod_rows, mod_all, mod_peer, pairs, queries = forward_attention(
        clip_len, latents[0], time_embed[0], w_ada, b_ada[None], w_qkv, count
    )
    text_rows = text_states[0].reshape(clip_count * text_slots, text_states.shape[3])
    mixed, grad_attention, grad_attn_out, sums, weights = middle_part(
        clip_len,
        text_len,
        latents[0],
        cotangent[0],
        attention,
        mod_rows,
        text_rows,
        gain_cross[None],
        w_ao,
        w_cq,
        w_ckv,
        w_co,
        w_up,
        w_down,
        count=count,
    )

    grad_latents, tail, weights = backward_attention(
        clip_len,
        latents[0],
        time_embed[0],
        mod_rows,
        grad_attn_out,
        sums,
        weights,
        grad_attention,
        attention,
        stats,
        mod_all,
        mod_peer,
        pairs,
        queries,
        w_qkv,
        *spread_matrices(width),
        count=count,
    )
    middle, first = [], 0
    for length in middle_lengths(width, text_rows.shape[1], w_up.shape[1]):
        middle.append(weights[first : first + length].astype(f32))
        first += length
    tail = tail.astype(f32)
    parts = [tail[first : first + width] for first in (0, width, 2 * width)]
    rows = tail[3 * width : 3 * width + 8 * 16].reshape(8, 16, width)
    spread_rows = jnp.concatenate([rows[part] for part in range(6)], axis=1)
    grad_w_ada = jnp.dot(rows[7].T, spread_rows, precision=highest)
    parted = 2 * (w_up.shape[1] // width)
    grad_w_down = jnp.concatenate(middle[0:parted:2], axis=0)
    grad_w_up = jnp.concatenate(middle[1:parted:2], axis=1)
    grad_w_co, text_keys, text_values, grad_w_cq, grad_w_ao = middle[parted:]
    return (
        mixed[None],
        grad_latents[None],
        grad_w_ada,
        jnp.sum(spread_rows, axis=0),
        jnp.concatenate(parts, axis=1),
        grad_w_ao,
        rows[6, 0],
        grad_w_cq,
        jnp.concatenate([text_keys, text_values], axis=1),
        grad_w_co,
        grad_w_up,
        grad_w_down,
    )


def solution(mesh):
    placed = (
        P("batch", "frame", None),
        P("batch", None, None),
        P("batch", None, None, None),
        P("batch", None),
        P("batch", None),
        P("batch", "frame", None),
    ) + (P(),) * 10
    return jax.shard_map(
        per_device,
        mesh=mesh,
        in_specs=placed,
        out_specs=(P("batch", "frame", None), P("batch", "frame", None)) + (P(),) * 10,
        check_vma=False,
    )
```

```python
import functools
import math

import jax
import jax.numpy as jnp
import numpy as np
from jax import lax
from jax.experimental import pallas as pl
from jax.experimental.pallas import tpu as pltpu
from jax.sharding import PartitionSpec as P

HEADS = 6
LANES = 128
MASKED = -1e30

f32 = jnp.float32
bf16 = jnp.bfloat16
eps_norm = 1e-06
MESH = pl.DeviceIdType.MESH

NT = (((1,), (1,)), ((), ()))
NN = (((1,), (0,)), ((), ()))
TN = (((0,), (0,)), ((), ()))


def dg(left, right, dims):
    return lax.dot_general(left, right, dims, preferred_element_type=f32)


def layer_norm(values):
    center = values - jnp.mean(values, axis=-1, keepdims=True)
    inverse = lax.rsqrt(jnp.mean(center * center, axis=-1, keepdims=True) + eps_norm)
    return (center * inverse, inverse)


def norm_back(grad, normed, inverse):
    mean_grad = jnp.mean(grad, axis=-1, keepdims=True)
    mean_prod = jnp.mean(grad * normed, axis=-1, keepdims=True)
    return (grad - mean_grad - normed * mean_prod) * inverse


def pieces(value):
    high = value.astype(bf16)
    rest = value - high.astype(f32)
    middle = rest.astype(bf16)
    low = (rest - middle.astype(f32)).astype(bf16)
    return high, middle, low


def nearest(step, me, count):
    lower = me < count // 2
    mine = jnp.where(lower, me, count - 1 - me)
    index = jnp.where(step - 1 < mine, step - 1, step)
    return jnp.where(lower, index, count - 1 - index)


def place():
    batch = lax.axis_index("batch")
    frame = lax.axis_index("frame")
    side = lax.rem(frame, 2)
    column = lax.div(frame, 2)
    return batch, frame, side, column, frame + 1 - 2 * side


def greet(batch, side, column, count, peer):
    barrier = pltpu.get_barrier_semaphore()
    pl.semaphore_signal(barrier, inc=1, device_id=(batch, peer), device_id_type=MESH)
    for step in range(1, count):
        other = nearest(step, column, count)
        pl.semaphore_signal(
            barrier, inc=1, device_id=(batch, 2 * other + side), device_id_type=MESH
        )
    pl.semaphore_wait(barrier, count)


def clip_ids(clip_len, clip_count, first, shape):
    position = first + lax.broadcasted_iota(jnp.int32, shape, 0)
    ids = jnp.zeros(shape, jnp.int32)
    end = 0
    for clip in range(clip_count):
        end = end + clip_len[0, clip]
        ids += (position >= end).astype(jnp.int32)
    return ids


def row_choice(ids, clip_count):
    lane = lax.broadcasted_iota(jnp.int32, ids.shape, 1)
    return ((lax.rem(lane, clip_count) == ids) & (lane < 3 * clip_count)).astype(bf16)


def head_tile(flat, head, tail):
    size = LANES - tail.shape[1]
    return jnp.concatenate([flat[:, head * size : (head + 1) * size], tail], axis=1)


def forward_kernel(
    frames,
    count,
    clip_count,
    clip_len,
    latents,
    time_embed,
    w_ada,
    b_ada,
    w_qkv,
    attention,
    stats,
    mod_rows,
    mod_all,
    mod_peer,
    pairs,
    queries,
    total,
    tops,
    part_out,
    part_in,
    stat_out,
    stat_in,
    send_sem,
    recv_sem,
):
    batch, frame, side, column, peer = place()
    width = latents.shape[1]
    head_size = width // HEADS
    greet(batch, side, column, count, peer)

    def to_peer(source, target, slot):
        return pltpu.make_async_remote_copy(
            src_ref=source,
            dst_ref=target,
            send_sem=send_sem.at[slot],
            recv_sem=recv_sem.at[slot],
            device_id=(batch, peer),
            device_id_type=MESH,
        )

    def to_column(step, other, slot):
        return pltpu.make_async_remote_copy(
            src_ref=mod_all.at[slot],
            dst_ref=mod_all.at[slot],
            send_sem=send_sem.at[2 + step],
            recv_sem=recv_sem.at[3 + slot],
            device_id=(batch, 2 * other + side),
            device_id_type=MESH,
        )

    time_low = time_embed[...].astype(f32)
    time_low = (time_low / (1.0 + jnp.exp(-time_low))).astype(bf16)
    modulation = dg(time_low, w_ada[...], NN) + b_ada[...]
    parts = [piece.astype(f32) for piece in pieces(modulation)]
    parts.append(jnp.zeros((16 - 3 * clip_count, modulation.shape[1]), f32))
    mod_rows[...] = jnp.concatenate(parts, axis=0).astype(bf16)
    choice = row_choice(clip_ids(clip_len, clip_count, frame * frames, (frames, 16)), clip_count)
    normed, inverse = layer_norm(latents[...].astype(f32))
    shift, scale = (
        dg(choice, mod_rows[:, part * width : (part + 1) * width], NN) for part in range(2)
    )
    mod_all[column] = (normed * (1.0 + scale) + shift).astype(bf16)
    swap = to_peer(mod_all.at[column], mod_peer, 0)
    relayed = count == 4

    def hop(block, up):
        other = column + 1 if up else column - 1
        return pltpu.make_async_remote_copy(
            src_ref=mod_all.at[block],
            dst_ref=mod_all.at[block],
            send_sem=send_sem.at[2 + block + (0 if up else count)],
            recv_sem=recv_sem.at[3 + block],
            device_id=(batch, 2 * other + side),
            device_id_type=MESH,
        )

    def each_hop(distance, act):
        for up in (True, False):
            block = column - distance if up else column + distance
            here = block >= 0 if up else block < count
            further = column < count - 1 if up else column > 0
            act(block, up, here, further)

    def begin(block, up, here, further):
        @pl.when(here & further)
        def _():
            hop(block, up).start()

    def take(block, up, here, further):
        @pl.when(here)
        def _():
            hop(block, up).wait_recv()

        begin(block, up, here, further)

    def end(block, up, here, further):
        @pl.when(here & further)
        def _():
            hop(block, up).wait_send()

    if relayed:
        each_hop(0, begin)
        swap.start()
    else:
        sends = [
            to_column(step, nearest(step, column, count), column) for step in range(1, count)
        ]
        for index, send in enumerate(sends):
            send.start()
            if index == 0:
                swap.start()
    total[...] = jnp.zeros_like(total)
    tops[...] = jnp.full_like(tops, -1e38)
    tail = (frames, LANES - head_size)
    lane = lax.broadcasted_iota(jnp.int32, tail, 1)
    ones = jnp.ones(tail, bf16)

    def make_queries(half, owner, source):
        rows = pl.ds(half * frames, frames)
        flat = dg(source, w_qkv[:, :width], NN).astype(bf16) * 0.125
        ids = clip_ids(clip_len, clip_count, owner * frames, tail)
        extra = (ids == lane).astype(f32).astype(bf16)
        for head in range(HEADS):
            queries[head, rows, :] = head_tile(flat, head, extra)

    def make_keys(block):
        source = mod_all[block]
        ids = clip_ids(clip_len, clip_count, (2 * block + side) * frames, tail)
        masks = jnp.where((ids == lane) | (lane > clip_count), 0.0, MASKED)
        extra = jnp.where(
            lane < clip_count, masks, jnp.where(lane < clip_count + 3, 1.0, 0.0)
        ).astype(bf16)
        flat = dg(source, w_qkv[:, width : 2 * width], NN).astype(bf16)
        for head in range(HEADS):
            pairs[block, 0, head] = head_tile(flat, head, extra)
        flat = dg(source, w_qkv[:, 2 * width :], NN).astype(bf16)
        for head in range(HEADS):
            pairs[block, 1, head] = head_tile(flat, head, ones)

    def attend(half, block):
        rows = pl.ds(half * frames, frames)

        def scores(head):
            now = dg(pairs[block, 0, head], queries[head, rows, :], NT)
            return now, jnp.max(now, axis=0, keepdims=True)

        ahead = scores(0)
        for head in range(HEADS):
            now, top = ahead
            if head + 1 < HEADS:
                ahead = scores(head + 1)
            before = tops[head, :1, rows]
            new = jnp.maximum(before, top)
            probs = jnp.exp(now - new).astype(bf16)
            total[head, :, rows] = total[head, :, rows] * jnp.exp(before - new) + dg(
                pairs[block, 1, head], probs, TN
            )
            tops[head, :, rows] = jnp.broadcast_to(new, (8, frames))

    def arrive(step):
        block = nearest(step, column, count)
        if not relayed:
            to_column(step, block, block).wait_recv()
        make_keys(block)
        return block

    make_queries(0, frame, mod_all[column])
    make_keys(column)
    attend(0, column)
    swap.wait()
    make_queries(1, peer, mod_peer[...])
    attend(1, column)

    if relayed:
        outer = (column == 0) | (column == count - 1)
        each_hop(1, take)
        block = arrive(1)
        attend(0, block)
        attend(1, block)

        @pl.when(outer)
        def _():
            each_hop(2, take)

        block = arrive(2)
        attend(0, block)

        @pl.when(jnp.logical_not(outer))
        def _():
            each_hop(2, take)

        attend(1, block)
        each_hop(3, take)
    else:

        def per_block(step, unused):
            block = arrive(step)
            attend(0, block)
            attend(1, block)
            return unused

        lax.fori_loop(1, count - 1, per_block, 0)
    block = arrive(count - 1)
    attend(1, block)
    there = pl.ds(frames, frames)
    for head in range(HEADS):
        part_out[head * head_size : (head + 1) * head_size, :] = total[
            head, :head_size, there
        ].astype(bf16)
        stat_out[head : head + 1, :] = tops[head, :1, there]
        stat_out[8 + head : 9 + head, :] = total[head, head_size : head_size + 1, there]
    parts = to_peer(part_out, part_in, 1)
    numbers = to_peer(stat_out, stat_in, 2)
    numbers.start()
    parts.start()
    attend(0, block)
    numbers.wait()
    parts.wait()
    here = pl.ds(0, frames)
    joined = []
    logs = []
    for head in range(HEADS):
        mine, theirs = tops[head, :1, here], stat_in[head : head + 1, :]
        new = jnp.maximum(mine, theirs)
        left, right = jnp.exp(mine - new), jnp.exp(theirs - new)
        row_sum = (
            total[head, head_size : head_size + 1, here] * left
            + stat_in[8 + head : 9 + head, :] * right
        )
        logs.append(new + jnp.log(row_sum))
        scale = 1.0 / row_sum
        joined.append(
            total[head, :head_size, here] * (left * scale)
            + part_in[head * head_size : (head + 1) * head_size, :].astype(f32) * (right * scale)
        )
    attention[...] = jnp.concatenate(joined, axis=0).T.astype(bf16)
    rows = [piece for log in logs for piece in log_pieces(log)]
    rows.append(jnp.zeros((LANES - len(rows), frames), f32))
    stats[...] = jnp.concatenate(rows, axis=0).T.astype(bf16)
    if relayed:
        for distance in range(count - 1):
            each_hop(distance, end)
    else:
        for send in sends:
            send.wait_send()


def log_pieces(log):
    high, middle, low = pieces(-log)
    return [high.astype(f32), middle.astype(f32), low.astype(f32)]


def forward_attention(clip_len, latents, time_embed, w_ada, b_ada, w_qkv, count):
    frames, width = latents.shape
    clip_count = clip_len.shape[1]
    vmem = pl.BlockSpec(memory_space=pltpu.VMEM)
    shapes = (
        jax.ShapeDtypeStruct((frames, width), bf16),
        jax.ShapeDtypeStruct((frames, LANES), bf16),
        jax.ShapeDtypeStruct((16, w_ada.shape[1]), bf16),
        jax.ShapeDtypeStruct((count, frames, width), bf16),
        jax.ShapeDtypeStruct((frames, width), bf16),
        jax.ShapeDtypeStruct((count, 2, HEADS, frames, LANES), bf16),
        jax.ShapeDtypeStruct((HEADS, 2 * frames, LANES), bf16),
    )
    return pl.pallas_call(
        functools.partial(forward_kernel, frames, count, clip_count),
        name="attention_forward",
        out_shape=shapes,
        in_specs=[pl.BlockSpec(memory_space=pltpu.SMEM)] + [vmem] * 5,
        out_specs=(vmem,) * 7,
        scratch_shapes=[
            pltpu.VMEM((HEADS, LANES, 2 * frames), f32),
            pltpu.VMEM((HEADS, 8, 2 * frames), f32),
            pltpu.VMEM((width, frames), bf16),
            pltpu.VMEM((width, frames), bf16),
            pltpu.VMEM((16, frames), f32),
            pltpu.VMEM((16, frames), f32),
            pltpu.SemaphoreType.DMA((2 + 2 * count,)),
            pltpu.SemaphoreType.DMA((3 + count,)),
        ],
        compiler_params=pltpu.CompilerParams(
            collective_id=1, has_side_effects=True, vmem_limit_bytes=62 * 2**20
        ),
    )(clip_len, latents, time_embed, w_ada, b_ada, w_qkv)


def clip_sums(choice, value):
    high = value.astype(bf16)
    low = (value - high.astype(f32)).astype(bf16)
    return dg(choice, high, TN) + dg(choice, low, TN)


def middle_kernel(
    frames,
    clip_count,
    clip_len,
    text_len,
    latents,
    cotangent,
    attention,
    mod_rows,
    text_rows,
    gain_cross,
    w_ao,
    w_cq,
    w_ckv,
    w_co,
    w_up,
    w_down,
    mixed,
    grad_att,
    grad_attn_out,
    sums,
    weights,
    key_tiles,
    query_tiles,
    grad_tiles,
    probs_kept,
    flat_kv,
):
    batch, frame, side, column, peer = place()
    width = latents.shape[1]
    head_size = width // HEADS
    slots = text_rows.shape[0]
    per_clip = slots // clip_count
    tail = (frames, LANES - head_size)

    wide_ids = clip_ids(clip_len, clip_count, frame * frames, (frames, 16))
    choice = row_choice(wide_ids, clip_count)
    group_lane = lax.broadcasted_iota(jnp.int32, (frames, 16), 1)
    members = ((group_lane == batch * clip_count + wide_ids) & (wide_ids < clip_count)).astype(f32)
    members = members.astype(bf16)
    ids = clip_ids(clip_len, clip_count, frame * frames, (frames, width))
    valid = (ids < clip_count).astype(f32)

    def mod_part(part):
        return dg(choice, mod_rows[:, part * width : (part + 1) * width], NN)

    gate_attn = mod_part(2) * valid
    branch_attn = dg(attention[...], w_ao[...], NN)
    after_attn = latents[...].astype(f32) + gate_attn * branch_attn
    normed_cross, inverse_cross = layer_norm(after_attn)
    gain = gain_cross[...]
    cross_in = (normed_cross * gain).astype(bf16)

    flat = dg(cross_in, w_cq[...], NN).astype(bf16) * 0.125
    lane = lax.broadcasted_iota(jnp.int32, tail, 1)
    extra = (clip_ids(clip_len, clip_count, frame * frames, tail) == lane).astype(f32).astype(bf16)
    for head in range(HEADS):
        query_tiles[head] = head_tile(flat, head, extra)
    slot = lax.broadcasted_iota(jnp.int32, (slots, LANES - head_size), 0)
    lane = lax.broadcasted_iota(jnp.int32, (slots, LANES - head_size), 1)
    live = jnp.zeros(lane.shape, jnp.bool_)
    for clip in range(clip_count):
        inside = (slot >= clip * per_clip) & (slot < clip * per_clip + text_len[0, clip])
        live = live | (inside & (lane == clip))
    extra = jnp.where(live | (lane >= clip_count), 0.0, MASKED).astype(bf16)
    flat = dg(text_rows[...], w_ckv[:, :width], NN).astype(bf16)
    for head in range(HEADS):
        key_tiles[0, head] = head_tile(flat, head, extra)
    extra = (lane < 3).astype(f32).astype(bf16)
    flat = dg(text_rows[...], w_ckv[:, width:], NN).astype(bf16)
    for head in range(HEADS):
        key_tiles[1, head] = head_tile(flat, head, extra)

    def scores(head):
        now = dg(key_tiles[0, head], query_tiles[head], NT)
        return now, jnp.max(now, axis=0, keepdims=True)

    joined = []
    ahead = scores(0)
    for head in range(HEADS):
        now, top = ahead
        if head + 1 < HEADS:
            ahead = scores(head + 1)
        probs = jnp.exp(now - top)
        probs = (probs * (1.0 / jnp.sum(probs, axis=0, keepdims=True))).astype(bf16)
        probs_kept[head] = probs
        joined.append(dg(key_tiles[1, head], probs, TN)[:head_size])
    cross_exact = jnp.concatenate(joined, axis=0).T
    cross = cross_exact.astype(bf16)
    after_cross = after_attn + dg(cross, w_co[...], NN) * valid
    normed_mlp, inverse_mlp = layer_norm(after_cross)
    scale_mlp = 1.0 + mod_part(4)
    mlp_in = (normed_mlp * scale_mlp + mod_part(3)).astype(bf16)
    gate_mlp = mod_part(5) * valid
    grad_out = cotangent[...].astype(f32)
    grad_mlp = (grad_out * gate_mlp).astype(bf16)
    root = math.sqrt(2.0 / math.pi)
    branch_mlp = jnp.zeros((frames, width), f32)
    grad_mlp_in = jnp.zeros((frames, width), f32)
    hidden_width = w_up.shape[1]
    first = 0
    for part in range(hidden_width // width):
        here = slice(part * width, (part + 1) * width)
        hidden = dg(mlp_in, w_up[:, here], NN)
        square = hidden * hidden
        bend = jnp.tanh(root * hidden * (1.0 + 0.044715 * square))
        half = 0.5 * (1.0 + bend)
        activated = (hidden * half).astype(bf16)
        slope = half + (0.5 * root) * hidden * (1.0 - bend * bend) * (1.0 + 0.134145 * square)
        grad_hidden = (dg(grad_mlp, w_down[here, :], NT) * slope).astype(bf16)
        branch_mlp += dg(activated, w_down[here, :], NN)
        grad_mlp_in += dg(grad_hidden, w_up[:, here], NT)
        weights[first : first + width, :] = dg(activated, grad_mlp, TN).astype(bf16)
        first += width
        weights[first : first + width, :] = dg(mlp_in, grad_hidden, TN).astype(bf16)
        first += width
    mixed[...] = (after_cross + gate_mlp * branch_mlp).astype(bf16)
    sums[3] = clip_sums(members, grad_out * branch_mlp)
    sums[1] = clip_sums(members, grad_mlp_in)
    sums[2] = clip_sums(members, grad_mlp_in * normed_mlp)
    grad_cross_out = grad_out + norm_back(grad_mlp_in * scale_mlp, normed_mlp, inverse_mlp)
    grad_branch = (grad_cross_out * valid).astype(bf16)
    weights[first : first + width, :] = dg(cross, grad_branch, TN).astype(bf16)
    first += width

    flat = dg(grad_branch, w_co[...], NT).astype(bf16)
    product = flat.astype(f32) * cross_exact
    lane = lax.broadcasted_iota(jnp.int32, tail, 1)
    for head in range(HEADS):
        part = product[:, head * head_size : (head + 1) * head_size]
        high, middle, low = pieces(-jnp.sum(part, axis=1, keepdims=True))
        extra = jnp.where(
            lane == 0,
            high.astype(f32),
            jnp.where(lane == 1, middle.astype(f32), jnp.where(lane == 2, low.astype(f32), 0.0)),
        ).astype(bf16)
        grad_tiles[head] = head_tile(flat, head, extra)
    joined = []
    for pair in range(HEADS // 2):
        kept = []
        for head in (2 * pair, 2 * pair + 1):
            probs = probs_kept[head]
            dscore = dg(key_tiles[1, head], grad_tiles[head], NT) * probs.astype(f32)
            dscore = dscore.astype(bf16)
            joined.append(dg(key_tiles[0, head], dscore, TN)[:head_size])
            kept.append(
                (
                    dg(dscore, query_tiles[head], NN)[:, :head_size],
                    dg(probs, grad_tiles[head], NN)[:, :head_size],
                )
            )
        for kind in range(2):
            start = kind * width + pair * LANES
            flat_kv[:, start : start + LANES] = jnp.concatenate(
                [kept[0][kind], kept[1][kind]], axis=1
            ).astype(bf16)
    for kind in range(2):
        grad = dg(text_rows[...], flat_kv[:, kind * width : (kind + 1) * width], TN)
        weights[first : first + grad.shape[0], :] = grad.astype(bf16)
        first += grad.shape[0]
    grad_queries = (jnp.concatenate(joined, axis=0) * 0.125).T.astype(bf16)
    weights[first : first + width, :] = dg(cross_in, grad_queries, TN).astype(bf16)
    first += width
    grad_cross_in = dg(grad_queries, w_cq[...], NT)
    grad_gain = jnp.sum(grad_cross_in * normed_cross, axis=0, keepdims=True)
    top_row = lax.broadcasted_iota(jnp.int32, (16, width), 0) == 0
    sums[4] = jnp.where(top_row, grad_gain, 0.0)
    grad_attn = grad_cross_out + norm_back(grad_cross_in * gain, normed_cross, inverse_cross)
    grad_attn_out[...] = grad_attn
    sums[0] = clip_sums(members, grad_attn * branch_attn)
    grad_branch = (grad_attn * gate_attn).astype(bf16)
    weights[first : first + width, :] = dg(attention[...], grad_branch, TN).astype(bf16)
    first += width
    grad_att[...] = dg(grad_branch, w_ao[...], NT).astype(bf16)
    weights[first:, :] = jnp.zeros((weights.shape[0] - first, width), bf16)


def middle_lengths(width, text_width, hidden_width):
    return [width] * (2 * hidden_width // width + 1) + [text_width] * 2 + [width] * 2


def middle_part(clip_len, text_len, latents, *others, count):
    frames, width = latents.shape
    text_rows, w_up = others[3], others[9]
    slots, text_width = text_rows.shape
    rows = round_up(sum(middle_lengths(width, text_width, w_up.shape[1])), count)
    vmem = pl.BlockSpec(memory_space=pltpu.VMEM)
    smem = pl.BlockSpec(memory_space=pltpu.SMEM)
    return pl.pallas_call(
        functools.partial(middle_kernel, frames, clip_len.shape[1]),
        name="middle",
        out_shape=(
            jax.ShapeDtypeStruct((frames, width), bf16),
            jax.ShapeDtypeStruct((frames, width), bf16),
            jax.ShapeDtypeStruct((frames, width), f32),
            jax.ShapeDtypeStruct((5, 16, width), f32),
            jax.ShapeDtypeStruct((rows, width), bf16),
        ),
        in_specs=[smem] * 2 + [vmem] * 12,
        out_specs=(vmem,) * 5,
        scratch_shapes=[
            pltpu.VMEM((2, HEADS, slots, LANES), bf16),
            pltpu.VMEM((HEADS, frames, LANES), bf16),
            pltpu.VMEM((HEADS, frames, LANES), bf16),
            pltpu.VMEM((HEADS, slots, frames), bf16),
            pltpu.VMEM((slots, 2 * width), bf16),
        ],
        compiler_params=pltpu.CompilerParams(vmem_limit_bytes=62 * 2**20),
    )(clip_len, text_len, latents, *others)


def tile_of(rows):
    return max(tile for tile in range(16, 129, 16) if rows % tile == 0)


def level_size(kind, count):
    return {"square": 4, "z": count}.get(kind, 2)


def level_place(kind):
    batch, frame, side, column, peer = place()
    core, across = lax.rem(batch, 2), lax.div(batch, 2)
    if kind == "core":
        return core, lambda member: (2 * across + member, frame)
    if kind == "x":
        return across, lambda member: (core + 2 * member, frame)
    if kind == "y":
        return side, lambda member: (batch, 2 * column + member)
    if kind == "square":
        return 2 * across + side, lambda member: (
            core + 2 * lax.div(member, 2),
            2 * column + lax.rem(member, 2),
        )
    if kind == "z":
        return column, lambda member: (batch, 2 * member + side)
    bit = int(kind)
    mine = lax.rem(lax.div(column, bit), 2)
    return mine, lambda member: (batch, 2 * (column + bit * (member - mine)) + side)


class Summing:
    def __init__(self, kinds, data, result, landings, send_sem, recv_sem, chunk, first, rows, count):
        self.kinds, self.data, self.result = kinds, data, result
        self.landings, self.send_sem, self.recv_sem, self.chunk = landings, send_sem, recv_sem, chunk
        self.sizes = [level_size(kind, count) for kind in kinds]
        self.places, self.devices = zip(*(level_place(kind) for kind in kinds))
        self.starts, self.lengths = [first], [rows]
        for size, mine in zip(self.sizes, self.places):
            self.lengths.append(self.lengths[-1] // size)
            self.starts.append(self.starts[-1] + mine * self.lengths[-1])
        self.sent = []

    def others(self, level):
        size = self.sizes[level]
        return [lax.rem(self.places[level] + step, size) for step in range(1, size)]

    def rows(self, start, length):
        return pl.ds(pl.multiple_of(start, 16), length)

    def copy(self, way, level, source, target, member, slot):
        base = way * sum(self.sizes) + sum(self.sizes[:level])
        return pltpu.make_async_remote_copy(
            src_ref=source,
            dst_ref=target,
            send_sem=self.send_sem.at[self.chunk, base + member],
            recv_sem=self.recv_sem.at[self.chunk, base + slot],
            device_id=self.devices[level](member),
            device_id_type=MESH,
        )

    def scatter(self, level):
        length = self.lengths[level + 1]
        for member in self.others(level):
            rows = self.rows(self.starts[level] + member * length, length)
            mine = self.places[level]
            copy = self.copy(
                0, level, self.data.at[rows], self.landings[level].at[mine], member, mine
            )
            copy.start()
            self.sent.append(copy)

    def add(self, level):
        length, start = self.lengths[level + 1], self.starts[level + 1]
        others = self.others(level)
        landing = self.landings[level]
        for member in others:
            rows = self.rows(start, length)
            self.copy(0, level, self.data.at[rows], landing.at[member], member, member).wait_recv()
        tile = tile_of(length)
        target = self.result if level == len(self.sizes) - 1 else self.data

        def body(index, unused):
            inner = self.rows(index * tile, tile)
            outer = self.rows(start + index * tile, tile)
            value = self.data[outer, :].astype(f32)
            for member in others:
                value += landing[member, inner, :].astype(f32)
            target[outer, :] = value.astype(bf16)
            return unused

        lax.fori_loop(0, length // tile, body, 0)

    def gather(self, level):
        rows = self.rows(self.starts[level + 1], self.lengths[level + 1])
        mine = self.places[level]
        for member in self.others(level):
            copy = self.copy(1, level, self.result.at[rows], self.result.at[rows], member, mine)
            copy.start()
            self.sent.append(copy)

    def gathered(self, level):
        length = self.lengths[level + 1]
        for member in self.others(level):
            rows = self.rows(self.starts[level] + member * length, length)
            self.copy(
                1, level, self.result.at[rows], self.result.at[rows], member, member
            ).wait_recv()

    def steps(self):
        def step(*calls):
            def run():
                for call, level in calls:
                    call(level)

            return run

        last = len(self.sizes) - 1
        runs = [step((self.scatter, 0))]
        for level in range(last):
            runs.append(step((self.add, level), (self.scatter, level + 1)))
        runs.append(step((self.add, last), (self.gather, last)))
        for level in range(last, 0, -1):
            runs.append(step((self.gathered, level), (self.gather, level - 1)))
        runs.append(step((self.gathered, 0)))
        return runs

    def finish(self):
        for copy in self.sent:
            copy.wait_send()


def middle_kinds(count):
    bits, bit = [], 1
    while bit < count:
        bits.append(str(bit))
        bit *= 2
    bits, back = tuple(bits), tuple(bits[::-1])
    return (
        ("core", "x", "y") + bits,
        ("core", "y", "x") + bits,
        ("core",) + bits + ("x", "y"),
        ("core", "x", "y") + bits,
        ("core", "y", "x") + bits,
        ("core",) + back + ("y", "x"),
    )


def chunk_rows(rows, chunks, count):
    unit = 128 * count
    units = rows // unit
    chunks = min(chunks, units)
    return [(units // chunks + (index < units % chunks)) * unit for index in range(chunks)]


def round_up(rows, count):
    unit = 128 * count
    return -(-rows // unit) * unit


def summing_scratch(kinds, rows, chunks, count):
    shapes = []
    for chunk, length in enumerate(chunk_rows(rows, chunks, count)):
        for kind in kinds[chunk % len(kinds)]:
            length //= level_size(kind, count)
            shapes.append(pltpu.VMEM((level_size(kind, count), length, 384), bf16))
    slots = 2 * sum(level_size(kind, count) for kind in kinds[0])
    return shapes + [pltpu.SemaphoreType.DMA((chunks, slots))] * 2


def make_summing(kinds, data, result, scratch, chunks, count):
    send_sem, recv_sem = scratch[-2:]
    levels = len(kinds[0])
    sums, first = [], 0
    for chunk, length in enumerate(chunk_rows(data.shape[0], chunks, count)):
        landings = scratch[levels * chunk : levels * (chunk + 1)]
        order = kinds[chunk % len(kinds)]
        sums.append(
            Summing(order, data, result, landings, send_sem, recv_sem, chunk, first, length, count)
        )
        first += length
    return sums


def greet_all(count):
    batch, frame, side, column, peer = place()
    core, across = lax.rem(batch, 2), lax.div(batch, 2)
    barrier = pltpu.get_barrier_semaphore()
    targets = [
        (batch + 1 - 2 * core, frame),
        (batch, peer),
        (core + 2 - 2 * across, frame),
        (core + 2 - 2 * across, peer),
    ]
    for step in range(1, count):
        targets.append((batch, 2 * lax.rem(column + step, count) + side))
    for target in targets:
        pl.semaphore_signal(barrier, inc=1, device_id=target, device_id_type=MESH)
    pl.semaphore_wait(barrier, len(targets))


TAIL_KINDS = (("core", "square", "z"), ("core", "z", "square"))
TAIL_CHUNKS = 3
MIDDLE_CHUNKS = 6
MIDDLE_TIMES = (0, 4, 15, 21, 25, 29, 33, 37, 43, 51, 56)
CHUNK_TIME = 0.6


def timed_steps(items):
    runs = [item.steps() for item in items]
    timed = []
    for step in range(len(runs[0])):
        for index, run in enumerate(runs):
            now = MIDDLE_TIMES[min(step, len(MIDDLE_TIMES) - 1)] + CHUNK_TIME * index
            timed.append((now, run[step]))
    return sorted(timed, key=lambda pair: pair[0])


def backward_kernel(
    frames,
    count,
    clip_count,
    clip_len,
    latents,
    time_embed,
    mod_rows,
    grad_attn_out,
    sums,
    weights,
    grad_att,
    attention,
    stats,
    mod_all,
    mod_peer,
    pairs,
    queries_in,
    w_qkv,
    spread_q,
    spread_o,
    sum_heads,
    grad_latents,
    tail_result,
    result,
    data,
    tail,
    grad_mod,
    grad_w,
    pack_out,
    pack_in,
    queries,
    grads,
    query_grad,
    key_grad,
    value_grad,
    flat_kv,
    part_out,
    part_in,
    peer_out,
    peer_in,
    held,
    held_mod,
    held_sem,
    load_sem,
    query_sem,
    send_sem,
    recv_sem,
    *scratch,
):
    batch, frame, side, column, peer = place()
    width = grad_att.shape[1]
    slots = part_out.shape[0]
    load = pltpu.make_async_copy(weights, data, load_sem)
    load.start()
    load_queries = pltpu.make_async_copy(queries_in, queries, query_sem)
    load_queries.start()
    head_size = width // HEADS

    def block_at(step):
        return jnp.where(step == count, column, nearest(count - step, column, count))

    def fetches(step):
        slot = lax.rem(step - 1, 2)
        block = block_at(step)
        return (
            pltpu.make_async_copy(pairs.at[block], held.at[slot], held_sem.at[slot]),
            pltpu.make_async_copy(mod_all.at[block], held_mod.at[slot], held_sem.at[2 + slot]),
        )

    def fetch(step):
        for copy in fetches(step):
            copy.start()

    def fetched(step):
        for copy in fetches(step):
            copy.wait()

    fetch(1)
    fetch(2)
    greet_all(count)
    load.wait()
    kinds = middle_kinds(count)
    levels = len(kinds[0])
    chunks = len(chunk_rows(data.shape[0], MIDDLE_CHUNKS, count))
    own = scratch[: levels * chunks + 2]
    items = make_summing(kinds, data, result, own, MIDDLE_CHUNKS, count)
    waiting = timed_steps(items)
    tail_items = make_summing(TAIL_KINDS, tail, tail_result, scratch[len(own) :], TAIL_CHUNKS, count)
    tail_waiting = [list(group) for group in zip(*(item.steps() for item in tail_items))]
    heads_done = [0]

    def advance():
        while waiting and waiting[0][0] <= heads_done[0]:
            waiting.pop(0)[1]()

    advance()

    def to_peer(source, target, slot):
        return pltpu.make_async_remote_copy(
            src_ref=source,
            dst_ref=target,
            send_sem=send_sem.at[slot],
            recv_sem=recv_sem.at[slot],
            device_id=(batch, peer),
            device_id_type=MESH,
        )

    def toward(step, owner):
        up = owner > column
        other = jnp.where(up, column + 1, column - 1)
        slot = jnp.where((other == owner) & jnp.logical_not(up), count, owner)
        return pltpu.make_async_remote_copy(
            src_ref=part_out.at[lax.rem(step, slots)],
            dst_ref=part_in.at[slot],
            send_sem=send_sem.at[2 + step],
            recv_sem=recv_sem.at[2 + slot],
            device_id=(batch, 2 * other + side),
            device_id_type=MESH,
        )

    def arrived(slot):
        pltpu.make_async_remote_copy(
            src_ref=part_out.at[0],
            dst_ref=part_in.at[slot],
            send_sem=send_sem.at[2],
            recv_sem=recv_sem.at[2 + slot],
            device_id=(batch, peer),
            device_id_type=MESH,
        ).wait_recv()

    def pass_on(step):
        block = block_at(step)
        arrived(block)
        slot = lax.rem(step, slots)
        part_out[slot] = (part_out[slot].astype(f32) + part_in[block].astype(f32)).astype(bf16)
        toward(step, block).start()

    def chain_kind(step):
        block = block_at(step)
        up = block > column
        begins = jnp.where(up, column == 0, column == count - 1)
        late = jnp.where(column < count // 2, up, jnp.logical_not(up))
        return begins, late

    def pass_late(step):
        begins, late = chain_kind(step)

        @pl.when(jnp.logical_not(begins) & late)
        def _():
            pass_on(step)

    grad_now = grad_att[...]
    product = grad_now.astype(f32) * attention[...].astype(f32)
    high, middle, low = pieces(product)
    delta = (
        dg(high, sum_heads[...], NN) + dg(middle, sum_heads[...], NN) + dg(low, sum_heads[...], NN)
    )
    high, middle, low = (piece.astype(f32) for piece in pieces(-delta))
    which = lax.rem(lax.broadcasted_iota(jnp.int32, delta.shape, 1), 3)
    extra = jnp.where(which == 0, high, jnp.where(which == 1, middle, low))
    pack_out[:, :width] = grad_now
    pack_out[:, width:] = stats[...] + extra.astype(bf16)
    swap = to_peer(pack_out, pack_in, 0)
    swap.start()
    query_grad[...] = jnp.zeros_like(query_grad)

    def prepare(half, source):
        rows = pl.ds(half * frames, frames)
        wide = dg(source, spread_o[...], NN)
        extra = dg(source[:, width:], spread_q[...], NN).astype(bf16)
        wide = wide.astype(bf16)
        for head in range(HEADS):
            lanes = slice(head * LANES, (head + 1) * LANES)
            grads[head, rows, :] = wide[:, lanes]
            queries[head, rows, :] += extra[:, lanes]

    def differentiate(half, slot, first, moving=True):
        rows = pl.ds(half * frames, frames)
        for head in range(HEADS):
            key, value = held[slot, 0, head], held[slot, 1, head]
            query, grad = queries[head, rows, :], grads[head, rows, :]
            probs = jnp.exp(dg(key, query, NT))
            dscore = (probs * dg(value, grad, NT)).astype(bf16)
            probs = probs.astype(bf16)
            more_k, more_v = dg(dscore, query, NN), dg(probs, grad, NN)
            if first:
                key_grad[slot, head] = more_k
                value_grad[slot, head] = more_v
            else:
                key_grad[slot, head] += more_k
                value_grad[slot, head] += more_v
            query_grad[head, :, rows] += dg(key, dscore, TN)
            if moving:
                heads_done[0] += 1
                advance()

    def finish_keys(slot):
        for kind, source in enumerate((key_grad, value_grad)):
            for pair in range(HEADS // 2):
                start = kind * width + pair * LANES
                flat_kv[:, start : start + LANES] = jnp.concatenate(
                    [
                        source[slot, 2 * pair][:, :head_size],
                        source[slot, 2 * pair + 1][:, :head_size],
                    ],
                    axis=1,
                ).astype(bf16)
        flat = flat_kv[...]
        return dg(flat, w_qkv[:, width:], NT), dg(held_mod[slot], flat, TN)

    def finish_queries(half, source):
        rows = pl.ds(half * frames, frames)
        flat = jnp.concatenate(
            [query_grad[head, :head_size, rows] for head in range(HEADS)], axis=0
        )
        flat = (flat * 0.125).T.astype(bf16)
        return dg(flat, w_qkv[:, :width], NT), dg(source, flat, TN)

    def send_block(step, slot, first):
        block = block_at(step)
        part, weight = finish_keys(slot)
        if not isinstance(step, int):

            @pl.when(step > slots)
            def _():
                toward(step - slots, block_at(step - slots)).wait_send()

        part_out[lax.rem(step, slots)] = part.astype(bf16)
        if first is False:
            pass_late(step - 1)
        begins, late = chain_kind(step)

        @pl.when(begins)
        def _():
            toward(step, block).start()

        @pl.when(jnp.logical_not(begins) & jnp.logical_not(late))
        def _():
            pass_on(step)

        if first:
            grad_w[:, width:] = weight
        else:
            grad_w[:, width:] += weight

        @pl.when(step + 2 <= count)
        def _():
            fetch(step + 2)

    load_queries.wait()
    prepare(0, pack_out[...])
    fetched(1)
    differentiate(0, 0, True)
    fetched(2)
    differentiate(0, 1, True)
    swap.wait()
    prepare(1, pack_in[...])
    differentiate(1, 0, False)
    send_block(1, 0, True)
    differentiate(1, 1, False)
    send_block(2, 1, False)

    def per_block(step, moving):
        slot = (step - 1) % 2 if isinstance(step, int) else lax.rem(step - 1, 2)
        fetched(step)
        differentiate(0, slot, True, moving)
        differentiate(1, slot, False, moving)
        send_block(step, slot, False)

    if count <= 4:
        for step in range(3, count):
            per_block(step, True)
    else:

        def looped(step, unused):
            per_block(step, False)
            return unused

        lax.fori_loop(3, count, looped, 0)
    slot = (count - 1) % 2
    fetched(count)
    differentiate(1, slot, True)
    pass_late(count - 1)
    part, weight = finish_queries(1, mod_peer[...])
    peer_out[...] = part.astype(bf16)
    back = to_peer(peer_out, peer_in, 1)
    back.start()
    grad_w[:, :width] = weight
    differentiate(0, slot, False)
    part, weight = finish_keys(slot)
    grad_w[:, width:] += weight
    mine, weight = finish_queries(0, held_mod[slot])
    grad_w[:, :width] += weight
    first = 0
    for part_index in range(3):
        tail[first : first + width, :] = grad_w[
            :, part_index * width : (part_index + 1) * width
        ].astype(bf16)
        first += width
    tail_waiting[0].pop(0)()
    grad_mod[...] = part + mine

    choice = row_choice(clip_ids(clip_len, clip_count, frame * frames, (frames, 16)), clip_count)
    ids = clip_ids(clip_len, clip_count, frame * frames, (frames, 16))
    lane = lax.broadcasted_iota(jnp.int32, (frames, 16), 1)
    members = ((lane == batch * clip_count + ids) & (ids < clip_count)).astype(f32).astype(bf16)
    normed, inverse = layer_norm(latents[...].astype(f32))
    scale = 1.0 + dg(choice, mod_rows[:, width : 2 * width], NN)
    first += 32
    for part in range(5):
        tail[first : first + 16, :] = sums[part].astype(bf16)
        first += 16
    time_low = time_embed[...].astype(f32)
    time_low = time_low / (1.0 + jnp.exp(-time_low))
    repeated = jnp.concatenate([time_low] * (16 // clip_count), axis=0)
    row = lax.broadcasted_iota(jnp.int32, (16, width), 0)
    mine = (lax.div(row, clip_count) == batch) & (frame == 0)
    tail[first : first + 16, :] = jnp.where(mine, repeated, 0.0).astype(bf16)
    first += 16
    tail[first:, :] = jnp.zeros((tail.shape[0] - first, width), bf16)

    @pl.when(column > 0)
    def _():
        arrived(column)
        grad_mod[...] += part_in[column].astype(f32)

    @pl.when(column < count - 1)
    def _():
        arrived(count)
        grad_mod[...] += part_in[count].astype(f32)

    back.wait()
    total = grad_mod[...] + peer_in[...].astype(f32)
    grad_latents[...] = (
        grad_attn_out[...] + norm_back(total * scale, normed, inverse)
    ).astype(bf16)
    first = 3 * width
    tail[first : first + 16, :] = clip_sums(members, total).astype(bf16)
    tail[first + 16 : first + 32, :] = clip_sums(members, total * normed).astype(bf16)

    for run in tail_waiting.pop(0):
        run()
    while waiting or tail_waiting:
        for unused in range(-(-len(waiting) // max(1, len(tail_waiting)))):
            waiting.pop(0)[1]()
        if tail_waiting:
            for run in tail_waiting.pop(0):
                run()

    def sent(step, unused):
        toward(step, block_at(step)).wait_send()
        return unused

    lax.fori_loop(max(1, count - slots), count, sent, 0)
    for item in items + tail_items:
        item.finish()


def backward_attention(clip_len, *given, count):
    latents, weights = given[0], given[5]
    frames, width = latents.shape
    slots = min(count, 4)
    tail_rows = round_up(3 * width + 8 * 16, count)
    vmem = pl.BlockSpec(memory_space=pltpu.VMEM)
    anywhere = pl.BlockSpec(memory_space=pl.ANY)
    specs = [vmem] * 5 + [anywhere] + [vmem] * 3 + [anywhere, vmem] + [anywhere] * 2 + [vmem] * 4
    return pl.pallas_call(
        functools.partial(backward_kernel, frames, count, clip_len.shape[1]),
        name="attention_backward",
        out_shape=(
            jax.ShapeDtypeStruct((frames, width), bf16),
            jax.ShapeDtypeStruct((tail_rows, width), bf16),
            jax.ShapeDtypeStruct(weights.shape, bf16),
        ),
        in_specs=[pl.BlockSpec(memory_space=pltpu.SMEM)] + specs,
        out_specs=(vmem,) * 3,
        scratch_shapes=[
            pltpu.VMEM(weights.shape, bf16),
            pltpu.VMEM((tail_rows, width), bf16),
            pltpu.VMEM((frames, width), f32),
            pltpu.VMEM((width, 3 * width), f32),
            pltpu.VMEM((frames, width + LANES), bf16),
            pltpu.VMEM((frames, width + LANES), bf16),
            pltpu.VMEM((HEADS, 2 * frames, LANES), bf16),
            pltpu.VMEM((HEADS, 2 * frames, LANES), bf16),
            pltpu.VMEM((HEADS, LANES, 2 * frames), f32),
            pltpu.VMEM((2, HEADS, frames, LANES), f32),
            pltpu.VMEM((2, HEADS, frames, LANES), f32),
            pltpu.VMEM((frames, 2 * width), bf16),
            pltpu.VMEM((slots, frames, width), bf16),
            pltpu.VMEM((count + 1, frames, width), bf16),
            pltpu.VMEM((frames, width), bf16),
            pltpu.VMEM((frames, width), bf16),
            pltpu.VMEM((2, 2, HEADS, frames, LANES), bf16),
            pltpu.VMEM((2, frames, width), bf16),
            pltpu.SemaphoreType.DMA((4,)),
            pltpu.SemaphoreType.DMA,
            pltpu.SemaphoreType.DMA,
            pltpu.SemaphoreType.DMA((2 + count,)),
            pltpu.SemaphoreType.DMA((3 + count,)),
        ]
        + summing_scratch(middle_kinds(count), weights.shape[0], MIDDLE_CHUNKS, count)
        + summing_scratch(TAIL_KINDS, tail_rows, TAIL_CHUNKS, count),
        compiler_params=pltpu.CompilerParams(
            collective_id=2, has_side_effects=True, vmem_limit_bytes=63 * 2**20
        ),
    )(clip_len, *given)


def spread_kernel(width, shapes, weights, tail, *refs):
    outs, (low, rows) = refs[: len(shapes)], refs[len(shapes) : len(shapes) + 2]
    stages, (load_sem, store_sem) = refs[len(shapes) + 2 : -2], refs[-2:]
    total = weights.shape[0]
    half = total // 2
    loads = [
        pltpu.make_async_copy(tail, rows, load_sem.at[0]),
        pltpu.make_async_copy(weights.at[pl.ds(0, half)], low.at[pl.ds(0, half)], load_sem.at[1]),
        pltpu.make_async_copy(
            weights.at[pl.ds(half, total - half)],
            low.at[pl.ds(half, total - half)],
            load_sem.at[2],
        ),
    ]
    for load in loads:
        load.start()
    stores = [
        pltpu.make_async_copy(stage, out, store_sem.at[index])
        for index, (stage, out) in enumerate(zip(stages, outs))
    ]
    ada, qkv, down, up, co, ckv, cq, ao, bias, gain = range(10)
    loads[0].wait()
    first = 3 * width
    marks = [rows[first + 16 * part : first + 16 * (part + 1), :] for part in range(8)]
    for part in range(6):
        here = slice(part * width, (part + 1) * width)
        stages[ada][:, here] = dg(marks[7], marks[part], TN)
        stages[bias][:, here] = jnp.sum(marks[part].astype(f32), axis=0, keepdims=True)
    stages[gain][...] = jnp.sum(marks[6].astype(f32), axis=0, keepdims=True)
    stores[ada].start()
    stores[bias].start()
    stores[gain].start()
    for part in range(3):
        stages[qkv][:, part * width : (part + 1) * width] = rows[
            part * width : (part + 1) * width, :
        ].astype(f32)
    stores[qkv].start()
    loads[1].wait()
    loads[2].wait()
    first = 0
    for part in range(shapes[down][0] // width):
        here = slice(part * width, (part + 1) * width)
        stages[down][here, :] = low[first : first + width, :].astype(f32)
        first += width
        stages[up][:, here] = low[first : first + width, :].astype(f32)
        first += width
    stores[down].start()
    stores[up].start()
    for index in (co, ckv, cq, ao):
        length = shapes[index][0]
        for part in range(shapes[index][1] // width):
            here = slice(part * width, (part + 1) * width)
            stages[index][:, here] = low[first : first + length, :].astype(f32)
            first += length
        stores[index].start()
    for store in stores:
        store.wait()


def spread_weights(weights, tail, text_width, hidden_width):
    width = weights.shape[1]
    square = (width, width)
    shapes = [
        (width, 6 * width),
        (width, 3 * width),
        (hidden_width, width),
        (width, hidden_width),
        square,
        (text_width, 2 * width),
        square,
        square,
        (1, 6 * width),
        (1, width),
    ]
    anywhere = pl.BlockSpec(memory_space=pl.ANY)
    return pl.pallas_call(
        functools.partial(spread_kernel, width, shapes),
        name="weight_gradients",
        out_shape=[jax.ShapeDtypeStruct(shape, f32) for shape in shapes],
        in_specs=[anywhere] * 2,
        out_specs=[anywhere] * len(shapes),
        scratch_shapes=[pltpu.VMEM(weights.shape, bf16), pltpu.VMEM(tail.shape, bf16)]
        + [pltpu.VMEM(shape, f32) for shape in shapes]
        + [pltpu.SemaphoreType.DMA((3,)), pltpu.SemaphoreType.DMA((len(shapes),))],
        compiler_params=pltpu.CompilerParams(vmem_limit_bytes=48 * 2**20),
    )(weights, tail)


def spread_matrices(width):
    head_size = width // HEADS
    lane = np.arange(HEADS * LANES, dtype=np.int32)[None, :]
    head, inner = lane // LANES, lane % LANES
    row = np.arange(LANES, dtype=np.int32)[:, None]
    spread_q = (row < 3 * HEADS) & (head == row // 3) & (inner == head_size + 4 + row % 3)
    row = np.arange(width, dtype=np.int32)[:, None]
    spread_o = [(head == row // head_size) & (inner == row % head_size)]
    row = np.arange(LANES, dtype=np.int32)[:, None] - 3 * HEADS
    spread_o.append((row >= 0) & (head == row // 3) & (inner == head_size + row % 3))
    column = np.arange(LANES, dtype=np.int32)[None, :] - 3 * HEADS
    sum_heads = np.arange(width, dtype=np.int32)[:, None] // head_size == column // 3
    return (
        spread_q.astype(bf16),
        np.concatenate(spread_o, axis=0).astype(bf16),
        sum_heads.astype(bf16),
    )


def per_device(
    latents,
    time_embed,
    text_states,
    text_len,
    clip_len,
    cotangent,
    w_ada,
    b_ada,
    w_qkv,
    w_ao,
    gain_cross,
    w_cq,
    w_ckv,
    w_co,
    w_up,
    w_down,
):
    frames = latents.shape[1]
    width = latents.shape[2]
    clip_count = time_embed.shape[1]
    text_slots = text_states.shape[2]
    count = lax.axis_size("frame") // 2
    attention, stats, mod_rows, mod_all, mod_peer, pairs, queries = forward_attention(
        clip_len, latents[0], time_embed[0], w_ada, b_ada[None], w_qkv, count
    )
    text_rows = text_states[0].reshape(clip_count * text_slots, text_states.shape[3])
    mixed, grad_attention, grad_attn_out, sums, weights = middle_part(
        clip_len,
        text_len,
        latents[0],
        cotangent[0],
        attention,
        mod_rows,
        text_rows,
        gain_cross[None],
        w_ao,
        w_cq,
        w_ckv,
        w_co,
        w_up,
        w_down,
        count=count,
    )

    grad_latents, tail, weights = backward_attention(
        clip_len,
        latents[0],
        time_embed[0],
        mod_rows,
        grad_attn_out,
        sums,
        weights,
        grad_attention,
        attention,
        stats,
        mod_all,
        mod_peer,
        pairs,
        queries,
        w_qkv,
        *spread_matrices(width),
        count=count,
    )
    ada, qkv, down, up, co, ckv, cq, ao, bias, gain = spread_weights(
        weights, tail, text_rows.shape[1], w_up.shape[1]
    )
    grads = (ada, bias[0], qkv, ao, gain[0], cq, ckv, co, up, down)
    return (mixed[None], grad_latents[None]) + grads


def solution(mesh):
    placed = (
        P("batch", "frame", None),
        P("batch", None, None),
        P("batch", None, None, None),
        P("batch", None),
        P("batch", None),
        P("batch", "frame", None),
    ) + (P(),) * 10
    return jax.shard_map(
        per_device,
        mesh=mesh,
        in_specs=placed,
        out_specs=(P("batch", "frame", None), P("batch", "frame", None)) + (P(),) * 10,
        check_vma=False,
    )
```

```python
import functools
import math

import jax
import jax.numpy as jnp
import numpy as np
from jax import lax
from jax.experimental import pallas as pl
from jax.experimental.pallas import tpu as pltpu
from jax.sharding import PartitionSpec as P

HEADS = 6
LANES = 128
MASKED = -1e30

f32 = jnp.float32
bf16 = jnp.bfloat16
eps_norm = 1e-06
MESH = pl.DeviceIdType.MESH

NT = (((1,), (1,)), ((), ()))
NN = (((1,), (0,)), ((), ()))
TN = (((0,), (0,)), ((), ()))


def dg(left, right, dims):
    return lax.dot_general(left, right, dims, preferred_element_type=f32)


def layer_norm(values):
    center = values - jnp.mean(values, axis=-1, keepdims=True)
    inverse = lax.rsqrt(jnp.mean(center * center, axis=-1, keepdims=True) + eps_norm)
    return (center * inverse, inverse)


def norm_back(grad, normed, inverse):
    mean_grad = jnp.mean(grad, axis=-1, keepdims=True)
    mean_prod = jnp.mean(grad * normed, axis=-1, keepdims=True)
    return (grad - mean_grad - normed * mean_prod) * inverse


def pieces(value):
    high = value.astype(bf16)
    rest = value - high.astype(f32)
    middle = rest.astype(bf16)
    low = (rest - middle.astype(f32)).astype(bf16)
    return high, middle, low


def nearest(step, me, count):
    lower = me < count // 2
    mine = jnp.where(lower, me, count - 1 - me)
    index = jnp.where(step - 1 < mine, step - 1, step)
    return jnp.where(lower, index, count - 1 - index)


def place():
    batch = lax.axis_index("batch")
    frame = lax.axis_index("frame")
    side = lax.rem(frame, 2)
    column = lax.div(frame, 2)
    return batch, frame, side, column, frame + 1 - 2 * side


def greet(batch, side, column, count, peer):
    barrier = pltpu.get_barrier_semaphore()
    pl.semaphore_signal(barrier, inc=1, device_id=(batch, peer), device_id_type=MESH)
    for step in range(1, count):
        other = nearest(step, column, count)
        pl.semaphore_signal(
            barrier, inc=1, device_id=(batch, 2 * other + side), device_id_type=MESH
        )


def met(signals):
    pl.semaphore_wait(pltpu.get_barrier_semaphore(), signals)


def clip_ids(clip_len, clip_count, first, shape):
    position = first + lax.broadcasted_iota(jnp.int32, shape, 0)
    ids = jnp.zeros(shape, jnp.int32)
    end = 0
    for clip in range(clip_count):
        end = end + clip_len[0, clip]
        ids += (position >= end).astype(jnp.int32)
    return ids


def row_choice(ids, clip_count):
    lane = lax.broadcasted_iota(jnp.int32, ids.shape, 1)
    return ((lax.rem(lane, clip_count) == ids) & (lane < 3 * clip_count)).astype(bf16)


def head_tile(flat, head, tail):
    size = LANES - tail.shape[1]
    return jnp.concatenate([flat[:, head * size : (head + 1) * size], tail], axis=1)


def forward_kernel(
    frames,
    count,
    clip_count,
    clip_len,
    latents,
    time_embed,
    w_ada,
    b_ada,
    w_qkv,
    attention,
    stats,
    mod_rows,
    mod_all,
    mod_peer,
    pairs_out,
    queries,
    pairs,
    total,
    tops,
    part_out,
    part_in,
    stat_out,
    stat_in,
    pairs_sem,
    send_sem,
    recv_sem,
):
    batch, frame, side, column, peer = place()
    width = latents.shape[1]
    head_size = width // HEADS
    greet(batch, side, column, count, peer)

    def to_peer(source, target, slot):
        return pltpu.make_async_remote_copy(
            src_ref=source,
            dst_ref=target,
            send_sem=send_sem.at[slot],
            recv_sem=recv_sem.at[slot],
            device_id=(batch, peer),
            device_id_type=MESH,
        )

    def to_column(step, other, slot):
        return pltpu.make_async_remote_copy(
            src_ref=mod_all.at[slot],
            dst_ref=mod_all.at[slot],
            send_sem=send_sem.at[4 + step],
            recv_sem=recv_sem.at[4 + slot],
            device_id=(batch, 2 * other + side),
            device_id_type=MESH,
        )

    time_low = time_embed[...].astype(f32)
    time_low = (time_low / (1.0 + jnp.exp(-time_low))).astype(bf16)
    modulation = dg(time_low, w_ada[...], NN) + b_ada[...][None, :]
    parts = [piece.astype(f32) for piece in pieces(modulation)]
    parts.append(jnp.zeros((16 - 3 * clip_count, modulation.shape[1]), f32))
    mod_rows[...] = jnp.concatenate(parts, axis=0).astype(bf16)
    choice = row_choice(clip_ids(clip_len, clip_count, frame * frames, (frames, 16)), clip_count)
    normed, inverse = layer_norm(latents[...].astype(f32))
    shift, scale = (
        dg(choice, mod_rows[:, part * width : (part + 1) * width], NN) for part in range(2)
    )
    mod_all[column] = (normed * (1.0 + scale) + shift).astype(bf16)
    met(count)
    swap = to_peer(mod_all.at[column], mod_peer, 0)
    relayed = count == 4

    def hop(block, up):
        other = column + 1 if up else column - 1
        return pltpu.make_async_remote_copy(
            src_ref=mod_all.at[block],
            dst_ref=mod_all.at[block],
            send_sem=send_sem.at[4 + block + (0 if up else count)],
            recv_sem=recv_sem.at[4 + block],
            device_id=(batch, 2 * other + side),
            device_id_type=MESH,
        )

    def each_hop(distance, act):
        for up in (True, False):
            block = column - distance if up else column + distance
            here = block >= 0 if up else block < count
            further = column < count - 1 if up else column > 0
            act(block, up, here, further)

    def begin(block, up, here, further):
        @pl.when(here & further)
        def _():
            hop(block, up).start()

    def take(block, up, here, further):
        @pl.when(here)
        def _():
            hop(block, up).wait_recv()

        begin(block, up, here, further)

    def end(block, up, here, further):
        @pl.when(here & further)
        def _():
            hop(block, up).wait_send()

    if relayed:
        each_hop(0, begin)
        swap.start()
    else:
        sends = [
            to_column(step, nearest(step, column, count), column) for step in range(1, count)
        ]
        for index, send in enumerate(sends):
            send.start()
            if index == 0:
                swap.start()
    total[...] = jnp.zeros_like(total)
    tops[...] = jnp.full_like(tops, -1e38)
    tail = (frames, LANES - head_size)
    lane = lax.broadcasted_iota(jnp.int32, tail, 1)
    ones = jnp.ones(tail, bf16)

    def make_queries(half, owner, source):
        rows = pl.ds(half * frames, frames)
        flat = dg(source, w_qkv[:, :width], NN).astype(bf16) * 0.125
        ids = clip_ids(clip_len, clip_count, owner * frames, tail)
        extra = (ids == lane).astype(f32).astype(bf16)
        for head in range(HEADS):
            queries[head, rows, :] = head_tile(flat, head, extra)

    def make_keys(block):
        source = mod_all[block]
        ids = clip_ids(clip_len, clip_count, (2 * block + side) * frames, tail)
        masks = jnp.where((ids == lane) | (lane > clip_count), 0.0, MASKED)
        extra = jnp.where(
            lane < clip_count, masks, jnp.where(lane < clip_count + 3, 1.0, 0.0)
        ).astype(bf16)
        flat = dg(source, w_qkv[:, width : 2 * width], NN).astype(bf16)
        for head in range(HEADS):
            pairs[block, 0, head] = head_tile(flat, head, extra)
        flat = dg(source, w_qkv[:, 2 * width :], NN).astype(bf16)
        for head in range(HEADS):
            pairs[block, 1, head] = head_tile(flat, head, ones)
        keep(block).start()

    def keep(block):
        return pltpu.make_async_copy(
            pairs.at[block], pairs_out.at[block], pairs_sem.at[block]
        )

    def attend(half, block, heads=range(HEADS)):
        rows = pl.ds(half * frames, frames)

        def scores(head):
            now = dg(pairs[block, 0, head], queries[head, rows, :], NT)
            return now, jnp.max(now, axis=0, keepdims=True)

        ahead = scores(heads[0])
        for head in heads:
            now, top = ahead
            if head != heads[-1]:
                ahead = scores(head + 1)
            before = tops[head, :1, rows]
            new = jnp.maximum(before, top)
            probs = jnp.exp(now - new).astype(bf16)
            total[head, :, rows] = total[head, :, rows] * jnp.exp(before - new) + dg(
                pairs[block, 1, head], probs, TN
            )
            tops[head, :, rows] = jnp.broadcast_to(new, (8, frames))

    def arrive(step):
        block = nearest(step, column, count)
        if not relayed:
            to_column(step, block, block).wait_recv()
        make_keys(block)
        return block

    make_queries(0, frame, mod_all[column])
    make_keys(column)
    attend(0, column)
    swap.wait()
    make_queries(1, peer, mod_peer[...])
    attend(1, column)

    if relayed:
        outer = (column == 0) | (column == count - 1)
        each_hop(1, take)
        block = arrive(1)
        attend(0, block)
        attend(1, block)

        @pl.when(outer)
        def _():
            each_hop(2, take)

        block = arrive(2)
        attend(0, block)

        @pl.when(jnp.logical_not(outer))
        def _():
            each_hop(2, take)

        attend(1, block)
        each_hop(3, take)
    else:

        def per_block(step, unused):
            block = arrive(step)
            attend(0, block)
            attend(1, block)
            return unused

        lax.fori_loop(1, count - 1, per_block, 0)
    block = arrive(count - 1)
    there = pl.ds(frames, frames)
    heads_half = HEADS // 2
    parts = []
    for side_part in range(2):
        heads = range(side_part * heads_half, (side_part + 1) * heads_half)
        attend(1, block, heads)
        for head in heads:
            part_out[head * head_size : (head + 1) * head_size, :] = total[
                head, :head_size, there
            ].astype(bf16)
            stat_out[head : head + 1, :] = tops[head, :1, there]
            stat_out[8 + head : 9 + head, :] = total[head, head_size : head_size + 1, there]
        chosen = pl.ds(side_part * heads_half * head_size, heads_half * head_size)
        parts.append(to_peer(part_out.at[chosen], part_in.at[chosen], 1 + side_part))
        parts[-1].start()
    parts.append(to_peer(stat_out, stat_in, 3))
    parts[-1].start()
    attend(0, block)
    for part in parts:
        part.wait()
    here = pl.ds(0, frames)
    joined = []
    logs = []
    for head in range(HEADS):
        mine, theirs = tops[head, :1, here], stat_in[head : head + 1, :]
        new = jnp.maximum(mine, theirs)
        left, right = jnp.exp(mine - new), jnp.exp(theirs - new)
        row_sum = (
            total[head, head_size : head_size + 1, here] * left
            + stat_in[8 + head : 9 + head, :] * right
        )
        logs.append(new + jnp.log(row_sum))
        scale = 1.0 / row_sum
        joined.append(
            total[head, :head_size, here] * (left * scale)
            + part_in[head * head_size : (head + 1) * head_size, :].astype(f32) * (right * scale)
        )
    attention[...] = jnp.concatenate(joined, axis=0).T.astype(bf16)
    rows = [piece for log in logs for piece in log_pieces(log)]
    rows.append(jnp.zeros((LANES - len(rows), frames), f32))
    stats[...] = jnp.concatenate(rows, axis=0).T.astype(bf16)
    for kept in range(count):
        keep(kept).wait()
    if relayed:
        for distance in range(count - 1):
            each_hop(distance, end)
    else:
        for send in sends:
            send.wait_send()


def log_pieces(log):
    high, middle, low = pieces(-log)
    return [high.astype(f32), middle.astype(f32), low.astype(f32)]


def forward_attention(clip_len, latents, time_embed, w_ada, b_ada, w_qkv, count):
    frames, width = latents.shape
    clip_count = clip_len.shape[1]
    vmem = pl.BlockSpec(memory_space=pltpu.VMEM)
    shapes = (
        jax.ShapeDtypeStruct((frames, width), bf16),
        jax.ShapeDtypeStruct((frames, LANES), bf16),
        jax.ShapeDtypeStruct((16, w_ada.shape[1]), bf16),
        jax.ShapeDtypeStruct((count, frames, width), bf16),
        jax.ShapeDtypeStruct((frames, width), bf16),
        jax.ShapeDtypeStruct((count, 2, HEADS, frames, LANES), bf16),
        jax.ShapeDtypeStruct((HEADS, 2 * frames, LANES), bf16),
    )
    return pl.pallas_call(
        functools.partial(forward_kernel, frames, count, clip_count),
        name="attention_forward",
        out_shape=shapes,
        in_specs=[pl.BlockSpec(memory_space=pltpu.SMEM)] + [vmem] * 5,
        out_specs=(vmem,) * 5 + (pl.BlockSpec(memory_space=pl.ANY), vmem),
        scratch_shapes=[
            pltpu.VMEM((count, 2, HEADS, frames, LANES), bf16),
            pltpu.VMEM((HEADS, LANES, 2 * frames), f32),
            pltpu.VMEM((HEADS, 8, 2 * frames), f32),
            pltpu.VMEM((width, frames), bf16),
            pltpu.VMEM((width, frames), bf16),
            pltpu.VMEM((16, frames), f32),
            pltpu.VMEM((16, frames), f32),
            pltpu.SemaphoreType.DMA((count,)),
            pltpu.SemaphoreType.DMA((4 + 2 * count,)),
            pltpu.SemaphoreType.DMA((4 + count,)),
        ],
        compiler_params=pltpu.CompilerParams(
            collective_id=1, has_side_effects=True, vmem_limit_bytes=62 * 2**20
        ),
    )(clip_len, latents, time_embed, w_ada, b_ada, w_qkv)


def clip_sums(choice, value):
    high = value.astype(bf16)
    low = (value - high.astype(f32)).astype(bf16)
    return dg(choice, high, TN) + dg(choice, low, TN)


def middle_kernel(
    frames,
    clip_count,
    clip_len,
    text_len,
    latents,
    cotangent,
    attention,
    mod_rows,
    text_rows,
    gain_cross,
    w_ao,
    w_cq,
    w_ckv,
    w_co,
    w_up_given,
    w_down_given,
    mixed,
    grad_att,
    grad_attn_out,
    sums,
    weights_out,
    weights,
    w_up,
    w_down,
    moves,
    key_tiles,
    query_tiles,
    grad_tiles,
    probs_kept,
    flat_kv,
):
    loads = [
        pltpu.make_async_copy(w_up_given, w_up, moves.at[0]),
        pltpu.make_async_copy(w_down_given, w_down, moves.at[1]),
    ]
    for load in loads:
        load.start()
    batch, frame, side, column, peer = place()
    width = latents.shape[1]
    head_size = width // HEADS
    slots = text_rows.shape[0]
    per_clip = slots // clip_count
    tail = (frames, LANES - head_size)

    wide_ids = clip_ids(clip_len, clip_count, frame * frames, (frames, 16))
    choice = row_choice(wide_ids, clip_count)
    group_lane = lax.broadcasted_iota(jnp.int32, (frames, 16), 1)
    members = ((group_lane == batch * clip_count + wide_ids) & (wide_ids < clip_count)).astype(f32)
    members = members.astype(bf16)
    ids = clip_ids(clip_len, clip_count, frame * frames, (frames, width))
    valid = (ids < clip_count).astype(f32)

    def mod_part(part):
        return dg(choice, mod_rows[:, part * width : (part + 1) * width], NN)

    gate_attn = mod_part(2) * valid
    branch_attn = dg(attention[...], w_ao[...], NN)
    after_attn = latents[...].astype(f32) + gate_attn * branch_attn
    normed_cross, inverse_cross = layer_norm(after_attn)
    gain = gain_cross[...]
    cross_in = (normed_cross * gain).astype(bf16)

    flat = dg(cross_in, w_cq[...], NN).astype(bf16) * 0.125
    lane = lax.broadcasted_iota(jnp.int32, tail, 1)
    extra = (clip_ids(clip_len, clip_count, frame * frames, tail) == lane).astype(f32).astype(bf16)
    for head in range(HEADS):
        query_tiles[head] = head_tile(flat, head, extra)
    slot = lax.broadcasted_iota(jnp.int32, (slots, LANES - head_size), 0)
    lane = lax.broadcasted_iota(jnp.int32, (slots, LANES - head_size), 1)
    live = jnp.zeros(lane.shape, jnp.bool_)
    for clip in range(clip_count):
        inside = (slot >= clip * per_clip) & (slot < clip * per_clip + text_len[0, clip])
        live = live | (inside & (lane == clip))
    extra = jnp.where(live | (lane >= clip_count), 0.0, MASKED).astype(bf16)
    flat = dg(text_rows[...], w_ckv[:, :width], NN).astype(bf16)
    for head in range(HEADS):
        key_tiles[0, head] = head_tile(flat, head, extra)
    extra = (lane < 3).astype(f32).astype(bf16)
    flat = dg(text_rows[...], w_ckv[:, width:], NN).astype(bf16)
    for head in range(HEADS):
        key_tiles[1, head] = head_tile(flat, head, extra)

    def scores(head):
        now = dg(key_tiles[0, head], query_tiles[head], NT)
        return now, jnp.max(now, axis=0, keepdims=True)

    joined = []
    ahead = scores(0)
    for head in range(HEADS):
        now, top = ahead
        if head + 1 < HEADS:
            ahead = scores(head + 1)
        probs = jnp.exp(now - top)
        probs = (probs * (1.0 / jnp.sum(probs, axis=0, keepdims=True))).astype(bf16)
        probs_kept[head] = probs
        joined.append(dg(key_tiles[1, head], probs, TN)[:head_size])
    cross_exact = jnp.concatenate(joined, axis=0).T
    cross = cross_exact.astype(bf16)
    after_cross = after_attn + dg(cross, w_co[...], NN) * valid
    normed_mlp, inverse_mlp = layer_norm(after_cross)
    scale_mlp = 1.0 + mod_part(4)
    mlp_in = (normed_mlp * scale_mlp + mod_part(3)).astype(bf16)
    gate_mlp = mod_part(5) * valid
    grad_out = cotangent[...].astype(f32)
    grad_mlp = (grad_out * gate_mlp).astype(bf16)
    root = math.sqrt(2.0 / math.pi)
    branch_mlp = jnp.zeros((frames, width), f32)
    grad_mlp_in = jnp.zeros((frames, width), f32)
    hidden_width = w_up.shape[1]
    first = 0
    for load in loads:
        load.wait()
    for part in range(hidden_width // width):
        here = slice(part * width, (part + 1) * width)
        hidden = dg(mlp_in, w_up[:, here], NN)
        square = hidden * hidden
        bend = jnp.tanh(root * hidden * (1.0 + 0.044715 * square))
        half = 0.5 * (1.0 + bend)
        activated = (hidden * half).astype(bf16)
        slope = half + (0.5 * root) * hidden * (1.0 - bend * bend) * (1.0 + 0.134145 * square)
        grad_hidden = (dg(grad_mlp, w_down[here, :], NT) * slope).astype(bf16)
        branch_mlp += dg(activated, w_down[here, :], NN)
        grad_mlp_in += dg(grad_hidden, w_up[:, here], NT)
        weights[first : first + width, :] = dg(activated, grad_mlp, TN).astype(bf16)
        first += width
        weights[first : first + width, :] = dg(mlp_in, grad_hidden, TN).astype(bf16)
        first += width
    stores = [
        pltpu.make_async_copy(
            weights.at[pl.ds(0, first)], weights_out.at[pl.ds(0, first)], moves.at[2]
        )
    ]
    stores[0].start()
    begun = first
    mixed[...] = (after_cross + gate_mlp * branch_mlp).astype(bf16)
    sums[3] = clip_sums(members, grad_out * branch_mlp)
    sums[1] = clip_sums(members, grad_mlp_in)
    sums[2] = clip_sums(members, grad_mlp_in * normed_mlp)
    grad_cross_out = grad_out + norm_back(grad_mlp_in * scale_mlp, normed_mlp, inverse_mlp)
    grad_branch = (grad_cross_out * valid).astype(bf16)
    weights[first : first + width, :] = dg(cross, grad_branch, TN).astype(bf16)
    first += width

    flat = dg(grad_branch, w_co[...], NT).astype(bf16)
    product = flat.astype(f32) * cross_exact
    lane = lax.broadcasted_iota(jnp.int32, tail, 1)
    for head in range(HEADS):
        part = product[:, head * head_size : (head + 1) * head_size]
        high, middle, low = pieces(-jnp.sum(part, axis=1, keepdims=True))
        extra = jnp.where(
            lane == 0,
            high.astype(f32),
            jnp.where(lane == 1, middle.astype(f32), jnp.where(lane == 2, low.astype(f32), 0.0)),
        ).astype(bf16)
        grad_tiles[head] = head_tile(flat, head, extra)
    joined = []
    for pair in range(HEADS // 2):
        kept = []
        for head in (2 * pair, 2 * pair + 1):
            probs = probs_kept[head]
            dscore = dg(key_tiles[1, head], grad_tiles[head], NT) * probs.astype(f32)
            dscore = dscore.astype(bf16)
            joined.append(dg(key_tiles[0, head], dscore, TN)[:head_size])
            kept.append(
                (
                    dg(dscore, query_tiles[head], NN)[:, :head_size],
                    dg(probs, grad_tiles[head], NN)[:, :head_size],
                )
            )
        for kind in range(2):
            start = kind * width + pair * LANES
            flat_kv[:, start : start + LANES] = jnp.concatenate(
                [kept[0][kind], kept[1][kind]], axis=1
            ).astype(bf16)
    for kind in range(2):
        grad = dg(text_rows[...], flat_kv[:, kind * width : (kind + 1) * width], TN)
        weights[first : first + grad.shape[0], :] = grad.astype(bf16)
        first += grad.shape[0]
    grad_queries = (jnp.concatenate(joined, axis=0) * 0.125).T.astype(bf16)
    weights[first : first + width, :] = dg(cross_in, grad_queries, TN).astype(bf16)
    first += width
    grad_cross_in = dg(grad_queries, w_cq[...], NT)
    grad_gain = jnp.sum(grad_cross_in * normed_cross, axis=0, keepdims=True)
    top_row = lax.broadcasted_iota(jnp.int32, (16, width), 0) == 0
    sums[4] = jnp.where(top_row, grad_gain, 0.0)
    grad_attn = grad_cross_out + norm_back(grad_cross_in * gain, normed_cross, inverse_cross)
    grad_attn_out[...] = grad_attn
    sums[0] = clip_sums(members, grad_attn * branch_attn)
    grad_branch = (grad_attn * gate_attn).astype(bf16)
    weights[first : first + width, :] = dg(attention[...], grad_branch, TN).astype(bf16)
    first += width
    grad_att[...] = dg(grad_branch, w_ao[...], NT).astype(bf16)
    weights[first:, :] = jnp.zeros((weights.shape[0] - first, width), bf16)
    rest = pl.ds(begun, weights.shape[0] - begun)
    stores.append(pltpu.make_async_copy(weights.at[rest], weights_out.at[rest], moves.at[3]))
    stores[1].start()
    for store in stores:
        store.wait()


def middle_lengths(width, text_width, hidden_width):
    return [width] * (2 * hidden_width // width + 1) + [text_width] * 2 + [width] * 2


def middle_part(clip_len, text_len, latents, *others, count):
    frames, width = latents.shape
    text_rows, w_up = others[3], others[9]
    slots, text_width = text_rows.shape
    rows = round_up(sum(middle_lengths(width, text_width, w_up.shape[1])), count)
    vmem = pl.BlockSpec(memory_space=pltpu.VMEM)
    smem = pl.BlockSpec(memory_space=pltpu.SMEM)
    anywhere = pl.BlockSpec(memory_space=pl.ANY)
    return pl.pallas_call(
        functools.partial(middle_kernel, frames, clip_len.shape[1]),
        name="middle",
        out_shape=(
            jax.ShapeDtypeStruct((frames, width), bf16),
            jax.ShapeDtypeStruct((frames, width), bf16),
            jax.ShapeDtypeStruct((frames, width), f32),
            jax.ShapeDtypeStruct((5, 16, width), f32),
            jax.ShapeDtypeStruct((rows, width), bf16),
        ),
        in_specs=[smem] * 2 + [vmem] * 10 + [anywhere] * 2,
        out_specs=(vmem,) * 4 + (anywhere,),
        scratch_shapes=[
            pltpu.VMEM((rows, width), bf16),
            pltpu.VMEM(w_up.shape, bf16),
            pltpu.VMEM(w_up.shape[::-1], bf16),
            pltpu.SemaphoreType.DMA((4,)),
            pltpu.VMEM((2, HEADS, slots, LANES), bf16),
            pltpu.VMEM((HEADS, frames, LANES), bf16),
            pltpu.VMEM((HEADS, frames, LANES), bf16),
            pltpu.VMEM((HEADS, slots, frames), bf16),
            pltpu.VMEM((slots, 2 * width), bf16),
        ],
        compiler_params=pltpu.CompilerParams(vmem_limit_bytes=62 * 2**20),
    )(clip_len, text_len, latents, *others)


def tile_of(rows):
    return max(tile for tile in range(16, 129, 16) if rows % tile == 0)


def level_size(kind, count):
    return {"square": 4, "z": count}.get(kind, 2)


def level_place(kind):
    batch, frame, side, column, peer = place()
    core, across = lax.rem(batch, 2), lax.div(batch, 2)
    if kind == "core":
        return core, lambda member: (2 * across + member, frame)
    if kind == "x":
        return across, lambda member: (core + 2 * member, frame)
    if kind == "y":
        return side, lambda member: (batch, 2 * column + member)
    if kind == "square":
        return 2 * across + side, lambda member: (
            core + 2 * lax.div(member, 2),
            2 * column + lax.rem(member, 2),
        )
    if kind == "z":
        return column, lambda member: (batch, 2 * member + side)
    bit = int(kind)
    mine = lax.rem(lax.div(column, bit), 2)
    return mine, lambda member: (batch, 2 * (column + bit * (member - mine)) + side)


class Summing:
    def __init__(self, kinds, data, result, landings, send_sem, recv_sem, chunk, first, rows, count):
        self.kinds, self.data, self.result = kinds, data, result
        self.landings, self.send_sem, self.recv_sem, self.chunk = landings, send_sem, recv_sem, chunk
        self.sizes = [level_size(kind, count) for kind in kinds]
        self.places, self.devices = zip(*(level_place(kind) for kind in kinds))
        self.starts, self.lengths = [first], [rows]
        for size, mine in zip(self.sizes, self.places):
            self.lengths.append(self.lengths[-1] // size)
            self.starts.append(self.starts[-1] + mine * self.lengths[-1])
        self.sent = []

    def others(self, level):
        size = self.sizes[level]
        return [lax.rem(self.places[level] + step, size) for step in range(1, size)]

    def rows(self, start, length):
        return pl.ds(pl.multiple_of(start, 16), length)

    def copy(self, way, level, source, target, member, slot):
        base = way * sum(self.sizes) + sum(self.sizes[:level])
        return pltpu.make_async_remote_copy(
            src_ref=source,
            dst_ref=target,
            send_sem=self.send_sem.at[self.chunk, base + member],
            recv_sem=self.recv_sem.at[self.chunk, base + slot],
            device_id=self.devices[level](member),
            device_id_type=MESH,
        )

    def scatter(self, level):
        length = self.lengths[level + 1]
        for member in self.others(level):
            rows = self.rows(self.starts[level] + member * length, length)
            mine = self.places[level]
            copy = self.copy(
                0, level, self.data.at[rows], self.landings[level].at[mine], member, mine
            )
            copy.start()
            self.sent.append(copy)

    def add(self, level):
        length, start = self.lengths[level + 1], self.starts[level + 1]
        others = self.others(level)
        landing = self.landings[level]
        for member in others:
            rows = self.rows(start, length)
            self.copy(0, level, self.data.at[rows], landing.at[member], member, member).wait_recv()
        tile = tile_of(length)
        target = self.result if level == len(self.sizes) - 1 else self.data

        def body(index, unused):
            inner = self.rows(index * tile, tile)
            outer = self.rows(start + index * tile, tile)
            value = self.data[outer, :].astype(f32)
            for member in others:
                value += landing[member, inner, :].astype(f32)
            target[outer, :] = value.astype(bf16)
            return unused

        lax.fori_loop(0, length // tile, body, 0)

    def gather(self, level):
        rows = self.rows(self.starts[level + 1], self.lengths[level + 1])
        mine = self.places[level]
        for member in self.others(level):
            copy = self.copy(1, level, self.result.at[rows], self.result.at[rows], member, mine)
            copy.start()
            self.sent.append(copy)

    def gathered(self, level):
        length = self.lengths[level + 1]
        for member in self.others(level):
            rows = self.rows(self.starts[level] + member * length, length)
            self.copy(
                1, level, self.result.at[rows], self.result.at[rows], member, member
            ).wait_recv()

    def steps(self):
        def step(*calls):
            def run():
                for call, level in calls:
                    call(level)

            return run

        last = len(self.sizes) - 1
        runs = [step((self.scatter, 0))]
        for level in range(last):
            runs.append(step((self.add, level), (self.scatter, level + 1)))
        runs.append(step((self.add, last), (self.gather, last)))
        for level in range(last, 0, -1):
            runs.append(step((self.gathered, level), (self.gather, level - 1)))
        runs.append(step((self.gathered, 0)))
        return runs

    def finish(self):
        for copy in self.sent:
            copy.wait_send()


def middle_kinds(count):
    bits, bit = [], 1
    while bit < count:
        bits.append(str(bit))
        bit *= 2
    return (("core","x","y","z"),("core","y","x","z"),("core","z","x","y"),("core","x","y","z"),("core","y","x","z"),("core","z","y","x"))


def chunk_rows(rows, chunks, count):
    unit = 128 * count
    units = rows // unit
    chunks = min(chunks, units)
    return [(units // chunks + (index < units % chunks)) * unit for index in range(chunks)]


def round_up(rows, count):
    unit = 128 * count
    return -(-rows // unit) * unit


def summing_scratch(kinds, rows, chunks, count):
    shapes = []
    for chunk, length in enumerate(chunk_rows(rows, chunks, count)):
        for kind in kinds[chunk % len(kinds)]:
            length //= level_size(kind, count)
            shapes.append(pltpu.VMEM((level_size(kind, count), length, 384), bf16))
    slots = 2 * sum(level_size(kind, count) for kind in kinds[0])
    return shapes + [pltpu.SemaphoreType.DMA((chunks, slots))] * 2


def make_summing(kinds, data, result, scratch, chunks, count):
    send_sem, recv_sem = scratch[-2:]
    levels = len(kinds[0])
    sums, first = [], 0
    for chunk, length in enumerate(chunk_rows(data.shape[0], chunks, count)):
        landings = scratch[levels * chunk : levels * (chunk + 1)]
        order = kinds[chunk % len(kinds)]
        sums.append(
            Summing(order, data, result, landings, send_sem, recv_sem, chunk, first, length, count)
        )
        first += length
    return sums


def greet_all(count):
    batch, frame, side, column, peer = place()
    core, across = lax.rem(batch, 2), lax.div(batch, 2)
    barrier = pltpu.get_barrier_semaphore()
    targets = [
        (batch + 1 - 2 * core, frame),
        (batch, peer),
        (core + 2 - 2 * across, frame),
        (core + 2 - 2 * across, peer),
    ]
    for step in range(1, count):
        targets.append((batch, 2 * lax.rem(column + step, count) + side))
    for target in targets:
        pl.semaphore_signal(barrier, inc=1, device_id=target, device_id_type=MESH)
    return len(targets)


TAIL_KINDS = (("core", "square", "z"), ("core", "z", "square"))
TAIL_CHUNKS = 3
MIDDLE_CHUNKS = 6
MIDDLE_TIMES = (0, 4, 16, 24, 30, 36, 44, 51, 56)
CHUNK_TIME = 0.6


def timed_steps(items):
    runs = [item.steps() for item in items]
    timed = []
    for step in range(len(runs[0])):
        for index, run in enumerate(runs):
            now = MIDDLE_TIMES[min(step, len(MIDDLE_TIMES) - 1)] + CHUNK_TIME * index
            timed.append((now, run[step]))
    return sorted(timed, key=lambda pair: pair[0])


def backward_kernel(
    frames,
    count,
    clip_count,
    clip_len,
    latents,
    time_embed,
    mod_rows,
    grad_attn_out,
    sums,
    weights,
    grad_att,
    attention,
    stats,
    mod_all,
    mod_peer,
    pairs,
    queries_in,
    w_qkv,
    spread_q,
    spread_o,
    sum_heads,
    grad_latents,
    tail_result,
    result,
    data,
    tail,
    grad_mod,
    grad_w,
    pack_out,
    pack_in,
    queries,
    grads,
    query_grad,
    key_grad,
    value_grad,
    flat_kv,
    part_out,
    part_in,
    peer_out,
    peer_in,
    held,
    held_mod,
    held_sem,
    load_sem,
    query_sem,
    send_sem,
    recv_sem,
    *scratch,
):
    batch, frame, side, column, peer = place()
    width = grad_att.shape[1]
    slots = part_out.shape[0]
    load = pltpu.make_async_copy(weights, data, load_sem)
    load.start()
    load_queries = pltpu.make_async_copy(queries_in, queries, query_sem)
    load_queries.start()
    head_size = width // HEADS

    def block_at(step):
        return jnp.where(step == count, column, nearest(count - step, column, count))

    def fetches(step):
        slot = lax.rem(step - 1, 2)
        block = block_at(step)
        return (
            pltpu.make_async_copy(pairs.at[block], held.at[slot], held_sem.at[slot]),
            pltpu.make_async_copy(mod_all.at[block], held_mod.at[slot], held_sem.at[2 + slot]),
        )

    def fetch(step):
        for copy in fetches(step):
            copy.start()

    def fetched(step):
        for copy in fetches(step):
            copy.wait()

    signals = greet_all(count)
    fetch(1)
    fetch(2)
    kinds = middle_kinds(count)
    levels = len(kinds[0])
    chunks = len(chunk_rows(data.shape[0], MIDDLE_CHUNKS, count))
    own = scratch[: levels * chunks + 2]
    items = make_summing(kinds, data, result, own, MIDDLE_CHUNKS, count)
    waiting = timed_steps(items)
    tail_items = make_summing(TAIL_KINDS, tail, tail_result, scratch[len(own) :], TAIL_CHUNKS, count)
    tail_waiting = [list(group) for group in zip(*(item.steps() for item in tail_items))]
    heads_done = [0]

    def advance():
        while waiting and waiting[0][0] <= heads_done[0]:
            waiting.pop(0)[1]()

    def to_peer(source, target, slot):
        return pltpu.make_async_remote_copy(
            src_ref=source,
            dst_ref=target,
            send_sem=send_sem.at[slot],
            recv_sem=recv_sem.at[slot],
            device_id=(batch, peer),
            device_id_type=MESH,
        )

    def toward(step, owner):
        up = owner > column
        other = jnp.where(up, column + 1, column - 1)
        slot = jnp.where((other == owner) & jnp.logical_not(up), count, owner)
        return pltpu.make_async_remote_copy(
            src_ref=part_out.at[lax.rem(step, slots)],
            dst_ref=part_in.at[slot],
            send_sem=send_sem.at[2 + step],
            recv_sem=recv_sem.at[2 + slot],
            device_id=(batch, 2 * other + side),
            device_id_type=MESH,
        )

    def arrived(slot):
        pltpu.make_async_remote_copy(
            src_ref=part_out.at[0],
            dst_ref=part_in.at[slot],
            send_sem=send_sem.at[2],
            recv_sem=recv_sem.at[2 + slot],
            device_id=(batch, peer),
            device_id_type=MESH,
        ).wait_recv()

    def pass_on(step):
        block = block_at(step)
        arrived(block)
        slot = lax.rem(step, slots)
        part_out[slot] = (part_out[slot].astype(f32) + part_in[block].astype(f32)).astype(bf16)
        toward(step, block).start()

    def chain_kind(step):
        block = block_at(step)
        up = block > column
        begins = jnp.where(up, column == 0, column == count - 1)
        late = jnp.where(column < count // 2, up, jnp.logical_not(up))
        return begins, late

    def pass_late(step):
        begins, late = chain_kind(step)

        @pl.when(jnp.logical_not(begins) & late)
        def _():
            pass_on(step)

    grad_now = grad_att[...]
    product = grad_now.astype(f32) * attention[...].astype(f32)
    high, middle, low = pieces(product)
    delta = (
        dg(high, sum_heads[...], NN) + dg(middle, sum_heads[...], NN) + dg(low, sum_heads[...], NN)
    )
    high, middle, low = (piece.astype(f32) for piece in pieces(-delta))
    which = lax.rem(lax.broadcasted_iota(jnp.int32, delta.shape, 1), 3)
    extra = jnp.where(which == 0, high, jnp.where(which == 1, middle, low))
    pack_out[:, :width] = grad_now
    pack_out[:, width:] = stats[...] + extra.astype(bf16)
    swap = to_peer(pack_out, pack_in, 0)
    load.wait()
    met(signals)
    swap.start()
    advance()
    query_grad[...] = jnp.zeros_like(query_grad)

    def prepare(half, source):
        rows = pl.ds(half * frames, frames)
        wide = dg(source, spread_o[...], NN)
        extra = dg(source[:, width:], spread_q[...], NN).astype(bf16)
        wide = wide.astype(bf16)
        for head in range(HEADS):
            lanes = slice(head * LANES, (head + 1) * LANES)
            grads[head, rows, :] = wide[:, lanes]
            queries[head, rows, :] += extra[:, lanes]

    def differentiate(half, slot, first, moving=True):
        rows = pl.ds(half * frames, frames)
        for head in range(HEADS):
            key, value = held[slot, 0, head], held[slot, 1, head]
            query, grad = queries[head, rows, :], grads[head, rows, :]
            probs = jnp.exp(dg(key, query, NT))
            dscore = (probs * dg(value, grad, NT)).astype(bf16)
            probs = probs.astype(bf16)
            more_k, more_v = dg(dscore, query, NN), dg(probs, grad, NN)
            if first:
                key_grad[slot, head] = more_k
                value_grad[slot, head] = more_v
            else:
                key_grad[slot, head] += more_k
                value_grad[slot, head] += more_v
            query_grad[head, :, rows] += dg(key, dscore, TN)
            if moving:
                heads_done[0] += 1
                advance()

    def finish_keys(slot):
        for kind, source in enumerate((key_grad, value_grad)):
            for pair in range(HEADS // 2):
                start = kind * width + pair * LANES
                flat_kv[:, start : start + LANES] = jnp.concatenate(
                    [
                        source[slot, 2 * pair][:, :head_size],
                        source[slot, 2 * pair + 1][:, :head_size],
                    ],
                    axis=1,
                ).astype(bf16)
        flat = flat_kv[...]
        return dg(flat, w_qkv[:, width:], NT), dg(held_mod[slot], flat, TN)

    def finish_queries(half, source):
        rows = pl.ds(half * frames, frames)
        flat = jnp.concatenate(
            [query_grad[head, :head_size, rows] for head in range(HEADS)], axis=0
        )
        flat = (flat * 0.125).T.astype(bf16)
        return dg(flat, w_qkv[:, :width], NT), dg(source, flat, TN)

    def send_block(step, slot, first):
        block = block_at(step)
        part, weight = finish_keys(slot)
        if not isinstance(step, int):

            @pl.when(step > slots)
            def _():
                toward(step - slots, block_at(step - slots)).wait_send()

        part_out[lax.rem(step, slots)] = part.astype(bf16)
        if first is False:
            pass_late(step - 1)
        begins, late = chain_kind(step)

        @pl.when(begins)
        def _():
            toward(step, block).start()

        @pl.when(jnp.logical_not(begins) & jnp.logical_not(late))
        def _():
            pass_on(step)

        if first:
            grad_w[:, width:] = weight
        else:
            grad_w[:, width:] += weight

        @pl.when(step + 2 <= count)
        def _():
            fetch(step + 2)

    load_queries.wait()
    prepare(0, pack_out[...])
    fetched(1)
    differentiate(0, 0, True)
    fetched(2)
    differentiate(0, 1, True)
    swap.wait()
    prepare(1, pack_in[...])
    differentiate(1, 0, False)
    send_block(1, 0, True)
    differentiate(1, 1, False)
    send_block(2, 1, False)

    def per_block(step, moving):
        slot = (step - 1) % 2 if isinstance(step, int) else lax.rem(step - 1, 2)
        fetched(step)
        differentiate(0, slot, True, moving)
        differentiate(1, slot, False, moving)
        send_block(step, slot, False)

    if count <= 4:
        for step in range(3, count):
            per_block(step, True)
    else:

        def looped(step, unused):
            per_block(step, False)
            return unused

        lax.fori_loop(3, count, looped, 0)
    slot = (count - 1) % 2
    fetched(count)
    differentiate(1, slot, True)
    pass_late(count - 1)
    part, weight = finish_queries(1, mod_peer[...])
    peer_out[...] = part.astype(bf16)
    back = to_peer(peer_out, peer_in, 1)
    back.start()
    grad_w[:, :width] = weight
    differentiate(0, slot, False)
    part, weight = finish_keys(slot)
    grad_w[:, width:] += weight
    mine, weight = finish_queries(0, held_mod[slot])
    grad_w[:, :width] += weight
    first = 0
    for part_index in range(3):
        tail[first : first + width, :] = grad_w[
            :, part_index * width : (part_index + 1) * width
        ].astype(bf16)
        first += width
    tail_waiting[0].pop(0)()
    grad_mod[...] = part + mine

    choice = row_choice(clip_ids(clip_len, clip_count, frame * frames, (frames, 16)), clip_count)
    ids = clip_ids(clip_len, clip_count, frame * frames, (frames, 16))
    lane = lax.broadcasted_iota(jnp.int32, (frames, 16), 1)
    members = ((lane == batch * clip_count + ids) & (ids < clip_count)).astype(f32).astype(bf16)
    normed, inverse = layer_norm(latents[...].astype(f32))
    scale = 1.0 + dg(choice, mod_rows[:, width : 2 * width], NN)
    first += 32
    for part in range(5):
        tail[first : first + 16, :] = sums[part].astype(bf16)
        first += 16
    time_low = time_embed[...].astype(f32)
    time_low = time_low / (1.0 + jnp.exp(-time_low))
    repeated = jnp.concatenate([time_low] * (16 // clip_count), axis=0)
    row = lax.broadcasted_iota(jnp.int32, (16, width), 0)
    mine = (lax.div(row, clip_count) == batch) & (frame == 0)
    tail[first : first + 16, :] = jnp.where(mine, repeated, 0.0).astype(bf16)
    first += 16
    tail[first:, :] = jnp.zeros((tail.shape[0] - first, width), bf16)

    @pl.when(column > 0)
    def _():
        arrived(column)
        grad_mod[...] += part_in[column].astype(f32)

    @pl.when(column < count - 1)
    def _():
        arrived(count)
        grad_mod[...] += part_in[count].astype(f32)

    back.wait()
    total = grad_mod[...] + peer_in[...].astype(f32)
    grad_latents[...] = (
        grad_attn_out[...] + norm_back(total * scale, normed, inverse)
    ).astype(bf16)
    first = 3 * width
    tail[first : first + 16, :] = clip_sums(members, total).astype(bf16)
    tail[first + 16 : first + 32, :] = clip_sums(members, total * normed).astype(bf16)

    for run in tail_waiting.pop(0):
        run()
    while waiting or tail_waiting:
        for unused in range(-(-len(waiting) // max(1, len(tail_waiting)))):
            waiting.pop(0)[1]()
        if tail_waiting:
            for run in tail_waiting.pop(0):
                run()

    def sent(step, unused):
        toward(step, block_at(step)).wait_send()
        return unused

    lax.fori_loop(max(1, count - slots), count, sent, 0)
    for item in items + tail_items:
        item.finish()


def backward_attention(clip_len, *given, count):
    latents, weights = given[0], given[5]
    frames, width = latents.shape
    slots = min(count, 4)
    tail_rows = round_up(3 * width + 8 * 16, count)
    vmem = pl.BlockSpec(memory_space=pltpu.VMEM)
    anywhere = pl.BlockSpec(memory_space=pl.ANY)
    specs = [vmem] * 5 + [anywhere] + [vmem] * 3 + [anywhere, vmem] + [anywhere] * 2 + [vmem] * 4
    return pl.pallas_call(
        functools.partial(backward_kernel, frames, count, clip_len.shape[1]),
        name="attention_backward",
        out_shape=(
            jax.ShapeDtypeStruct((frames, width), bf16),
            jax.ShapeDtypeStruct((tail_rows, width), bf16),
            jax.ShapeDtypeStruct(weights.shape, bf16),
        ),
        in_specs=[pl.BlockSpec(memory_space=pltpu.SMEM)] + specs,
        out_specs=(vmem,) * 3,
        scratch_shapes=[
            pltpu.VMEM(weights.shape, bf16),
            pltpu.VMEM((tail_rows, width), bf16),
            pltpu.VMEM((frames, width), f32),
            pltpu.VMEM((width, 3 * width), f32),
            pltpu.VMEM((frames, width + LANES), bf16),
            pltpu.VMEM((frames, width + LANES), bf16),
            pltpu.VMEM((HEADS, 2 * frames, LANES), bf16),
            pltpu.VMEM((HEADS, 2 * frames, LANES), bf16),
            pltpu.VMEM((HEADS, LANES, 2 * frames), f32),
            pltpu.VMEM((2, HEADS, frames, LANES), f32),
            pltpu.VMEM((2, HEADS, frames, LANES), f32),
            pltpu.VMEM((frames, 2 * width), bf16),
            pltpu.VMEM((slots, frames, width), bf16),
            pltpu.VMEM((count + 1, frames, width), bf16),
            pltpu.VMEM((frames, width), bf16),
            pltpu.VMEM((frames, width), bf16),
            pltpu.VMEM((2, 2, HEADS, frames, LANES), bf16),
            pltpu.VMEM((2, frames, width), bf16),
            pltpu.SemaphoreType.DMA((4,)),
            pltpu.SemaphoreType.DMA,
            pltpu.SemaphoreType.DMA,
            pltpu.SemaphoreType.DMA((2 + count,)),
            pltpu.SemaphoreType.DMA((3 + count,)),
        ]
        + summing_scratch(middle_kinds(count), weights.shape[0], MIDDLE_CHUNKS, count)
        + summing_scratch(TAIL_KINDS, tail_rows, TAIL_CHUNKS, count),
        compiler_params=pltpu.CompilerParams(
            collective_id=2, has_side_effects=True, vmem_limit_bytes=63 * 2**20
        ),
    )(clip_len, *given)


def spread_kernel(width, shapes, weights, tail, *refs):
    outs, (low, rows) = refs[: len(shapes)], refs[len(shapes) : len(shapes) + 2]
    stages, (load_sem, store_sem) = refs[len(shapes) + 2 : -2], refs[-2:]
    total = weights.shape[0]
    half = total // 2
    loads = [
        pltpu.make_async_copy(tail, rows, load_sem.at[0]),
        pltpu.make_async_copy(weights.at[pl.ds(0, half)], low.at[pl.ds(0, half)], load_sem.at[1]),
        pltpu.make_async_copy(
            weights.at[pl.ds(half, total - half)],
            low.at[pl.ds(half, total - half)],
            load_sem.at[2],
        ),
    ]
    for load in loads:
        load.start()
    stores = [
        pltpu.make_async_copy(stage, out, store_sem.at[index])
        for index, (stage, out) in enumerate(zip(stages, outs))
    ]
    ada, qkv, down, up, co, ckv, cq, ao, bias, gain = range(10)
    loads[0].wait()
    first = 3 * width
    marks = [rows[first + 16 * part : first + 16 * (part + 1), :] for part in range(8)]
    for part in range(6):
        here = slice(part * width, (part + 1) * width)
        stages[ada][:, here] = dg(marks[7], marks[part], TN)
        stages[bias][:, here] = jnp.sum(marks[part].astype(f32), axis=0, keepdims=True)
    stages[gain][...] = jnp.sum(marks[6].astype(f32), axis=0, keepdims=True)
    stores[ada].start()
    stores[bias].start()
    stores[gain].start()
    for part in range(3):
        stages[qkv][:, part * width : (part + 1) * width] = rows[
            part * width : (part + 1) * width, :
        ].astype(f32)
    stores[qkv].start()
    loads[1].wait()
    loads[2].wait()
    first = 0
    for part in range(shapes[down][0] // width):
        here = slice(part * width, (part + 1) * width)
        stages[down][here, :] = low[first : first + width, :].astype(f32)
        first += width
        stages[up][:, here] = low[first : first + width, :].astype(f32)
        first += width
    stores[down].start()
    stores[up].start()
    for index in (co, ckv, cq, ao):
        length = shapes[index][0]
        for part in range(shapes[index][1] // width):
            here = slice(part * width, (part + 1) * width)
            stages[index][:, here] = low[first : first + length, :].astype(f32)
            first += length
        stores[index].start()
    for store in stores:
        store.wait()


def spread_weights(weights, tail, text_width, hidden_width):
    width = weights.shape[1]
    square = (width, width)
    shapes = [
        (width, 6 * width),
        (width, 3 * width),
        (hidden_width, width),
        (width, hidden_width),
        square,
        (text_width, 2 * width),
        square,
        square,
        (1, 6 * width),
        (1, width),
    ]
    anywhere = pl.BlockSpec(memory_space=pl.ANY)
    return pl.pallas_call(
        functools.partial(spread_kernel, width, shapes),
        name="weight_gradients",
        out_shape=[jax.ShapeDtypeStruct(shape, f32) for shape in shapes],
        in_specs=[anywhere] * 2,
        out_specs=[anywhere] * len(shapes),
        scratch_shapes=[pltpu.VMEM(weights.shape, bf16), pltpu.VMEM(tail.shape, bf16)]
        + [pltpu.VMEM(shape, f32) for shape in shapes]
        + [pltpu.SemaphoreType.DMA((3,)), pltpu.SemaphoreType.DMA((len(shapes),))],
        compiler_params=pltpu.CompilerParams(vmem_limit_bytes=48 * 2**20),
    )(weights, tail)


def spread_matrices(width):
    head_size = width // HEADS
    lane = np.arange(HEADS * LANES, dtype=np.int32)[None, :]
    head, inner = lane // LANES, lane % LANES
    row = np.arange(LANES, dtype=np.int32)[:, None]
    spread_q = (row < 3 * HEADS) & (head == row // 3) & (inner == head_size + 4 + row % 3)
    row = np.arange(width, dtype=np.int32)[:, None]
    spread_o = [(head == row // head_size) & (inner == row % head_size)]
    row = np.arange(LANES, dtype=np.int32)[:, None] - 3 * HEADS
    spread_o.append((row >= 0) & (head == row // 3) & (inner == head_size + row % 3))
    column = np.arange(LANES, dtype=np.int32)[None, :] - 3 * HEADS
    sum_heads = np.arange(width, dtype=np.int32)[:, None] // head_size == column // 3
    return (
        spread_q.astype(bf16),
        np.concatenate(spread_o, axis=0).astype(bf16),
        sum_heads.astype(bf16),
    )


def per_device(
    latents,
    time_embed,
    text_states,
    text_len,
    clip_len,
    cotangent,
    w_ada,
    b_ada,
    w_qkv,
    w_ao,
    gain_cross,
    w_cq,
    w_ckv,
    w_co,
    w_up,
    w_down,
):
    frames = latents.shape[1]
    width = latents.shape[2]
    clip_count = time_embed.shape[1]
    text_slots = text_states.shape[2]
    count = lax.axis_size("frame") // 2
    attention, stats, mod_rows, mod_all, mod_peer, pairs, queries = forward_attention(
        clip_len, latents[0], time_embed[0], w_ada, b_ada, w_qkv, count
    )
    text_rows = text_states[0].reshape(clip_count * text_slots, text_states.shape[3])
    mixed, grad_attention, grad_attn_out, sums, weights = middle_part(
        clip_len,
        text_len,
        latents[0],
        cotangent[0],
        attention,
        mod_rows,
        text_rows,
        gain_cross[None],
        w_ao,
        w_cq,
        w_ckv,
        w_co,
        w_up,
        w_down,
        count=count,
    )

    grad_latents, tail, weights = backward_attention(
        clip_len,
        latents[0],
        time_embed[0],
        mod_rows,
        grad_attn_out,
        sums,
        weights,
        grad_attention,
        attention,
        stats,
        mod_all,
        mod_peer,
        pairs,
        queries,
        w_qkv,
        *spread_matrices(width),
        count=count,
    )
    ada, qkv, down, up, co, ckv, cq, ao, bias, gain = spread_weights(
        weights, tail, text_rows.shape[1], w_up.shape[1]
    )
    grads = (ada, bias[0], qkv, ao, gain[0], cq, ckv, co, up, down)
    return (mixed[None], grad_latents[None]) + grads


def solution(mesh):
    placed = (
        P("batch", "frame", None),
        P("batch", None, None),
        P("batch", None, None, None),
        P("batch", None),
        P("batch", None),
        P("batch", "frame", None),
    ) + (P(),) * 10
    return jax.shard_map(
        per_device,
        mesh=mesh,
        in_specs=placed,
        out_specs=(P("batch", "frame", None), P("batch", "frame", None)) + (P(),) * 10,
        check_vma=False,
    )
```

```python
import functools
import math

import jax
import jax.numpy as jnp
import numpy as np
from jax import lax
from jax.experimental import pallas as pl
from jax.experimental.pallas import tpu as pltpu
from jax.sharding import PartitionSpec as P

HEADS = 6
LANES = 128
MASKED = -1e30

f32 = jnp.float32
bf16 = jnp.bfloat16
eps_norm = 1e-06
MESH = pl.DeviceIdType.MESH

NT = (((1,), (1,)), ((), ()))
NN = (((1,), (0,)), ((), ()))
TN = (((0,), (0,)), ((), ()))


def dg(left, right, dims):
    return lax.dot_general(left, right, dims, preferred_element_type=f32)


def layer_norm(values):
    center = values - jnp.mean(values, axis=-1, keepdims=True)
    inverse = lax.rsqrt(jnp.mean(center * center, axis=-1, keepdims=True) + eps_norm)
    return (center * inverse, inverse)


def norm_back(grad, normed, inverse):
    mean_grad = jnp.mean(grad, axis=-1, keepdims=True)
    mean_prod = jnp.mean(grad * normed, axis=-1, keepdims=True)
    return (grad - mean_grad - normed * mean_prod) * inverse


def pieces(value):
    high = value.astype(bf16)
    rest = value - high.astype(f32)
    middle = rest.astype(bf16)
    low = (rest - middle.astype(f32)).astype(bf16)
    return high, middle, low


def nearest(step, me, count):
    lower = me < count // 2
    mine = jnp.where(lower, me, count - 1 - me)
    index = jnp.where(step - 1 < mine, step - 1, step)
    return jnp.where(lower, index, count - 1 - index)


def place():
    batch = lax.axis_index("batch")
    frame = lax.axis_index("frame")
    side = lax.rem(frame, 2)
    column = lax.div(frame, 2)
    return batch, frame, side, column, frame + 1 - 2 * side


def greet(batch, side, column, count, peer):
    barrier = pltpu.get_barrier_semaphore()
    pl.semaphore_signal(barrier, inc=1, device_id=(batch, peer), device_id_type=MESH)
    for step in range(1, count):
        other = nearest(step, column, count)
        pl.semaphore_signal(
            barrier, inc=1, device_id=(batch, 2 * other + side), device_id_type=MESH
        )


def met(signals):
    pl.semaphore_wait(pltpu.get_barrier_semaphore(), signals)


def clip_ids(clip_len, clip_count, first, shape):
    position = first + lax.broadcasted_iota(jnp.int32, shape, 0)
    ids = jnp.zeros(shape, jnp.int32)
    end = 0
    for clip in range(clip_count):
        end = end + clip_len[0, clip]
        ids += (position >= end).astype(jnp.int32)
    return ids


def row_choice(ids, clip_count):
    lane = lax.broadcasted_iota(jnp.int32, ids.shape, 1)
    return ((lax.rem(lane, clip_count) == ids) & (lane < 3 * clip_count)).astype(bf16)


def head_tile(flat, head, tail):
    size = LANES - tail.shape[1]
    return jnp.concatenate([flat[:, head * size : (head + 1) * size], tail], axis=1)


def forward_kernel(
    frames,
    count,
    clip_count,
    clip_len,
    latents,
    time_embed,
    w_ada,
    b_ada,
    w_qkv,
    attention,
    stats,
    mod_rows,
    mod_all,
    mod_peer,
    pairs_out,
    queries,
    pairs,
    total,
    tops,
    part_out,
    part_in,
    stat_out,
    stat_in,
    pairs_sem,
    send_sem,
    recv_sem,
):
    batch, frame, side, column, peer = place()
    width = latents.shape[1]
    head_size = width // HEADS
    greet(batch, side, column, count, peer)

    def to_peer(source, target, slot):
        return pltpu.make_async_remote_copy(
            src_ref=source,
            dst_ref=target,
            send_sem=send_sem.at[slot],
            recv_sem=recv_sem.at[slot],
            device_id=(batch, peer),
            device_id_type=MESH,
        )

    def to_column(step, other, slot):
        return pltpu.make_async_remote_copy(
            src_ref=mod_all.at[slot],
            dst_ref=mod_all.at[slot],
            send_sem=send_sem.at[4 + step],
            recv_sem=recv_sem.at[4 + slot],
            device_id=(batch, 2 * other + side),
            device_id_type=MESH,
        )

    time_low = time_embed[...].astype(f32)
    time_low = (time_low / (1.0 + jnp.exp(-time_low))).astype(bf16)
    modulation = dg(time_low, w_ada[...], NN) + b_ada[...][None, :]
    parts = [piece.astype(f32) for piece in pieces(modulation)]
    parts.append(jnp.zeros((16 - 3 * clip_count, modulation.shape[1]), f32))
    mod_rows[...] = jnp.concatenate(parts, axis=0).astype(bf16)
    choice = row_choice(clip_ids(clip_len, clip_count, frame * frames, (frames, 16)), clip_count)
    normed, inverse = layer_norm(latents[...].astype(f32))
    shift, scale = (
        dg(choice, mod_rows[:, part * width : (part + 1) * width], NN) for part in range(2)
    )
    mod_all[column] = (normed * (1.0 + scale) + shift).astype(bf16)
    met(count)
    swap = to_peer(mod_all.at[column], mod_peer, 0)
    relayed = count == 4

    def hop(block, up):
        other = column + 1 if up else column - 1
        return pltpu.make_async_remote_copy(
            src_ref=mod_all.at[block],
            dst_ref=mod_all.at[block],
            send_sem=send_sem.at[4 + block + (0 if up else count)],
            recv_sem=recv_sem.at[4 + block],
            device_id=(batch, 2 * other + side),
            device_id_type=MESH,
        )

    def each_hop(distance, act):
        for up in (True, False):
            block = column - distance if up else column + distance
            here = block >= 0 if up else block < count
            further = column < count - 1 if up else column > 0
            act(block, up, here, further)

    def begin(block, up, here, further):
        @pl.when(here & further)
        def _():
            hop(block, up).start()

    def take(block, up, here, further):
        @pl.when(here)
        def _():
            hop(block, up).wait_recv()

        begin(block, up, here, further)

    def end(block, up, here, further):
        @pl.when(here & further)
        def _():
            hop(block, up).wait_send()

    if relayed:
        each_hop(0, begin)
        swap.start()
    else:
        sends = [
            to_column(step, nearest(step, column, count), column) for step in range(1, count)
        ]
        for index, send in enumerate(sends):
            send.start()
            if index == 0:
                swap.start()
    total[...] = jnp.zeros_like(total)
    tops[...] = jnp.full_like(tops, -1e38)
    tail = (frames, LANES - head_size)
    lane = lax.broadcasted_iota(jnp.int32, tail, 1)
    ones = jnp.ones(tail, bf16)

    def make_queries(half, owner, source):
        rows = pl.ds(half * frames, frames)
        flat = dg(source, w_qkv[:, :width], NN).astype(bf16) * 0.125
        ids = clip_ids(clip_len, clip_count, owner * frames, tail)
        extra = (ids == lane).astype(f32).astype(bf16)
        for head in range(HEADS):
            queries[head, rows, :] = head_tile(flat, head, extra)

    def make_keys(block):
        source = mod_all[block]
        ids = clip_ids(clip_len, clip_count, (2 * block + side) * frames, tail)
        masks = jnp.where((ids == lane) | (lane > clip_count), 0.0, MASKED)
        extra = jnp.where(
            lane < clip_count, masks, jnp.where(lane < clip_count + 3, 1.0, 0.0)
        ).astype(bf16)
        flat = dg(source, w_qkv[:, width : 2 * width], NN).astype(bf16)
        for head in range(HEADS):
            pairs[block, 0, head] = head_tile(flat, head, extra)
        flat = dg(source, w_qkv[:, 2 * width :], NN).astype(bf16)
        for head in range(HEADS):
            pairs[block, 1, head] = head_tile(flat, head, ones)
        keep(block).start()

    def keep(block):
        return pltpu.make_async_copy(
            pairs.at[block], pairs_out.at[block], pairs_sem.at[block]
        )

    def attend(half, block, heads=range(HEADS)):
        rows = pl.ds(half * frames, frames)

        def scores(head):
            now = dg(pairs[block, 0, head], queries[head, rows, :], NT)
            return now, jnp.max(now, axis=0, keepdims=True)

        ahead = scores(heads[0])
        for head in heads:
            now, top = ahead
            if head != heads[-1]:
                ahead = scores(head + 1)
            before = tops[head, :1, rows]
            new = jnp.maximum(before, top)
            probs = jnp.exp(now - new).astype(bf16)
            total[head, :, rows] = total[head, :, rows] * jnp.exp(before - new) + dg(
                pairs[block, 1, head], probs, TN
            )
            tops[head, :, rows] = jnp.broadcast_to(new, (8, frames))

    def arrive(step):
        block = nearest(step, column, count)
        if not relayed:
            to_column(step, block, block).wait_recv()
        make_keys(block)
        return block

    make_queries(0, frame, mod_all[column])
    make_keys(column)
    attend(0, column)
    swap.wait()
    make_queries(1, peer, mod_peer[...])
    attend(1, column)

    if relayed:
        outer = (column == 0) | (column == count - 1)
        each_hop(1, take)
        block = arrive(1)
        attend(0, block)
        attend(1, block)

        @pl.when(outer)
        def _():
            each_hop(2, take)

        block = arrive(2)
        attend(0, block)

        @pl.when(jnp.logical_not(outer))
        def _():
            each_hop(2, take)

        attend(1, block)
        each_hop(3, take)
    else:

        def per_block(step, unused):
            block = arrive(step)
            attend(0, block)
            attend(1, block)
            return unused

        lax.fori_loop(1, count - 1, per_block, 0)
    block = arrive(count - 1)
    there = pl.ds(frames, frames)
    heads_half = HEADS // 2
    parts = []
    for side_part in range(2):
        heads = range(side_part * heads_half, (side_part + 1) * heads_half)
        attend(1, block, heads)
        for head in heads:
            part_out[head * head_size : (head + 1) * head_size, :] = total[
                head, :head_size, there
            ].astype(bf16)
            stat_out[head : head + 1, :] = tops[head, :1, there]
            stat_out[8 + head : 9 + head, :] = total[head, head_size : head_size + 1, there]
        chosen = pl.ds(side_part * heads_half * head_size, heads_half * head_size)
        parts.append(to_peer(part_out.at[chosen], part_in.at[chosen], 1 + side_part))
        parts[-1].start()
    parts.append(to_peer(stat_out, stat_in, 3))
    parts[-1].start()
    attend(0, block)
    for part in parts:
        part.wait()
    here = pl.ds(0, frames)
    joined = []
    logs = []
    for head in range(HEADS):
        mine, theirs = tops[head, :1, here], stat_in[head : head + 1, :]
        new = jnp.maximum(mine, theirs)
        left, right = jnp.exp(mine - new), jnp.exp(theirs - new)
        row_sum = (
            total[head, head_size : head_size + 1, here] * left
            + stat_in[8 + head : 9 + head, :] * right
        )
        logs.append(new + jnp.log(row_sum))
        scale = 1.0 / row_sum
        joined.append(
            total[head, :head_size, here] * (left * scale)
            + part_in[head * head_size : (head + 1) * head_size, :].astype(f32) * (right * scale)
        )
    attention[...] = jnp.concatenate(joined, axis=0).T.astype(bf16)
    rows = [piece for log in logs for piece in log_pieces(log)]
    rows.append(jnp.zeros((LANES - len(rows), frames), f32))
    stats[...] = jnp.concatenate(rows, axis=0).T.astype(bf16)
    for kept in range(count):
        keep(kept).wait()
    if relayed:
        for distance in range(count - 1):
            each_hop(distance, end)
    else:
        for send in sends:
            send.wait_send()


def log_pieces(log):
    high, middle, low = pieces(-log)
    return [high.astype(f32), middle.astype(f32), low.astype(f32)]


def forward_attention(clip_len, latents, time_embed, w_ada, b_ada, w_qkv, count):
    frames, width = latents.shape
    clip_count = clip_len.shape[1]
    vmem = pl.BlockSpec(memory_space=pltpu.VMEM)
    shapes = (
        jax.ShapeDtypeStruct((frames, width), bf16),
        jax.ShapeDtypeStruct((frames, LANES), bf16),
        jax.ShapeDtypeStruct((16, w_ada.shape[1]), bf16),
        jax.ShapeDtypeStruct((count, frames, width), bf16),
        jax.ShapeDtypeStruct((frames, width), bf16),
        jax.ShapeDtypeStruct((count, 2, HEADS, frames, LANES), bf16),
        jax.ShapeDtypeStruct((HEADS, 2 * frames, LANES), bf16),
    )
    return pl.pallas_call(
        functools.partial(forward_kernel, frames, count, clip_count),
        name="attention_forward",
        out_shape=shapes,
        in_specs=[pl.BlockSpec(memory_space=pltpu.SMEM)] + [vmem] * 5,
        out_specs=(vmem,) * 5 + (pl.BlockSpec(memory_space=pl.ANY), vmem),
        scratch_shapes=[
            pltpu.VMEM((count, 2, HEADS, frames, LANES), bf16),
            pltpu.VMEM((HEADS, LANES, 2 * frames), f32),
            pltpu.VMEM((HEADS, 8, 2 * frames), f32),
            pltpu.VMEM((width, frames), bf16),
            pltpu.VMEM((width, frames), bf16),
            pltpu.VMEM((16, frames), f32),
            pltpu.VMEM((16, frames), f32),
            pltpu.SemaphoreType.DMA((count,)),
            pltpu.SemaphoreType.DMA((4 + 2 * count,)),
            pltpu.SemaphoreType.DMA((4 + count,)),
        ],
        compiler_params=pltpu.CompilerParams(
            collective_id=1, has_side_effects=True, vmem_limit_bytes=62 * 2**20
        ),
    )(clip_len, latents, time_embed, w_ada, b_ada, w_qkv)


def clip_sums(choice, value):
    high = value.astype(bf16)
    low = (value - high.astype(f32)).astype(bf16)
    return dg(choice, high, TN) + dg(choice, low, TN)


def middle_kernel(
    frames,
    clip_count,
    clip_len,
    text_len,
    latents,
    cotangent,
    attention,
    mod_rows,
    text_rows,
    gain_cross,
    w_ao,
    w_cq,
    w_ckv,
    w_co,
    w_up_given,
    w_down_given,
    mixed,
    grad_att,
    grad_attn_out,
    sums,
    weights_out,
    weights,
    w_up,
    w_down,
    moves,
    key_tiles,
    query_tiles,
    grad_tiles,
    probs_kept,
    flat_kv,
):
    loads = [
        pltpu.make_async_copy(w_up_given, w_up, moves.at[0]),
        pltpu.make_async_copy(w_down_given, w_down, moves.at[1]),
    ]
    for load in loads:
        load.start()
    batch, frame, side, column, peer = place()
    width = latents.shape[1]
    head_size = width // HEADS
    slots = text_rows.shape[0]
    per_clip = slots // clip_count
    tail = (frames, LANES - head_size)

    wide_ids = clip_ids(clip_len, clip_count, frame * frames, (frames, 16))
    choice = row_choice(wide_ids, clip_count)
    group_lane = lax.broadcasted_iota(jnp.int32, (frames, 16), 1)
    members = ((group_lane == batch * clip_count + wide_ids) & (wide_ids < clip_count)).astype(f32)
    members = members.astype(bf16)
    ids = clip_ids(clip_len, clip_count, frame * frames, (frames, width))
    valid = (ids < clip_count).astype(f32)

    def mod_part(part):
        return dg(choice, mod_rows[:, part * width : (part + 1) * width], NN)

    gate_attn = mod_part(2) * valid
    branch_attn = dg(attention[...], w_ao[...], NN)
    after_attn = latents[...].astype(f32) + gate_attn * branch_attn
    normed_cross, inverse_cross = layer_norm(after_attn)
    gain = gain_cross[...][None, :]
    cross_in = (normed_cross * gain).astype(bf16)

    flat = dg(cross_in, w_cq[...], NN).astype(bf16) * 0.125
    lane = lax.broadcasted_iota(jnp.int32, tail, 1)
    extra = (clip_ids(clip_len, clip_count, frame * frames, tail) == lane).astype(f32).astype(bf16)
    for head in range(HEADS):
        query_tiles[head] = head_tile(flat, head, extra)
    slot = lax.broadcasted_iota(jnp.int32, (slots, LANES - head_size), 0)
    lane = lax.broadcasted_iota(jnp.int32, (slots, LANES - head_size), 1)
    live = jnp.zeros(lane.shape, jnp.bool_)
    for clip in range(clip_count):
        inside = (slot >= clip * per_clip) & (slot < clip * per_clip + text_len[0, clip])
        live = live | (inside & (lane == clip))
    extra = jnp.where(live | (lane >= clip_count), 0.0, MASKED).astype(bf16)
    flat = dg(text_rows[...], w_ckv[:, :width], NN).astype(bf16)
    for head in range(HEADS):
        key_tiles[0, head] = head_tile(flat, head, extra)
    extra = (lane < 3).astype(f32).astype(bf16)
    flat = dg(text_rows[...], w_ckv[:, width:], NN).astype(bf16)
    for head in range(HEADS):
        key_tiles[1, head] = head_tile(flat, head, extra)

    def scores(head):
        now = dg(key_tiles[0, head], query_tiles[head], NT)
        return now, jnp.max(now, axis=0, keepdims=True)

    joined = []
    ahead = scores(0)
    for head in range(HEADS):
        now, top = ahead
        if head + 1 < HEADS:
            ahead = scores(head + 1)
        probs = jnp.exp(now - top)
        probs = (probs * (1.0 / jnp.sum(probs, axis=0, keepdims=True))).astype(bf16)
        probs_kept[head] = probs
        joined.append(dg(key_tiles[1, head], probs, TN)[:head_size])
    cross_exact = jnp.concatenate(joined, axis=0).T
    cross = cross_exact.astype(bf16)
    after_cross = after_attn + dg(cross, w_co[...], NN) * valid
    normed_mlp, inverse_mlp = layer_norm(after_cross)
    scale_mlp = 1.0 + mod_part(4)
    mlp_in = (normed_mlp * scale_mlp + mod_part(3)).astype(bf16)
    gate_mlp = mod_part(5) * valid
    grad_out = cotangent[...].astype(f32)
    grad_mlp = (grad_out * gate_mlp).astype(bf16)
    root = math.sqrt(2.0 / math.pi)
    branch_mlp = jnp.zeros((frames, width), f32)
    grad_mlp_in = jnp.zeros((frames, width), f32)
    hidden_width = w_up.shape[1]
    first = 0
    for load in loads:
        load.wait()
    for part in range(hidden_width // width):
        here = slice(part * width, (part + 1) * width)
        hidden = dg(mlp_in, w_up[:, here], NN)
        square = hidden * hidden
        bend = jnp.tanh(root * hidden * (1.0 + 0.044715 * square))
        half = 0.5 * (1.0 + bend)
        activated = (hidden * half).astype(bf16)
        slope = half + (0.5 * root) * hidden * (1.0 - bend * bend) * (1.0 + 0.134145 * square)
        grad_hidden = (dg(grad_mlp, w_down[here, :], NT) * slope).astype(bf16)
        branch_mlp += dg(activated, w_down[here, :], NN)
        grad_mlp_in += dg(grad_hidden, w_up[:, here], NT)
        weights[first : first + width, :] = dg(activated, grad_mlp, TN).astype(bf16)
        first += width
        weights[first : first + width, :] = dg(mlp_in, grad_hidden, TN).astype(bf16)
        first += width
    stores = [
        pltpu.make_async_copy(
            weights.at[pl.ds(0, first)], weights_out.at[pl.ds(0, first)], moves.at[2]
        )
    ]
    stores[0].start()
    begun = first
    mixed[...] = (after_cross + gate_mlp * branch_mlp).astype(bf16)
    sums[3] = clip_sums(members, grad_out * branch_mlp)
    sums[1] = clip_sums(members, grad_mlp_in)
    sums[2] = clip_sums(members, grad_mlp_in * normed_mlp)
    grad_cross_out = grad_out + norm_back(grad_mlp_in * scale_mlp, normed_mlp, inverse_mlp)
    grad_branch = (grad_cross_out * valid).astype(bf16)
    weights[first : first + width, :] = dg(cross, grad_branch, TN).astype(bf16)
    first += width

    flat = dg(grad_branch, w_co[...], NT).astype(bf16)
    product = flat.astype(f32) * cross_exact
    lane = lax.broadcasted_iota(jnp.int32, tail, 1)
    for head in range(HEADS):
        part = product[:, head * head_size : (head + 1) * head_size]
        high, middle, low = pieces(-jnp.sum(part, axis=1, keepdims=True))
        extra = jnp.where(
            lane == 0,
            high.astype(f32),
            jnp.where(lane == 1, middle.astype(f32), jnp.where(lane == 2, low.astype(f32), 0.0)),
        ).astype(bf16)
        grad_tiles[head] = head_tile(flat, head, extra)
    joined = []
    for pair in range(HEADS // 2):
        kept = []
        for head in (2 * pair, 2 * pair + 1):
            probs = probs_kept[head]
            dscore = dg(key_tiles[1, head], grad_tiles[head], NT) * probs.astype(f32)
            dscore = dscore.astype(bf16)
            joined.append(dg(key_tiles[0, head], dscore, TN)[:head_size])
            kept.append(
                (
                    dg(dscore, query_tiles[head], NN)[:, :head_size],
                    dg(probs, grad_tiles[head], NN)[:, :head_size],
                )
            )
        for kind in range(2):
            start = kind * width + pair * LANES
            flat_kv[:, start : start + LANES] = jnp.concatenate(
                [kept[0][kind], kept[1][kind]], axis=1
            ).astype(bf16)
    for kind in range(2):
        grad = dg(text_rows[...], flat_kv[:, kind * width : (kind + 1) * width], TN)
        weights[first : first + grad.shape[0], :] = grad.astype(bf16)
        first += grad.shape[0]
    grad_queries = (jnp.concatenate(joined, axis=0) * 0.125).T.astype(bf16)
    weights[first : first + width, :] = dg(cross_in, grad_queries, TN).astype(bf16)
    first += width
    grad_cross_in = dg(grad_queries, w_cq[...], NT)
    grad_gain = jnp.sum(grad_cross_in * normed_cross, axis=0, keepdims=True)
    top_row = lax.broadcasted_iota(jnp.int32, (16, width), 0) == 0
    sums[4] = jnp.where(top_row, grad_gain, 0.0)
    grad_attn = grad_cross_out + norm_back(grad_cross_in * gain, normed_cross, inverse_cross)
    grad_attn_out[...] = grad_attn
    sums[0] = clip_sums(members, grad_attn * branch_attn)
    grad_branch = (grad_attn * gate_attn).astype(bf16)
    weights[first : first + width, :] = dg(attention[...], grad_branch, TN).astype(bf16)
    first += width
    grad_att[...] = dg(grad_branch, w_ao[...], NT).astype(bf16)
    weights[first:, :] = jnp.zeros((weights.shape[0] - first, width), bf16)
    rest = pl.ds(begun, weights.shape[0] - begun)
    stores.append(pltpu.make_async_copy(weights.at[rest], weights_out.at[rest], moves.at[3]))
    stores[1].start()
    for store in stores:
        store.wait()


def middle_lengths(width, text_width, hidden_width):
    return [width] * (2 * hidden_width // width + 1) + [text_width] * 2 + [width] * 2


def middle_part(clip_len, text_len, latents, *others, count):
    frames, width = latents.shape
    text_rows, w_up = others[3], others[9]
    slots, text_width = text_rows.shape
    rows = round_up(sum(middle_lengths(width, text_width, w_up.shape[1])), count)
    vmem = pl.BlockSpec(memory_space=pltpu.VMEM)
    smem = pl.BlockSpec(memory_space=pltpu.SMEM)
    anywhere = pl.BlockSpec(memory_space=pl.ANY)
    return pl.pallas_call(
        functools.partial(middle_kernel, frames, clip_len.shape[1]),
        name="middle",
        out_shape=(
            jax.ShapeDtypeStruct((frames, width), bf16),
            jax.ShapeDtypeStruct((frames, width), bf16),
            jax.ShapeDtypeStruct((frames, width), f32),
            jax.ShapeDtypeStruct((5, 16, width), f32),
            jax.ShapeDtypeStruct((rows, width), bf16),
        ),
        in_specs=[smem] * 2 + [vmem] * 10 + [anywhere] * 2,
        out_specs=(vmem,) * 4 + (anywhere,),
        scratch_shapes=[
            pltpu.VMEM((rows, width), bf16),
            pltpu.VMEM(w_up.shape, bf16),
            pltpu.VMEM(w_up.shape[::-1], bf16),
            pltpu.SemaphoreType.DMA((4,)),
            pltpu.VMEM((2, HEADS, slots, LANES), bf16),
            pltpu.VMEM((HEADS, frames, LANES), bf16),
            pltpu.VMEM((HEADS, frames, LANES), bf16),
            pltpu.VMEM((HEADS, slots, frames), bf16),
            pltpu.VMEM((slots, 2 * width), bf16),
        ],
        compiler_params=pltpu.CompilerParams(vmem_limit_bytes=62 * 2**20),
    )(clip_len, text_len, latents, *others)


def tile_of(rows):
    return max(tile for tile in range(16, 129, 16) if rows % tile == 0)


def level_size(kind, count):
    return {"square": 4, "z": count}.get(kind, 2)


def level_place(kind):
    batch, frame, side, column, peer = place()
    core, across = lax.rem(batch, 2), lax.div(batch, 2)
    if kind == "core":
        return core, lambda member: (2 * across + member, frame)
    if kind == "x":
        return across, lambda member: (core + 2 * member, frame)
    if kind == "y":
        return side, lambda member: (batch, 2 * column + member)
    if kind == "square":
        return 2 * across + side, lambda member: (
            core + 2 * lax.div(member, 2),
            2 * column + lax.rem(member, 2),
        )
    if kind == "z":
        return column, lambda member: (batch, 2 * member + side)
    bit = int(kind)
    mine = lax.rem(lax.div(column, bit), 2)
    return mine, lambda member: (batch, 2 * (column + bit * (member - mine)) + side)


class Summing:
    def __init__(self, kinds, data, result, landings, send_sem, recv_sem, chunk, first, rows, count):
        self.kinds, self.data, self.result = kinds, data, result
        self.landings, self.send_sem, self.recv_sem, self.chunk = landings, send_sem, recv_sem, chunk
        self.sizes = [level_size(kind, count) for kind in kinds]
        self.places, self.devices = zip(*(level_place(kind) for kind in kinds))
        self.starts, self.lengths = [first], [rows]
        for size, mine in zip(self.sizes, self.places):
            self.lengths.append(self.lengths[-1] // size)
            self.starts.append(self.starts[-1] + mine * self.lengths[-1])
        self.sent = []

    def others(self, level):
        size = self.sizes[level]
        return [lax.rem(self.places[level] + step, size) for step in range(1, size)]

    def rows(self, start, length):
        return pl.ds(pl.multiple_of(start, 16), length)

    def copy(self, way, level, source, target, member, slot):
        base = way * sum(self.sizes) + sum(self.sizes[:level])
        return pltpu.make_async_remote_copy(
            src_ref=source,
            dst_ref=target,
            send_sem=self.send_sem.at[self.chunk, base + member],
            recv_sem=self.recv_sem.at[self.chunk, base + slot],
            device_id=self.devices[level](member),
            device_id_type=MESH,
        )

    def scatter(self, level):
        length = self.lengths[level + 1]
        for member in self.others(level):
            rows = self.rows(self.starts[level] + member * length, length)
            mine = self.places[level]
            copy = self.copy(
                0, level, self.data.at[rows], self.landings[level].at[mine], member, mine
            )
            copy.start()
            self.sent.append(copy)

    def add(self, level):
        length, start = self.lengths[level + 1], self.starts[level + 1]
        others = self.others(level)
        landing = self.landings[level]
        for member in others:
            rows = self.rows(start, length)
            self.copy(0, level, self.data.at[rows], landing.at[member], member, member).wait_recv()
        tile = tile_of(length)
        target = self.result if level == len(self.sizes) - 1 else self.data

        def body(index, unused):
            inner = self.rows(index * tile, tile)
            outer = self.rows(start + index * tile, tile)
            value = self.data[outer, :].astype(f32)
            for member in others:
                value += landing[member, inner, :].astype(f32)
            target[outer, :] = value.astype(bf16)
            return unused

        lax.fori_loop(0, length // tile, body, 0)

    def gather(self, level):
        rows = self.rows(self.starts[level + 1], self.lengths[level + 1])
        mine = self.places[level]
        for member in self.others(level):
            copy = self.copy(1, level, self.result.at[rows], self.result.at[rows], member, mine)
            copy.start()
            self.sent.append(copy)

    def gathered(self, level):
        length = self.lengths[level + 1]
        for member in self.others(level):
            rows = self.rows(self.starts[level] + member * length, length)
            self.copy(
                1, level, self.result.at[rows], self.result.at[rows], member, member
            ).wait_recv()

    def steps(self):
        def step(*calls):
            def run():
                for call, level in calls:
                    call(level)

            return run

        last = len(self.sizes) - 1
        runs = [step((self.scatter, 0))]
        for level in range(last):
            runs.append(step((self.add, level), (self.scatter, level + 1)))
        runs.append(step((self.add, last), (self.gather, last)))
        for level in range(last, 0, -1):
            runs.append(step((self.gathered, level), (self.gather, level - 1)))
        runs.append(step((self.gathered, 0)))
        return runs

    def finish(self):
        for copy in self.sent:
            copy.wait_send()


def middle_kinds(count):
    bits, bit = [], 1
    while bit < count:
        bits.append(str(bit))
        bit *= 2
    return (("core","x","y","z"),("core","y","x","z"),("core","z","x","y"),("core","x","y","z"),("core","y","x","z"),("core","z","y","x"))


def chunk_rows(rows, chunks, count):
    unit = 128 * count
    units = rows // unit
    chunks = min(chunks, units)
    return [(units // chunks + (index < units % chunks)) * unit for index in range(chunks)]


def round_up(rows, count):
    unit = 128 * count
    return -(-rows // unit) * unit


def summing_scratch(kinds, rows, chunks, count):
    shapes = []
    for chunk, length in enumerate(chunk_rows(rows, chunks, count)):
        for kind in kinds[chunk % len(kinds)]:
            length //= level_size(kind, count)
            shapes.append(pltpu.VMEM((level_size(kind, count), length, 384), bf16))
    slots = 2 * sum(level_size(kind, count) for kind in kinds[0])
    return shapes + [pltpu.SemaphoreType.DMA((chunks, slots))] * 2


def make_summing(kinds, data, result, scratch, chunks, count):
    send_sem, recv_sem = scratch[-2:]
    levels = len(kinds[0])
    sums, first = [], 0
    for chunk, length in enumerate(chunk_rows(data.shape[0], chunks, count)):
        landings = scratch[levels * chunk : levels * (chunk + 1)]
        order = kinds[chunk % len(kinds)]
        sums.append(
            Summing(order, data, result, landings, send_sem, recv_sem, chunk, first, length, count)
        )
        first += length
    return sums


def greet_all(count):
    batch, frame, side, column, peer = place()
    core, across = lax.rem(batch, 2), lax.div(batch, 2)
    barrier = pltpu.get_barrier_semaphore()
    targets = [
        (batch + 1 - 2 * core, frame),
        (batch, peer),
        (core + 2 - 2 * across, frame),
        (core + 2 - 2 * across, peer),
    ]
    for step in range(1, count):
        targets.append((batch, 2 * lax.rem(column + step, count) + side))
    for target in targets:
        pl.semaphore_signal(barrier, inc=1, device_id=target, device_id_type=MESH)
    return len(targets)


TAIL_KINDS = (("core", "square", "z"), ("core", "z", "square"))
TAIL_CHUNKS = 3
MIDDLE_CHUNKS = 6
MIDDLE_TIMES = (0, 4, 16, 24, 30, 36, 44, 51, 56)
CHUNK_TIME = 0.6


def timed_steps(items):
    runs = [item.steps() for item in items]
    timed = []
    for step in range(len(runs[0])):
        for index, run in enumerate(runs):
            now = MIDDLE_TIMES[min(step, len(MIDDLE_TIMES) - 1)] + CHUNK_TIME * index
            timed.append((now, run[step]))
    return sorted(timed, key=lambda pair: pair[0])


def backward_kernel(
    frames,
    count,
    clip_count,
    clip_len,
    latents,
    time_embed,
    mod_rows,
    grad_attn_out,
    sums,
    weights,
    grad_att,
    attention,
    stats,
    mod_all,
    mod_peer,
    pairs,
    queries_in,
    w_qkv,
    spread_q,
    spread_o,
    sum_heads,
    grad_latents,
    tail_result,
    result,
    data,
    tail,
    grad_mod,
    grad_w,
    pack_out,
    pack_in,
    queries,
    grads,
    query_grad,
    key_grad,
    value_grad,
    flat_kv,
    part_out,
    part_in,
    peer_out,
    peer_in,
    held,
    held_mod,
    held_sem,
    load_sem,
    query_sem,
    send_sem,
    recv_sem,
    *scratch,
):
    batch, frame, side, column, peer = place()
    width = grad_att.shape[1]
    slots = part_out.shape[0]
    load = pltpu.make_async_copy(weights, data, load_sem)
    load.start()
    load_queries = pltpu.make_async_copy(queries_in, queries, query_sem)
    load_queries.start()
    head_size = width // HEADS

    def block_at(step):
        return jnp.where(step == count, column, nearest(count - step, column, count))

    def fetches(step):
        slot = lax.rem(step - 1, 2)
        block = block_at(step)
        return (
            pltpu.make_async_copy(pairs.at[block], held.at[slot], held_sem.at[slot]),
            pltpu.make_async_copy(mod_all.at[block], held_mod.at[slot], held_sem.at[2 + slot]),
        )

    def fetch(step):
        for copy in fetches(step):
            copy.start()

    def fetched(step):
        for copy in fetches(step):
            copy.wait()

    signals = greet_all(count)
    fetch(1)
    fetch(2)
    kinds = middle_kinds(count)
    levels = len(kinds[0])
    chunks = len(chunk_rows(data.shape[0], MIDDLE_CHUNKS, count))
    own = scratch[: levels * chunks + 2]
    items = make_summing(kinds, data, result, own, MIDDLE_CHUNKS, count)
    waiting = timed_steps(items)
    tail_items = make_summing(TAIL_KINDS, tail, tail_result, scratch[len(own) :], TAIL_CHUNKS, count)
    tail_waiting = [list(group) for group in zip(*(item.steps() for item in tail_items))]
    heads_done = [0]

    def advance():
        while waiting and waiting[0][0] <= heads_done[0]:
            waiting.pop(0)[1]()

    def to_peer(source, target, slot):
        return pltpu.make_async_remote_copy(
            src_ref=source,
            dst_ref=target,
            send_sem=send_sem.at[slot],
            recv_sem=recv_sem.at[slot],
            device_id=(batch, peer),
            device_id_type=MESH,
        )

    def toward(step, owner):
        up = owner > column
        other = jnp.where(up, column + 1, column - 1)
        slot = jnp.where((other == owner) & jnp.logical_not(up), count, owner)
        return pltpu.make_async_remote_copy(
            src_ref=part_out.at[lax.rem(step, slots)],
            dst_ref=part_in.at[slot],
            send_sem=send_sem.at[2 + step],
            recv_sem=recv_sem.at[2 + slot],
            device_id=(batch, 2 * other + side),
            device_id_type=MESH,
        )

    def arrived(slot):
        pltpu.make_async_remote_copy(
            src_ref=part_out.at[0],
            dst_ref=part_in.at[slot],
            send_sem=send_sem.at[2],
            recv_sem=recv_sem.at[2 + slot],
            device_id=(batch, peer),
            device_id_type=MESH,
        ).wait_recv()

    def pass_on(step):
        block = block_at(step)
        arrived(block)
        slot = lax.rem(step, slots)
        part_out[slot] = (part_out[slot].astype(f32) + part_in[block].astype(f32)).astype(bf16)
        toward(step, block).start()

    def chain_kind(step):
        block = block_at(step)
        up = block > column
        begins = jnp.where(up, column == 0, column == count - 1)
        late = jnp.where(column < count // 2, up, jnp.logical_not(up))
        return begins, late

    def pass_late(step):
        begins, late = chain_kind(step)

        @pl.when(jnp.logical_not(begins) & late)
        def _():
            pass_on(step)

    grad_now = grad_att[...]
    product = grad_now.astype(f32) * attention[...].astype(f32)
    high, middle, low = pieces(product)
    delta = (
        dg(high, sum_heads[...], NN) + dg(middle, sum_heads[...], NN) + dg(low, sum_heads[...], NN)
    )
    high, middle, low = (piece.astype(f32) for piece in pieces(-delta))
    which = lax.rem(lax.broadcasted_iota(jnp.int32, delta.shape, 1), 3)
    extra = jnp.where(which == 0, high, jnp.where(which == 1, middle, low))
    pack_out[:, :width] = grad_now
    pack_out[:, width:] = stats[...] + extra.astype(bf16)
    swap = to_peer(pack_out, pack_in, 0)
    load.wait()
    met(signals)
    swap.start()
    advance()
    query_grad[...] = jnp.zeros_like(query_grad)

    def prepare(half, source):
        rows = pl.ds(half * frames, frames)
        wide = dg(source, spread_o[...], NN)
        extra = dg(source[:, width:], spread_q[...], NN).astype(bf16)
        wide = wide.astype(bf16)
        for head in range(HEADS):
            lanes = slice(head * LANES, (head + 1) * LANES)
            grads[head, rows, :] = wide[:, lanes]
            queries[head, rows, :] += extra[:, lanes]

    def differentiate(half, slot, first, moving=True):
        rows = pl.ds(half * frames, frames)
        for head in range(HEADS):
            key, value = held[slot, 0, head], held[slot, 1, head]
            query, grad = queries[head, rows, :], grads[head, rows, :]
            probs = jnp.exp(dg(key, query, NT))
            dscore = (probs * dg(value, grad, NT)).astype(bf16)
            probs = probs.astype(bf16)
            more_k, more_v = dg(dscore, query, NN), dg(probs, grad, NN)
            if first:
                key_grad[slot, head] = more_k
                value_grad[slot, head] = more_v
            else:
                key_grad[slot, head] += more_k
                value_grad[slot, head] += more_v
            query_grad[head, :, rows] += dg(key, dscore, TN)
            if moving:
                heads_done[0] += 1
                advance()

    def finish_keys(slot):
        for kind, source in enumerate((key_grad, value_grad)):
            for pair in range(HEADS // 2):
                start = kind * width + pair * LANES
                flat_kv[:, start : start + LANES] = jnp.concatenate(
                    [
                        source[slot, 2 * pair][:, :head_size],
                        source[slot, 2 * pair + 1][:, :head_size],
                    ],
                    axis=1,
                ).astype(bf16)
        flat = flat_kv[...]
        return dg(flat, w_qkv[:, width:], NT), dg(held_mod[slot], flat, TN)

    def finish_queries(half, source):
        rows = pl.ds(half * frames, frames)
        flat = jnp.concatenate(
            [query_grad[head, :head_size, rows] for head in range(HEADS)], axis=0
        )
        flat = (flat * 0.125).T.astype(bf16)
        return dg(flat, w_qkv[:, :width], NT), dg(source, flat, TN)

    def send_block(step, slot, first):
        block = block_at(step)
        part, weight = finish_keys(slot)
        if not isinstance(step, int):

            @pl.when(step > slots)
            def _():
                toward(step - slots, block_at(step - slots)).wait_send()

        part_out[lax.rem(step, slots)] = part.astype(bf16)
        if first is False:
            pass_late(step - 1)
        begins, late = chain_kind(step)

        @pl.when(begins)
        def _():
            toward(step, block).start()

        @pl.when(jnp.logical_not(begins) & jnp.logical_not(late))
        def _():
            pass_on(step)

        if first:
            grad_w[:, width:] = weight
        else:
            grad_w[:, width:] += weight

        @pl.when(step + 2 <= count)
        def _():
            fetch(step + 2)

    load_queries.wait()
    prepare(0, pack_out[...])
    fetched(1)
    differentiate(0, 0, True)
    fetched(2)
    differentiate(0, 1, True)
    swap.wait()
    prepare(1, pack_in[...])
    differentiate(1, 0, False)
    send_block(1, 0, True)
    differentiate(1, 1, False)
    send_block(2, 1, False)

    def per_block(step, moving):
        slot = (step - 1) % 2 if isinstance(step, int) else lax.rem(step - 1, 2)
        fetched(step)
        differentiate(0, slot, True, moving)
        differentiate(1, slot, False, moving)
        send_block(step, slot, False)

    if count <= 4:
        for step in range(3, count):
            per_block(step, True)
    else:

        def looped(step, unused):
            per_block(step, False)
            return unused

        lax.fori_loop(3, count, looped, 0)
    slot = (count - 1) % 2
    fetched(count)
    differentiate(1, slot, True)
    pass_late(count - 1)
    part, weight = finish_queries(1, mod_peer[...])
    peer_out[...] = part.astype(bf16)
    back = to_peer(peer_out, peer_in, 1)
    back.start()
    grad_w[:, :width] = weight
    differentiate(0, slot, False)
    part, weight = finish_keys(slot)
    grad_w[:, width:] += weight
    mine, weight = finish_queries(0, held_mod[slot])
    grad_w[:, :width] += weight
    first = 0
    for part_index in range(3):
        tail[first : first + width, :] = grad_w[
            :, part_index * width : (part_index + 1) * width
        ].astype(bf16)
        first += width
    tail_waiting[0].pop(0)()
    grad_mod[...] = part + mine

    choice = row_choice(clip_ids(clip_len, clip_count, frame * frames, (frames, 16)), clip_count)
    ids = clip_ids(clip_len, clip_count, frame * frames, (frames, 16))
    lane = lax.broadcasted_iota(jnp.int32, (frames, 16), 1)
    members = ((lane == batch * clip_count + ids) & (ids < clip_count)).astype(f32).astype(bf16)
    normed, inverse = layer_norm(latents[...].astype(f32))
    scale = 1.0 + dg(choice, mod_rows[:, width : 2 * width], NN)
    first += 32
    for part in range(5):
        tail[first : first + 16, :] = sums[part].astype(bf16)
        first += 16
    time_low = time_embed[...].astype(f32)
    time_low = time_low / (1.0 + jnp.exp(-time_low))
    repeated = jnp.concatenate([time_low] * (16 // clip_count), axis=0)
    row = lax.broadcasted_iota(jnp.int32, (16, width), 0)
    mine = (lax.div(row, clip_count) == batch) & (frame == 0)
    tail[first : first + 16, :] = jnp.where(mine, repeated, 0.0).astype(bf16)
    first += 16
    tail[first:, :] = jnp.zeros((tail.shape[0] - first, width), bf16)

    @pl.when(column > 0)
    def _():
        arrived(column)
        grad_mod[...] += part_in[column].astype(f32)

    @pl.when(column < count - 1)
    def _():
        arrived(count)
        grad_mod[...] += part_in[count].astype(f32)

    back.wait()
    total = grad_mod[...] + peer_in[...].astype(f32)
    grad_latents[...] = (
        grad_attn_out[...] + norm_back(total * scale, normed, inverse)
    ).astype(bf16)
    first = 3 * width
    tail[first : first + 16, :] = clip_sums(members, total).astype(bf16)
    tail[first + 16 : first + 32, :] = clip_sums(members, total * normed).astype(bf16)

    for run in tail_waiting.pop(0):
        run()
    while waiting or tail_waiting:
        for unused in range(-(-len(waiting) // max(1, len(tail_waiting)))):
            waiting.pop(0)[1]()
        if tail_waiting:
            for run in tail_waiting.pop(0):
                run()

    def sent(step, unused):
        toward(step, block_at(step)).wait_send()
        return unused

    lax.fori_loop(max(1, count - slots), count, sent, 0)
    for item in items + tail_items:
        item.finish()


def backward_attention(clip_len, *given, count):
    latents, weights = given[0], given[5]
    frames, width = latents.shape
    slots = min(count, 4)
    tail_rows = round_up(3 * width + 8 * 16, count)
    vmem = pl.BlockSpec(memory_space=pltpu.VMEM)
    anywhere = pl.BlockSpec(memory_space=pl.ANY)
    specs = [vmem] * 5 + [anywhere] + [vmem] * 3 + [anywhere, vmem] + [anywhere] * 2 + [vmem] * 4
    return pl.pallas_call(
        functools.partial(backward_kernel, frames, count, clip_len.shape[1]),
        name="attention_backward",
        out_shape=(
            jax.ShapeDtypeStruct((frames, width), bf16),
            jax.ShapeDtypeStruct((tail_rows, width), bf16),
            jax.ShapeDtypeStruct(weights.shape, bf16),
        ),
        in_specs=[pl.BlockSpec(memory_space=pltpu.SMEM)] + specs,
        out_specs=(vmem,) * 3,
        scratch_shapes=[
            pltpu.VMEM(weights.shape, bf16),
            pltpu.VMEM((tail_rows, width), bf16),
            pltpu.VMEM((frames, width), f32),
            pltpu.VMEM((width, 3 * width), f32),
            pltpu.VMEM((frames, width + LANES), bf16),
            pltpu.VMEM((frames, width + LANES), bf16),
            pltpu.VMEM((HEADS, 2 * frames, LANES), bf16),
            pltpu.VMEM((HEADS, 2 * frames, LANES), bf16),
            pltpu.VMEM((HEADS, LANES, 2 * frames), f32),
            pltpu.VMEM((2, HEADS, frames, LANES), f32),
            pltpu.VMEM((2, HEADS, frames, LANES), f32),
            pltpu.VMEM((frames, 2 * width), bf16),
            pltpu.VMEM((slots, frames, width), bf16),
            pltpu.VMEM((count + 1, frames, width), bf16),
            pltpu.VMEM((frames, width), bf16),
            pltpu.VMEM((frames, width), bf16),
            pltpu.VMEM((2, 2, HEADS, frames, LANES), bf16),
            pltpu.VMEM((2, frames, width), bf16),
            pltpu.SemaphoreType.DMA((4,)),
            pltpu.SemaphoreType.DMA,
            pltpu.SemaphoreType.DMA,
            pltpu.SemaphoreType.DMA((2 + count,)),
            pltpu.SemaphoreType.DMA((3 + count,)),
        ]
        + summing_scratch(middle_kinds(count), weights.shape[0], MIDDLE_CHUNKS, count)
        + summing_scratch(TAIL_KINDS, tail_rows, TAIL_CHUNKS, count),
        compiler_params=pltpu.CompilerParams(
            collective_id=2, has_side_effects=True, vmem_limit_bytes=63 * 2**20
        ),
    )(clip_len, *given)


def spread_kernel(width, shapes, weights, tail, *refs):
    outs, (low, rows) = refs[: len(shapes)], refs[len(shapes) : len(shapes) + 2]
    stages, (load_sem, store_sem) = refs[len(shapes) + 2 : -2], refs[-2:]
    total = weights.shape[0]
    piece = 512
    loads = [pltpu.make_async_copy(tail, rows, load_sem.at[0])] + [
        pltpu.make_async_copy(
            weights.at[pl.ds(first, piece)], low.at[pl.ds(first, piece)], load_sem.at[1 + index]
        )
        for index, first in enumerate(range(0, total, piece))
    ]
    held = [0]

    def need(end):
        while held[0] * piece < end:
            held[0] += 1
            loads[held[0]].wait()

    for load in loads:
        load.start()
    stores = [
        pltpu.make_async_copy(stage, out, store_sem.at[index])
        for index, (stage, out) in enumerate(zip(stages, outs))
    ]
    ada, qkv, down, up, co, ckv, cq, ao, bias, gain = range(10)
    loads[0].wait()
    first = 3 * width
    marks = [rows[first + 16 * part : first + 16 * (part + 1), :] for part in range(8)]
    for part in range(6):
        here = slice(part * width, (part + 1) * width)
        stages[ada][:, here] = dg(marks[7], marks[part], TN)
        stages[bias][here] = jnp.sum(marks[part].astype(f32), axis=0)
    stages[gain][...] = jnp.sum(marks[6].astype(f32), axis=0)
    stores[ada].start()
    stores[bias].start()
    stores[gain].start()
    for part in range(3):
        stages[qkv][:, part * width : (part + 1) * width] = rows[
            part * width : (part + 1) * width, :
        ].astype(f32)
    stores[qkv].start()
    first = 0
    for part in range(shapes[down][0] // width):
        here = slice(part * width, (part + 1) * width)
        need(first + 2 * width)
        stages[down][here, :] = low[first : first + width, :].astype(f32)
        first += width
        stages[up][:, here] = low[first : first + width, :].astype(f32)
        first += width
    stores[down].start()
    stores[up].start()
    for index in (co, ckv, cq, ao):
        length = shapes[index][0]
        for part in range(shapes[index][1] // width):
            here = slice(part * width, (part + 1) * width)
            need(first + length)
            stages[index][:, here] = low[first : first + length, :].astype(f32)
            first += length
        stores[index].start()
    need(total)
    for store in stores:
        store.wait()


def spread_weights(weights, tail, text_width, hidden_width):
    width = weights.shape[1]
    square = (width, width)
    shapes = [
        (width, 6 * width),
        (width, 3 * width),
        (hidden_width, width),
        (width, hidden_width),
        square,
        (text_width, 2 * width),
        square,
        square,
        (6 * width,),
        (width,),
    ]
    anywhere = pl.BlockSpec(memory_space=pl.ANY)
    return pl.pallas_call(
        functools.partial(spread_kernel, width, shapes),
        name="weight_gradients",
        out_shape=[jax.ShapeDtypeStruct(shape, f32) for shape in shapes],
        in_specs=[anywhere] * 2,
        out_specs=[anywhere] * len(shapes),
        scratch_shapes=[pltpu.VMEM(weights.shape, bf16), pltpu.VMEM(tail.shape, bf16)]
        + [pltpu.VMEM(shape, f32) for shape in shapes]
        + [pltpu.SemaphoreType.DMA((1 + weights.shape[0] // 512,)), pltpu.SemaphoreType.DMA((len(shapes),))],
        compiler_params=pltpu.CompilerParams(vmem_limit_bytes=62 * 2**20),
    )(weights, tail)


def spread_matrices(width):
    head_size = width // HEADS
    lane = np.arange(HEADS * LANES, dtype=np.int32)[None, :]
    head, inner = lane // LANES, lane % LANES
    row = np.arange(LANES, dtype=np.int32)[:, None]
    spread_q = (row < 3 * HEADS) & (head == row // 3) & (inner == head_size + 4 + row % 3)
    row = np.arange(width, dtype=np.int32)[:, None]
    spread_o = [(head == row // head_size) & (inner == row % head_size)]
    row = np.arange(LANES, dtype=np.int32)[:, None] - 3 * HEADS
    spread_o.append((row >= 0) & (head == row // 3) & (inner == head_size + row % 3))
    column = np.arange(LANES, dtype=np.int32)[None, :] - 3 * HEADS
    sum_heads = np.arange(width, dtype=np.int32)[:, None] // head_size == column // 3
    return (
        spread_q.astype(bf16),
        np.concatenate(spread_o, axis=0).astype(bf16),
        sum_heads.astype(bf16),
    )


def per_device(
    latents,
    time_embed,
    text_states,
    text_len,
    clip_len,
    cotangent,
    w_ada,
    b_ada,
    w_qkv,
    w_ao,
    gain_cross,
    w_cq,
    w_ckv,
    w_co,
    w_up,
    w_down,
):
    frames = latents.shape[1]
    width = latents.shape[2]
    clip_count = time_embed.shape[1]
    text_slots = text_states.shape[2]
    count = lax.axis_size("frame") // 2
    attention, stats, mod_rows, mod_all, mod_peer, pairs, queries = forward_attention(
        clip_len, latents[0], time_embed[0], w_ada, b_ada, w_qkv, count
    )
    text_rows = text_states[0].reshape(clip_count * text_slots, text_states.shape[3])
    mixed, grad_attention, grad_attn_out, sums, weights = middle_part(
        clip_len,
        text_len,
        latents[0],
        cotangent[0],
        attention,
        mod_rows,
        text_rows,
        gain_cross,
        w_ao,
        w_cq,
        w_ckv,
        w_co,
        w_up,
        w_down,
        count=count,
    )

    grad_latents, tail, weights = backward_attention(
        clip_len,
        latents[0],
        time_embed[0],
        mod_rows,
        grad_attn_out,
        sums,
        weights,
        grad_attention,
        attention,
        stats,
        mod_all,
        mod_peer,
        pairs,
        queries,
        w_qkv,
        *spread_matrices(width),
        count=count,
    )
    ada, qkv, down, up, co, ckv, cq, ao, bias, gain = spread_weights(
        weights, tail, text_rows.shape[1], w_up.shape[1]
    )
    grads = (ada, bias, qkv, ao, gain, cq, ckv, co, up, down)
    return (mixed[None], grad_latents[None]) + grads


def solution(mesh):
    placed = (
        P("batch", "frame", None),
        P("batch", None, None),
        P("batch", None, None, None),
        P("batch", None),
        P("batch", None),
        P("batch", "frame", None),
    ) + (P(),) * 10
    return jax.shard_map(
        per_device,
        mesh=mesh,
        in_specs=placed,
        out_specs=(P("batch", "frame", None), P("batch", "frame", None)) + (P(),) * 10,
        check_vma=False,
    )
```

```python
import functools
import math

import jax
import jax.numpy as jnp
import numpy as np
from jax import lax
from jax.experimental import pallas as pl
from jax.experimental.pallas import tpu as pltpu
from jax.sharding import PartitionSpec as P

HEADS = 6
LANES = 128
MASKED = -1e30

f32 = jnp.float32
bf16 = jnp.bfloat16
eps_norm = 1e-06
MESH = pl.DeviceIdType.MESH

NT = (((1,), (1,)), ((), ()))
NN = (((1,), (0,)), ((), ()))
TN = (((0,), (0,)), ((), ()))


def dg(left, right, dims):
    return lax.dot_general(left, right, dims, preferred_element_type=f32)


def layer_norm(values):
    center = values - jnp.mean(values, axis=-1, keepdims=True)
    inverse = lax.rsqrt(jnp.mean(center * center, axis=-1, keepdims=True) + eps_norm)
    return (center * inverse, inverse)


def norm_back(grad, normed, inverse):
    mean_grad = jnp.mean(grad, axis=-1, keepdims=True)
    mean_prod = jnp.mean(grad * normed, axis=-1, keepdims=True)
    return (grad - mean_grad - normed * mean_prod) * inverse


def pieces(value):
    high = value.astype(bf16)
    rest = value - high.astype(f32)
    middle = rest.astype(bf16)
    low = (rest - middle.astype(f32)).astype(bf16)
    return high, middle, low


def nearest(step, me, count):
    lower = me < count // 2
    mine = jnp.where(lower, me, count - 1 - me)
    index = jnp.where(step - 1 < mine, step - 1, step)
    return jnp.where(lower, index, count - 1 - index)


def place():
    batch = lax.axis_index("batch")
    frame = lax.axis_index("frame")
    side = lax.rem(frame, 2)
    column = lax.div(frame, 2)
    return batch, frame, side, column, frame + 1 - 2 * side


def greet(batch, side, column, count, peer):
    barrier = pltpu.get_barrier_semaphore()
    pl.semaphore_signal(barrier, inc=1, device_id=(batch, peer), device_id_type=MESH)
    for step in range(1, count):
        other = nearest(step, column, count)
        pl.semaphore_signal(
            barrier, inc=1, device_id=(batch, 2 * other + side), device_id_type=MESH
        )


def met(signals):
    pl.semaphore_wait(pltpu.get_barrier_semaphore(), signals)


def clip_ids(clip_len, clip_count, first, shape):
    position = first + lax.broadcasted_iota(jnp.int32, shape, 0)
    ids = jnp.zeros(shape, jnp.int32)
    end = 0
    for clip in range(clip_count):
        end = end + clip_len[0, clip]
        ids += (position >= end).astype(jnp.int32)
    return ids


def row_choice(ids, clip_count):
    lane = lax.broadcasted_iota(jnp.int32, ids.shape, 1)
    return ((lax.rem(lane, clip_count) == ids) & (lane < 3 * clip_count)).astype(bf16)


def head_tile(flat, head, tail):
    size = LANES - tail.shape[1]
    return jnp.concatenate([flat[:, head * size : (head + 1) * size], tail], axis=1)


def forward_kernel(
    frames,
    count,
    clip_count,
    clip_len,
    latents,
    time_embed,
    w_ada,
    b_ada,
    w_qkv,
    attention,
    stats,
    mod_rows,
    mod_all,
    mod_peer,
    pairs_out,
    queries,
    pairs,
    total,
    tops,
    part_out,
    part_in,
    stat_out,
    stat_in,
    pairs_sem,
    send_sem,
    recv_sem,
):
    batch, frame, side, column, peer = place()
    width = latents.shape[1]
    head_size = width // HEADS
    greet(batch, side, column, count, peer)

    def to_peer(source, target, slot):
        return pltpu.make_async_remote_copy(
            src_ref=source,
            dst_ref=target,
            send_sem=send_sem.at[slot],
            recv_sem=recv_sem.at[slot],
            device_id=(batch, peer),
            device_id_type=MESH,
        )

    def to_column(step, other, slot):
        return pltpu.make_async_remote_copy(
            src_ref=mod_all.at[slot],
            dst_ref=mod_all.at[slot],
            send_sem=send_sem.at[4 + step],
            recv_sem=recv_sem.at[4 + slot],
            device_id=(batch, 2 * other + side),
            device_id_type=MESH,
        )

    time_low = time_embed[...].astype(f32)
    time_low = (time_low / (1.0 + jnp.exp(-time_low))).astype(bf16)
    modulation = dg(time_low, w_ada[...], NN) + b_ada[...][None, :]
    parts = [piece.astype(f32) for piece in pieces(modulation)]
    parts.append(jnp.zeros((16 - 3 * clip_count, modulation.shape[1]), f32))
    mod_rows[...] = jnp.concatenate(parts, axis=0).astype(bf16)
    choice = row_choice(clip_ids(clip_len, clip_count, frame * frames, (frames, 16)), clip_count)
    normed, inverse = layer_norm(latents[...].astype(f32))
    shift, scale = (
        dg(choice, mod_rows[:, part * width : (part + 1) * width], NN) for part in range(2)
    )
    mod_all[column] = (normed * (1.0 + scale) + shift).astype(bf16)
    met(count)
    swap = to_peer(mod_all.at[column], mod_peer, 0)
    relayed = count == 4

    def hop(block, up):
        other = column + 1 if up else column - 1
        return pltpu.make_async_remote_copy(
            src_ref=mod_all.at[block],
            dst_ref=mod_all.at[block],
            send_sem=send_sem.at[4 + block + (0 if up else count)],
            recv_sem=recv_sem.at[4 + block],
            device_id=(batch, 2 * other + side),
            device_id_type=MESH,
        )

    def each_hop(distance, act):
        for up in (True, False):
            block = column - distance if up else column + distance
            here = block >= 0 if up else block < count
            further = column < count - 1 if up else column > 0
            act(block, up, here, further)

    def begin(block, up, here, further):
        @pl.when(here & further)
        def _():
            hop(block, up).start()

    def take(block, up, here, further):
        @pl.when(here)
        def _():
            hop(block, up).wait_recv()

        begin(block, up, here, further)

    def end(block, up, here, further):
        @pl.when(here & further)
        def _():
            hop(block, up).wait_send()

    if relayed:
        each_hop(0, begin)
        swap.start()
    else:
        sends = [
            to_column(step, nearest(step, column, count), column) for step in range(1, count)
        ]
        for index, send in enumerate(sends):
            send.start()
            if index == 0:
                swap.start()
    total[...] = jnp.zeros_like(total)
    tops[...] = jnp.full_like(tops, -1e38)
    tail = (frames, LANES - head_size)
    lane = lax.broadcasted_iota(jnp.int32, tail, 1)
    ones = jnp.ones(tail, bf16)

    def make_queries(half, owner, source):
        rows = pl.ds(half * frames, frames)
        flat = dg(source, w_qkv[:, :width], NN).astype(bf16) * 0.125
        ids = clip_ids(clip_len, clip_count, owner * frames, tail)
        extra = (ids == lane).astype(f32).astype(bf16)
        for head in range(HEADS):
            queries[head, rows, :] = head_tile(flat, head, extra)

    def make_keys(block):
        source = mod_all[block]
        ids = clip_ids(clip_len, clip_count, (2 * block + side) * frames, tail)
        masks = jnp.where((ids == lane) | (lane > clip_count), 0.0, MASKED)
        extra = jnp.where(
            lane < clip_count, masks, jnp.where(lane < clip_count + 3, 1.0, 0.0)
        ).astype(bf16)
        flat = dg(source, w_qkv[:, width : 2 * width], NN).astype(bf16)
        for head in range(HEADS):
            pairs[block, 0, head] = head_tile(flat, head, extra)
        flat = dg(source, w_qkv[:, 2 * width :], NN).astype(bf16)
        for head in range(HEADS):
            pairs[block, 1, head] = head_tile(flat, head, ones)
        keep(block).start()

    def keep(block):
        return pltpu.make_async_copy(
            pairs.at[block], pairs_out.at[block], pairs_sem.at[block]
        )

    def attend(half, block, heads=range(HEADS)):
        rows = pl.ds(half * frames, frames)

        def scores(head):
            now = dg(pairs[block, 0, head], queries[head, rows, :], NT)
            return now, jnp.max(now, axis=0, keepdims=True)

        ahead = scores(heads[0])
        for head in heads:
            now, top = ahead
            if head != heads[-1]:
                ahead = scores(head + 1)
            before = tops[head, :1, rows]
            new = jnp.maximum(before, top)
            probs = jnp.exp(now - new).astype(bf16)
            total[head, :, rows] = total[head, :, rows] * jnp.exp(before - new) + dg(
                pairs[block, 1, head], probs, TN
            )
            tops[head, :, rows] = jnp.broadcast_to(new, (8, frames))

    def arrive(step):
        block = nearest(step, column, count)
        if not relayed:
            to_column(step, block, block).wait_recv()
        make_keys(block)
        return block

    make_queries(0, frame, mod_all[column])
    make_keys(column)
    attend(0, column)
    swap.wait()
    make_queries(1, peer, mod_peer[...])
    attend(1, column)

    if relayed:
        outer = (column == 0) | (column == count - 1)
        each_hop(1, take)
        block = arrive(1)
        attend(0, block)
        attend(1, block)

        @pl.when(outer)
        def _():
            each_hop(2, take)

        block = arrive(2)
        attend(0, block)

        @pl.when(jnp.logical_not(outer))
        def _():
            each_hop(2, take)

        attend(1, block)
        each_hop(3, take)
    else:

        def per_block(step, unused):
            block = arrive(step)
            attend(0, block)
            attend(1, block)
            return unused

        lax.fori_loop(1, count - 1, per_block, 0)
    block = arrive(count - 1)
    there = pl.ds(frames, frames)
    heads_half = HEADS // 2
    parts = []
    for side_part in range(2):
        heads = range(side_part * heads_half, (side_part + 1) * heads_half)
        attend(1, block, heads)
        for head in heads:
            part_out[head * head_size : (head + 1) * head_size, :] = total[
                head, :head_size, there
            ].astype(bf16)
            stat_out[head : head + 1, :] = tops[head, :1, there]
            stat_out[8 + head : 9 + head, :] = total[head, head_size : head_size + 1, there]
        chosen = pl.ds(side_part * heads_half * head_size, heads_half * head_size)
        parts.append(to_peer(part_out.at[chosen], part_in.at[chosen], 1 + side_part))
        parts[-1].start()
    parts.append(to_peer(stat_out, stat_in, 3))
    parts[-1].start()
    attend(0, block)
    for part in parts:
        part.wait()
    here = pl.ds(0, frames)
    joined = []
    logs = []
    for head in range(HEADS):
        mine, theirs = tops[head, :1, here], stat_in[head : head + 1, :]
        new = jnp.maximum(mine, theirs)
        left, right = jnp.exp(mine - new), jnp.exp(theirs - new)
        row_sum = (
            total[head, head_size : head_size + 1, here] * left
            + stat_in[8 + head : 9 + head, :] * right
        )
        logs.append(new + jnp.log(row_sum))
        scale = 1.0 / row_sum
        joined.append(
            total[head, :head_size, here] * (left * scale)
            + part_in[head * head_size : (head + 1) * head_size, :].astype(f32) * (right * scale)
        )
    attention[...] = jnp.concatenate(joined, axis=0).T.astype(bf16)
    rows = [piece for log in logs for piece in log_pieces(log)]
    rows.append(jnp.zeros((LANES - len(rows), frames), f32))
    stats[...] = jnp.concatenate(rows, axis=0).T.astype(bf16)
    for kept in range(count):
        keep(kept).wait()
    if relayed:
        for distance in range(count - 1):
            each_hop(distance, end)
    else:
        for send in sends:
            send.wait_send()


def log_pieces(log):
    high, middle, low = pieces(-log)
    return [high.astype(f32), middle.astype(f32), low.astype(f32)]


def forward_attention(clip_len, latents, time_embed, w_ada, b_ada, w_qkv, count):
    frames, width = latents.shape
    clip_count = clip_len.shape[1]
    vmem = pl.BlockSpec(memory_space=pltpu.VMEM)
    shapes = (
        jax.ShapeDtypeStruct((frames, width), bf16),
        jax.ShapeDtypeStruct((frames, LANES), bf16),
        jax.ShapeDtypeStruct((16, w_ada.shape[1]), bf16),
        jax.ShapeDtypeStruct((count, frames, width), bf16),
        jax.ShapeDtypeStruct((frames, width), bf16),
        jax.ShapeDtypeStruct((count, 2, HEADS, frames, LANES), bf16),
        jax.ShapeDtypeStruct((HEADS, 2 * frames, LANES), bf16),
    )
    return pl.pallas_call(
        functools.partial(forward_kernel, frames, count, clip_count),
        name="attention_forward",
        out_shape=shapes,
        in_specs=[pl.BlockSpec(memory_space=pltpu.SMEM)] + [vmem] * 5,
        out_specs=(vmem,) * 5 + (pl.BlockSpec(memory_space=pl.ANY), vmem),
        scratch_shapes=[
            pltpu.VMEM((count, 2, HEADS, frames, LANES), bf16),
            pltpu.VMEM((HEADS, LANES, 2 * frames), f32),
            pltpu.VMEM((HEADS, 8, 2 * frames), f32),
            pltpu.VMEM((width, frames), bf16),
            pltpu.VMEM((width, frames), bf16),
            pltpu.VMEM((16, frames), f32),
            pltpu.VMEM((16, frames), f32),
            pltpu.SemaphoreType.DMA((count,)),
            pltpu.SemaphoreType.DMA((4 + 2 * count,)),
            pltpu.SemaphoreType.DMA((4 + count,)),
        ],
        compiler_params=pltpu.CompilerParams(
            collective_id=1, has_side_effects=True, vmem_limit_bytes=62 * 2**20
        ),
    )(clip_len, latents, time_embed, w_ada, b_ada, w_qkv)


def clip_sums(choice, value):
    high = value.astype(bf16)
    low = (value - high.astype(f32)).astype(bf16)
    return dg(choice, high, TN) + dg(choice, low, TN)


def middle_kernel(
    frames,
    clip_count,
    clip_len,
    text_len,
    latents,
    cotangent,
    attention,
    mod_rows,
    text_rows,
    gain_cross,
    w_ao,
    w_cq,
    w_ckv,
    w_co,
    w_up_given,
    w_down_given,
    mixed,
    grad_att,
    grad_attn_out,
    sums,
    weights_out,
    weights,
    w_up,
    w_down,
    moves,
    key_tiles,
    query_tiles,
    grad_tiles,
    probs_kept,
    flat_kv,
):
    loads = [
        pltpu.make_async_copy(w_up_given, w_up, moves.at[0]),
        pltpu.make_async_copy(w_down_given, w_down, moves.at[1]),
    ]
    for load in loads:
        load.start()
    batch, frame, side, column, peer = place()
    width = latents.shape[1]
    head_size = width // HEADS
    slots = text_rows.shape[0]
    per_clip = slots // clip_count
    tail = (frames, LANES - head_size)

    wide_ids = clip_ids(clip_len, clip_count, frame * frames, (frames, 16))
    choice = row_choice(wide_ids, clip_count)
    group_lane = lax.broadcasted_iota(jnp.int32, (frames, 16), 1)
    members = ((group_lane == batch * clip_count + wide_ids) & (wide_ids < clip_count)).astype(f32)
    members = members.astype(bf16)
    ids = clip_ids(clip_len, clip_count, frame * frames, (frames, width))
    valid = (ids < clip_count).astype(f32)

    def mod_part(part):
        return dg(choice, mod_rows[:, part * width : (part + 1) * width], NN)

    gate_attn = mod_part(2) * valid
    branch_attn = dg(attention[...], w_ao[...], NN)
    after_attn = latents[...].astype(f32) + gate_attn * branch_attn
    normed_cross, inverse_cross = layer_norm(after_attn)
    gain = gain_cross[...][None, :]
    cross_in = (normed_cross * gain).astype(bf16)

    flat = dg(cross_in, w_cq[...], NN).astype(bf16) * 0.125
    lane = lax.broadcasted_iota(jnp.int32, tail, 1)
    extra = (clip_ids(clip_len, clip_count, frame * frames, tail) == lane).astype(f32).astype(bf16)
    for head in range(HEADS):
        query_tiles[head] = head_tile(flat, head, extra)
    slot = lax.broadcasted_iota(jnp.int32, (slots, LANES - head_size), 0)
    lane = lax.broadcasted_iota(jnp.int32, (slots, LANES - head_size), 1)
    live = jnp.zeros(lane.shape, jnp.bool_)
    for clip in range(clip_count):
        inside = (slot >= clip * per_clip) & (slot < clip * per_clip + text_len[0, clip])
        live = live | (inside & (lane == clip))
    extra = jnp.where(live | (lane >= clip_count), 0.0, MASKED).astype(bf16)
    flat = dg(text_rows[...], w_ckv[:, :width], NN).astype(bf16)
    for head in range(HEADS):
        key_tiles[0, head] = head_tile(flat, head, extra)
    extra = (lane < 3).astype(f32).astype(bf16)
    flat = dg(text_rows[...], w_ckv[:, width:], NN).astype(bf16)
    for head in range(HEADS):
        key_tiles[1, head] = head_tile(flat, head, extra)

    def scores(head):
        now = dg(key_tiles[0, head], query_tiles[head], NT)
        return now, jnp.max(now, axis=0, keepdims=True)

    joined = []
    ahead = scores(0)
    for head in range(HEADS):
        now, top = ahead
        if head + 1 < HEADS:
            ahead = scores(head + 1)
        probs = jnp.exp(now - top)
        probs = (probs * (1.0 / jnp.sum(probs, axis=0, keepdims=True))).astype(bf16)
        probs_kept[head] = probs
        joined.append(dg(key_tiles[1, head], probs, TN)[:head_size])
    cross_exact = jnp.concatenate(joined, axis=0).T
    cross = cross_exact.astype(bf16)
    after_cross = after_attn + dg(cross, w_co[...], NN) * valid
    normed_mlp, inverse_mlp = layer_norm(after_cross)
    scale_mlp = 1.0 + mod_part(4)
    mlp_in = (normed_mlp * scale_mlp + mod_part(3)).astype(bf16)
    gate_mlp = mod_part(5) * valid
    grad_out = cotangent[...].astype(f32)
    grad_mlp = (grad_out * gate_mlp).astype(bf16)
    root = math.sqrt(2.0 / math.pi)
    branch_mlp = jnp.zeros((frames, width), f32)
    grad_mlp_in = jnp.zeros((frames, width), f32)
    hidden_width = w_up.shape[1]
    first = 0
    for load in loads:
        load.wait()
    for part in range(hidden_width // width):
        here = slice(part * width, (part + 1) * width)
        hidden = dg(mlp_in, w_up[:, here], NN)
        square = hidden * hidden
        bend = jnp.tanh(root * hidden * (1.0 + 0.044715 * square))
        half = 0.5 * (1.0 + bend)
        activated = (hidden * half).astype(bf16)
        slope = half + (0.5 * root) * hidden * (1.0 - bend * bend) * (1.0 + 0.134145 * square)
        grad_hidden = (dg(grad_mlp, w_down[here, :], NT) * slope).astype(bf16)
        branch_mlp += dg(activated, w_down[here, :], NN)
        grad_mlp_in += dg(grad_hidden, w_up[:, here], NT)
        weights[first : first + width, :] = dg(activated, grad_mlp, TN).astype(bf16)
        first += width
        weights[first : first + width, :] = dg(mlp_in, grad_hidden, TN).astype(bf16)
        first += width
    stores = [
        pltpu.make_async_copy(
            weights.at[pl.ds(0, first)], weights_out.at[pl.ds(0, first)], moves.at[2]
        )
    ]
    stores[0].start()
    begun = first
    mixed[...] = (after_cross + gate_mlp * branch_mlp).astype(bf16)
    sums[3] = clip_sums(members, grad_out * branch_mlp)
    sums[1] = clip_sums(members, grad_mlp_in)
    sums[2] = clip_sums(members, grad_mlp_in * normed_mlp)
    grad_cross_out = grad_out + norm_back(grad_mlp_in * scale_mlp, normed_mlp, inverse_mlp)
    grad_branch = (grad_cross_out * valid).astype(bf16)
    weights[first : first + width, :] = dg(cross, grad_branch, TN).astype(bf16)
    first += width

    flat = dg(grad_branch, w_co[...], NT).astype(bf16)
    product = flat.astype(f32) * cross_exact
    lane = lax.broadcasted_iota(jnp.int32, tail, 1)
    for head in range(HEADS):
        part = product[:, head * head_size : (head + 1) * head_size]
        high, middle, low = pieces(-jnp.sum(part, axis=1, keepdims=True))
        extra = jnp.where(
            lane == 0,
            high.astype(f32),
            jnp.where(lane == 1, middle.astype(f32), jnp.where(lane == 2, low.astype(f32), 0.0)),
        ).astype(bf16)
        grad_tiles[head] = head_tile(flat, head, extra)
    joined = []
    for pair in range(HEADS // 2):
        kept = []
        for head in (2 * pair, 2 * pair + 1):
            probs = probs_kept[head]
            dscore = dg(key_tiles[1, head], grad_tiles[head], NT) * probs.astype(f32)
            dscore = dscore.astype(bf16)
            joined.append(dg(key_tiles[0, head], dscore, TN)[:head_size])
            kept.append(
                (
                    dg(dscore, query_tiles[head], NN)[:, :head_size],
                    dg(probs, grad_tiles[head], NN)[:, :head_size],
                )
            )
        for kind in range(2):
            start = kind * width + pair * LANES
            flat_kv[:, start : start + LANES] = jnp.concatenate(
                [kept[0][kind], kept[1][kind]], axis=1
            ).astype(bf16)
    for kind in range(2):
        grad = dg(text_rows[...], flat_kv[:, kind * width : (kind + 1) * width], TN)
        weights[first : first + grad.shape[0], :] = grad.astype(bf16)
        first += grad.shape[0]
    grad_queries = (jnp.concatenate(joined, axis=0) * 0.125).T.astype(bf16)
    weights[first : first + width, :] = dg(cross_in, grad_queries, TN).astype(bf16)
    first += width
    grad_cross_in = dg(grad_queries, w_cq[...], NT)
    grad_gain = jnp.sum(grad_cross_in * normed_cross, axis=0, keepdims=True)
    top_row = lax.broadcasted_iota(jnp.int32, (16, width), 0) == 0
    sums[4] = jnp.where(top_row, grad_gain, 0.0)
    grad_attn = grad_cross_out + norm_back(grad_cross_in * gain, normed_cross, inverse_cross)
    grad_attn_out[...] = grad_attn
    sums[0] = clip_sums(members, grad_attn * branch_attn)
    grad_branch = (grad_attn * gate_attn).astype(bf16)
    weights[first : first + width, :] = dg(attention[...], grad_branch, TN).astype(bf16)
    first += width
    grad_att[...] = dg(grad_branch, w_ao[...], NT).astype(bf16)
    weights[first:, :] = jnp.zeros((weights.shape[0] - first, width), bf16)
    rest = pl.ds(begun, weights.shape[0] - begun)
    stores.append(pltpu.make_async_copy(weights.at[rest], weights_out.at[rest], moves.at[3]))
    stores[1].start()
    for store in stores:
        store.wait()


def middle_lengths(width, text_width, hidden_width):
    return [width] * (2 * hidden_width // width + 1) + [text_width] * 2 + [width] * 2


def middle_part(clip_len, text_len, latents, *others, count):
    frames, width = latents.shape
    text_rows, w_up = others[3], others[9]
    slots, text_width = text_rows.shape
    rows = round_up(sum(middle_lengths(width, text_width, w_up.shape[1])), count)
    vmem = pl.BlockSpec(memory_space=pltpu.VMEM)
    smem = pl.BlockSpec(memory_space=pltpu.SMEM)
    anywhere = pl.BlockSpec(memory_space=pl.ANY)
    return pl.pallas_call(
        functools.partial(middle_kernel, frames, clip_len.shape[1]),
        name="middle",
        out_shape=(
            jax.ShapeDtypeStruct((frames, width), bf16),
            jax.ShapeDtypeStruct((frames, width), bf16),
            jax.ShapeDtypeStruct((frames, width), f32),
            jax.ShapeDtypeStruct((5, 16, width), f32),
            jax.ShapeDtypeStruct((rows, width), bf16),
        ),
        in_specs=[smem] * 2 + [vmem] * 10 + [anywhere] * 2,
        out_specs=(vmem,) * 4 + (anywhere,),
        scratch_shapes=[
            pltpu.VMEM((rows, width), bf16),
            pltpu.VMEM(w_up.shape, bf16),
            pltpu.VMEM(w_up.shape[::-1], bf16),
            pltpu.SemaphoreType.DMA((4,)),
            pltpu.VMEM((2, HEADS, slots, LANES), bf16),
            pltpu.VMEM((HEADS, frames, LANES), bf16),
            pltpu.VMEM((HEADS, frames, LANES), bf16),
            pltpu.VMEM((HEADS, slots, frames), bf16),
            pltpu.VMEM((slots, 2 * width), bf16),
        ],
        compiler_params=pltpu.CompilerParams(vmem_limit_bytes=62 * 2**20),
    )(clip_len, text_len, latents, *others)


def tile_of(rows):
    return max(tile for tile in range(16, 129, 16) if rows % tile == 0)


def level_size(kind, count):
    return {"square": 4, "z": count}.get(kind, 2)


def level_place(kind):
    batch, frame, side, column, peer = place()
    core, across = lax.rem(batch, 2), lax.div(batch, 2)
    if kind == "core":
        return core, lambda member: (2 * across + member, frame)
    if kind == "x":
        return across, lambda member: (core + 2 * member, frame)
    if kind == "y":
        return side, lambda member: (batch, 2 * column + member)
    if kind == "square":
        return 2 * across + side, lambda member: (
            core + 2 * lax.div(member, 2),
            2 * column + lax.rem(member, 2),
        )
    if kind == "z":
        return column, lambda member: (batch, 2 * member + side)
    bit = int(kind)
    mine = lax.rem(lax.div(column, bit), 2)
    return mine, lambda member: (batch, 2 * (column + bit * (member - mine)) + side)


class Summing:
    def __init__(self, kinds, data, result, landings, send_sem, recv_sem, chunk, first, rows, count):
        self.kinds, self.data, self.result = kinds, data, result
        self.landings, self.send_sem, self.recv_sem, self.chunk = landings, send_sem, recv_sem, chunk
        self.sizes = [level_size(kind, count) for kind in kinds]
        self.places, self.devices = zip(*(level_place(kind) for kind in kinds))
        self.starts, self.lengths = [first], [rows]
        for size, mine in zip(self.sizes, self.places):
            self.lengths.append(self.lengths[-1] // size)
            self.starts.append(self.starts[-1] + mine * self.lengths[-1])
        self.sent = []

    def others(self, level):
        size = self.sizes[level]
        return [lax.rem(self.places[level] + step, size) for step in range(1, size)]

    def rows(self, start, length):
        return pl.ds(pl.multiple_of(start, 16), length)

    def copy(self, way, level, source, target, member, slot):
        base = way * sum(self.sizes) + sum(self.sizes[:level])
        return pltpu.make_async_remote_copy(
            src_ref=source,
            dst_ref=target,
            send_sem=self.send_sem.at[self.chunk, base + member],
            recv_sem=self.recv_sem.at[self.chunk, base + slot],
            device_id=self.devices[level](member),
            device_id_type=MESH,
        )

    def scatter(self, level):
        length = self.lengths[level + 1]
        for member in self.others(level):
            rows = self.rows(self.starts[level] + member * length, length)
            mine = self.places[level]
            copy = self.copy(
                0, level, self.data.at[rows], self.landings[level].at[mine], member, mine
            )
            copy.start()
            self.sent.append(copy)

    def add(self, level):
        length, start = self.lengths[level + 1], self.starts[level + 1]
        others = self.others(level)
        landing = self.landings[level]
        for member in others:
            rows = self.rows(start, length)
            self.copy(0, level, self.data.at[rows], landing.at[member], member, member).wait_recv()
        tile = tile_of(length)
        target = self.result if level == len(self.sizes) - 1 else self.data

        def body(index, unused):
            inner = self.rows(index * tile, tile)
            outer = self.rows(start + index * tile, tile)
            value = self.data[outer, :].astype(f32)
            for member in others:
                value += landing[member, inner, :].astype(f32)
            target[outer, :] = value.astype(bf16)
            return unused

        lax.fori_loop(0, length // tile, body, 0)

    def gather(self, level):
        rows = self.rows(self.starts[level + 1], self.lengths[level + 1])
        mine = self.places[level]
        for member in self.others(level):
            copy = self.copy(1, level, self.result.at[rows], self.result.at[rows], member, mine)
            copy.start()
            self.sent.append(copy)

    def gathered(self, level):
        length = self.lengths[level + 1]
        for member in self.others(level):
            rows = self.rows(self.starts[level] + member * length, length)
            self.copy(
                1, level, self.result.at[rows], self.result.at[rows], member, member
            ).wait_recv()

    def steps(self):
        def step(*calls):
            def run():
                for call, level in calls:
                    call(level)

            return run

        last = len(self.sizes) - 1
        runs = [step((self.scatter, 0))]
        for level in range(last):
            runs.append(step((self.add, level), (self.scatter, level + 1)))
        runs.append(step((self.add, last), (self.gather, last)))
        for level in range(last, 0, -1):
            runs.append(step((self.gathered, level), (self.gather, level - 1)))
        runs.append(step((self.gathered, 0)))
        return runs

    def finish(self):
        for copy in self.sent:
            copy.wait_send()


def middle_kinds(count):
    bits, bit = [], 1
    while bit < count:
        bits.append(str(bit))
        bit *= 2
    return (("core","x","y","z"),("core","y","x","z"),("core","z","x","y"),("core","x","y","z"),("core","y","x","z"),("core","z","y","x"))


def chunk_rows(rows, chunks, count):
    unit = 128 * count
    units = rows // unit
    chunks = min(chunks, units)
    return [(units // chunks + (index < units % chunks)) * unit for index in range(chunks)]


def round_up(rows, count):
    unit = 128 * count
    return -(-rows // unit) * unit


def summing_scratch(kinds, rows, chunks, count):
    shapes = []
    for chunk, length in enumerate(chunk_rows(rows, chunks, count)):
        for kind in kinds[chunk % len(kinds)]:
            length //= level_size(kind, count)
            shapes.append(pltpu.VMEM((level_size(kind, count), length, 384), bf16))
    slots = 2 * sum(level_size(kind, count) for kind in kinds[0])
    return shapes + [pltpu.SemaphoreType.DMA((chunks, slots))] * 2


def make_summing(kinds, data, result, scratch, chunks, count):
    send_sem, recv_sem = scratch[-2:]
    levels = len(kinds[0])
    sums, first = [], 0
    for chunk, length in enumerate(chunk_rows(data.shape[0], chunks, count)):
        landings = scratch[levels * chunk : levels * (chunk + 1)]
        order = kinds[chunk % len(kinds)]
        sums.append(
            Summing(order, data, result, landings, send_sem, recv_sem, chunk, first, length, count)
        )
        first += length
    return sums


def greet_all(count):
    batch, frame, side, column, peer = place()
    core, across = lax.rem(batch, 2), lax.div(batch, 2)
    barrier = pltpu.get_barrier_semaphore()
    targets = [
        (batch + 1 - 2 * core, frame),
        (batch, peer),
        (core + 2 - 2 * across, frame),
        (core + 2 - 2 * across, peer),
    ]
    for step in range(1, count):
        targets.append((batch, 2 * lax.rem(column + step, count) + side))
    for target in targets:
        pl.semaphore_signal(barrier, inc=1, device_id=target, device_id_type=MESH)
    return len(targets)


TAIL_KINDS = (("core", "square", "z"), ("core", "z", "square"))
TAIL_CHUNKS = 2
MIDDLE_CHUNKS = 6
MIDDLE_TIMES = (0, 4, 16, 24, 30, 36, 44, 51, 56)
CHUNK_TIME = 0.9


def timed_steps(items):
    runs = [item.steps() for item in items]
    timed = []
    for step in range(len(runs[0])):
        for index, run in enumerate(runs):
            now = MIDDLE_TIMES[min(step, len(MIDDLE_TIMES) - 1)] + CHUNK_TIME * index
            timed.append((now, run[step]))
    return sorted(timed, key=lambda pair: pair[0])


def backward_kernel(
    frames,
    count,
    clip_count,
    clip_len,
    latents,
    time_embed,
    mod_rows,
    grad_attn_out,
    sums,
    weights,
    grad_att,
    attention,
    stats,
    mod_all,
    mod_peer,
    pairs,
    queries_in,
    w_qkv,
    spread_q,
    spread_o,
    sum_heads,
    grad_latents,
    tail_result,
    result,
    data,
    tail,
    grad_mod,
    grad_w,
    pack_out,
    pack_in,
    queries,
    grads,
    query_grad,
    key_grad,
    value_grad,
    flat_kv,
    part_out,
    part_in,
    peer_out,
    peer_in,
    held,
    held_mod,
    held_sem,
    load_sem,
    query_sem,
    send_sem,
    recv_sem,
    *scratch,
):
    batch, frame, side, column, peer = place()
    width = grad_att.shape[1]
    slots = part_out.shape[0]
    load = pltpu.make_async_copy(weights, data, load_sem)
    load.start()
    load_queries = pltpu.make_async_copy(queries_in, queries, query_sem)
    load_queries.start()
    head_size = width // HEADS

    def block_at(step):
        return jnp.where(step == count, column, nearest(count - step, column, count))

    def fetches(step):
        slot = lax.rem(step - 1, 2)
        block = block_at(step)
        return (
            pltpu.make_async_copy(pairs.at[block], held.at[slot], held_sem.at[slot]),
            pltpu.make_async_copy(mod_all.at[block], held_mod.at[slot], held_sem.at[2 + slot]),
        )

    def fetch(step):
        for copy in fetches(step):
            copy.start()

    def fetched(step):
        for copy in fetches(step):
            copy.wait()

    signals = greet_all(count)
    fetch(1)
    fetch(2)
    kinds = middle_kinds(count)
    levels = len(kinds[0])
    chunks = len(chunk_rows(data.shape[0], MIDDLE_CHUNKS, count))
    own = scratch[: levels * chunks + 2]
    items = make_summing(kinds, data, result, own, MIDDLE_CHUNKS, count)
    waiting = timed_steps(items)
    tail_items = make_summing(TAIL_KINDS, tail, tail_result, scratch[len(own) :], TAIL_CHUNKS, count)
    tail_waiting = [list(group) for group in zip(*(item.steps() for item in tail_items))]
    heads_done = [0]

    def advance():
        while waiting and waiting[0][0] <= heads_done[0]:
            waiting.pop(0)[1]()

    def to_peer(source, target, slot):
        return pltpu.make_async_remote_copy(
            src_ref=source,
            dst_ref=target,
            send_sem=send_sem.at[slot],
            recv_sem=recv_sem.at[slot],
            device_id=(batch, peer),
            device_id_type=MESH,
        )

    def toward(step, owner):
        up = owner > column
        other = jnp.where(up, column + 1, column - 1)
        slot = jnp.where((other == owner) & jnp.logical_not(up), count, owner)
        return pltpu.make_async_remote_copy(
            src_ref=part_out.at[lax.rem(step, slots)],
            dst_ref=part_in.at[slot],
            send_sem=send_sem.at[2 + step],
            recv_sem=recv_sem.at[2 + slot],
            device_id=(batch, 2 * other + side),
            device_id_type=MESH,
        )

    def arrived(slot):
        pltpu.make_async_remote_copy(
            src_ref=part_out.at[0],
            dst_ref=part_in.at[slot],
            send_sem=send_sem.at[2],
            recv_sem=recv_sem.at[2 + slot],
            device_id=(batch, peer),
            device_id_type=MESH,
        ).wait_recv()

    def pass_on(step):
        block = block_at(step)
        arrived(block)
        slot = lax.rem(step, slots)
        part_out[slot] = (part_out[slot].astype(f32) + part_in[block].astype(f32)).astype(bf16)
        toward(step, block).start()

    def chain_kind(step):
        block = block_at(step)
        up = block > column
        begins = jnp.where(up, column == 0, column == count - 1)
        late = jnp.where(column < count // 2, up, jnp.logical_not(up))
        return begins, late

    def pass_late(step):
        begins, late = chain_kind(step)

        @pl.when(jnp.logical_not(begins) & late)
        def _():
            pass_on(step)

    grad_now = grad_att[...]
    product = grad_now.astype(f32) * attention[...].astype(f32)
    high, middle, low = pieces(product)
    delta = (
        dg(high, sum_heads[...], NN) + dg(middle, sum_heads[...], NN) + dg(low, sum_heads[...], NN)
    )
    high, middle, low = (piece.astype(f32) for piece in pieces(-delta))
    which = lax.rem(lax.broadcasted_iota(jnp.int32, delta.shape, 1), 3)
    extra = jnp.where(which == 0, high, jnp.where(which == 1, middle, low))
    pack_out[:, :width] = grad_now
    pack_out[:, width:] = stats[...] + extra.astype(bf16)
    swap = to_peer(pack_out, pack_in, 0)
    load.wait()
    met(signals)
    swap.start()
    advance()
    query_grad[...] = jnp.zeros_like(query_grad)

    def prepare(half, source):
        rows = pl.ds(half * frames, frames)
        wide = dg(source, spread_o[...], NN)
        extra = dg(source[:, width:], spread_q[...], NN).astype(bf16)
        wide = wide.astype(bf16)
        for head in range(HEADS):
            lanes = slice(head * LANES, (head + 1) * LANES)
            grads[head, rows, :] = wide[:, lanes]
            queries[head, rows, :] += extra[:, lanes]

    def differentiate(half, slot, first, moving=True):
        rows = pl.ds(half * frames, frames)
        for head in range(HEADS):
            key, value = held[slot, 0, head], held[slot, 1, head]
            query, grad = queries[head, rows, :], grads[head, rows, :]
            probs = jnp.exp(dg(key, query, NT))
            dscore = (probs * dg(value, grad, NT)).astype(bf16)
            probs = probs.astype(bf16)
            more_k, more_v = dg(dscore, query, NN), dg(probs, grad, NN)
            if first:
                key_grad[slot, head] = more_k
                value_grad[slot, head] = more_v
            else:
                key_grad[slot, head] += more_k
                value_grad[slot, head] += more_v
            query_grad[head, :, rows] += dg(key, dscore, TN)
            if moving:
                heads_done[0] += 1
                advance()

    def finish_keys(slot):
        for kind, source in enumerate((key_grad, value_grad)):
            for pair in range(HEADS // 2):
                start = kind * width + pair * LANES
                flat_kv[:, start : start + LANES] = jnp.concatenate(
                    [
                        source[slot, 2 * pair][:, :head_size],
                        source[slot, 2 * pair + 1][:, :head_size],
                    ],
                    axis=1,
                ).astype(bf16)
        flat = flat_kv[...]
        return dg(flat, w_qkv[:, width:], NT), dg(held_mod[slot], flat, TN)

    def finish_queries(half, source):
        rows = pl.ds(half * frames, frames)
        flat = jnp.concatenate(
            [query_grad[head, :head_size, rows] for head in range(HEADS)], axis=0
        )
        flat = (flat * 0.125).T.astype(bf16)
        return dg(flat, w_qkv[:, :width], NT), dg(source, flat, TN)

    def send_block(step, slot, first):
        block = block_at(step)
        part, weight = finish_keys(slot)
        if not isinstance(step, int):

            @pl.when(step > slots)
            def _():
                toward(step - slots, block_at(step - slots)).wait_send()

        part_out[lax.rem(step, slots)] = part.astype(bf16)
        if first is False:
            pass_late(step - 1)
        begins, late = chain_kind(step)

        @pl.when(begins)
        def _():
            toward(step, block).start()

        @pl.when(jnp.logical_not(begins) & jnp.logical_not(late))
        def _():
            pass_on(step)

        if first:
            grad_w[:, width:] = weight
        else:
            grad_w[:, width:] += weight

        @pl.when(step + 2 <= count)
        def _():
            fetch(step + 2)

    load_queries.wait()
    prepare(0, pack_out[...])
    fetched(1)
    differentiate(0, 0, True)
    fetched(2)
    differentiate(0, 1, True)
    swap.wait()
    prepare(1, pack_in[...])
    differentiate(1, 0, False)
    send_block(1, 0, True)
    differentiate(1, 1, False)
    send_block(2, 1, False)

    def per_block(step, moving):
        slot = (step - 1) % 2 if isinstance(step, int) else lax.rem(step - 1, 2)
        fetched(step)
        differentiate(0, slot, True, moving)
        differentiate(1, slot, False, moving)
        send_block(step, slot, False)

    if count <= 4:
        for step in range(3, count):
            per_block(step, True)
    else:

        def looped(step, unused):
            per_block(step, False)
            return unused

        lax.fori_loop(3, count, looped, 0)
    slot = (count - 1) % 2
    fetched(count)
    differentiate(1, slot, True)
    pass_late(count - 1)
    part, weight = finish_queries(1, mod_peer[...])
    peer_out[...] = part.astype(bf16)
    back = to_peer(peer_out, peer_in, 1)
    back.start()
    grad_w[:, :width] = weight
    differentiate(0, slot, False)
    part, weight = finish_keys(slot)
    grad_w[:, width:] += weight
    mine, weight = finish_queries(0, held_mod[slot])
    grad_w[:, :width] += weight
    first = 0
    for part_index in range(3):
        tail[first : first + width, :] = grad_w[
            :, part_index * width : (part_index + 1) * width
        ].astype(bf16)
        first += width
    tail_waiting[0].pop(0)()
    grad_mod[...] = part + mine

    choice = row_choice(clip_ids(clip_len, clip_count, frame * frames, (frames, 16)), clip_count)
    ids = clip_ids(clip_len, clip_count, frame * frames, (frames, 16))
    lane = lax.broadcasted_iota(jnp.int32, (frames, 16), 1)
    members = ((lane == batch * clip_count + ids) & (ids < clip_count)).astype(f32).astype(bf16)
    normed, inverse = layer_norm(latents[...].astype(f32))
    scale = 1.0 + dg(choice, mod_rows[:, width : 2 * width], NN)
    first += 32
    for part in range(5):
        tail[first : first + 16, :] = sums[part].astype(bf16)
        first += 16
    time_low = time_embed[...].astype(f32)
    time_low = time_low / (1.0 + jnp.exp(-time_low))
    repeated = jnp.concatenate([time_low] * (16 // clip_count), axis=0)
    row = lax.broadcasted_iota(jnp.int32, (16, width), 0)
    mine = (lax.div(row, clip_count) == batch) & (frame == 0)
    tail[first : first + 16, :] = jnp.where(mine, repeated, 0.0).astype(bf16)
    first += 16
    tail[first:, :] = jnp.zeros((tail.shape[0] - first, width), bf16)

    @pl.when(column > 0)
    def _():
        arrived(column)
        grad_mod[...] += part_in[column].astype(f32)

    @pl.when(column < count - 1)
    def _():
        arrived(count)
        grad_mod[...] += part_in[count].astype(f32)

    back.wait()
    total = grad_mod[...] + peer_in[...].astype(f32)
    grad_latents[...] = (
        grad_attn_out[...] + norm_back(total * scale, normed, inverse)
    ).astype(bf16)
    first = 3 * width
    tail[first : first + 16, :] = clip_sums(members, total).astype(bf16)
    tail[first + 16 : first + 32, :] = clip_sums(members, total * normed).astype(bf16)

    for run in tail_waiting.pop(0):
        run()
    while waiting or tail_waiting:
        for unused in range(-(-len(waiting) // max(1, len(tail_waiting)))):
            waiting.pop(0)[1]()
        if tail_waiting:
            for run in tail_waiting.pop(0):
                run()

    def sent(step, unused):
        toward(step, block_at(step)).wait_send()
        return unused

    lax.fori_loop(max(1, count - slots), count, sent, 0)
    for item in items + tail_items:
        item.finish()


def backward_attention(clip_len, *given, count):
    latents, weights = given[0], given[5]
    frames, width = latents.shape
    slots = min(count, 4)
    tail_rows = round_up(3 * width + 8 * 16, count)
    vmem = pl.BlockSpec(memory_space=pltpu.VMEM)
    anywhere = pl.BlockSpec(memory_space=pl.ANY)
    specs = [vmem] * 5 + [anywhere] + [vmem] * 3 + [anywhere, vmem] + [anywhere] * 2 + [vmem] * 4
    return pl.pallas_call(
        functools.partial(backward_kernel, frames, count, clip_len.shape[1]),
        name="attention_backward",
        out_shape=(
            jax.ShapeDtypeStruct((frames, width), bf16),
            jax.ShapeDtypeStruct((tail_rows, width), bf16),
            jax.ShapeDtypeStruct(weights.shape, bf16),
        ),
        in_specs=[pl.BlockSpec(memory_space=pltpu.SMEM)] + specs,
        out_specs=(vmem,) * 3,
        scratch_shapes=[
            pltpu.VMEM(weights.shape, bf16),
            pltpu.VMEM((tail_rows, width), bf16),
            pltpu.VMEM((frames, width), f32),
            pltpu.VMEM((width, 3 * width), f32),
            pltpu.VMEM((frames, width + LANES), bf16),
            pltpu.VMEM((frames, width + LANES), bf16),
            pltpu.VMEM((HEADS, 2 * frames, LANES), bf16),
            pltpu.VMEM((HEADS, 2 * frames, LANES), bf16),
            pltpu.VMEM((HEADS, LANES, 2 * frames), f32),
            pltpu.VMEM((2, HEADS, frames, LANES), f32),
            pltpu.VMEM((2, HEADS, frames, LANES), f32),
            pltpu.VMEM((frames, 2 * width), bf16),
            pltpu.VMEM((slots, frames, width), bf16),
            pltpu.VMEM((count + 1, frames, width), bf16),
            pltpu.VMEM((frames, width), bf16),
            pltpu.VMEM((frames, width), bf16),
            pltpu.VMEM((2, 2, HEADS, frames, LANES), bf16),
            pltpu.VMEM((2, frames, width), bf16),
            pltpu.SemaphoreType.DMA((4,)),
            pltpu.SemaphoreType.DMA,
            pltpu.SemaphoreType.DMA,
            pltpu.SemaphoreType.DMA((2 + count,)),
            pltpu.SemaphoreType.DMA((3 + count,)),
        ]
        + summing_scratch(middle_kinds(count), weights.shape[0], MIDDLE_CHUNKS, count)
        + summing_scratch(TAIL_KINDS, tail_rows, TAIL_CHUNKS, count),
        compiler_params=pltpu.CompilerParams(
            collective_id=2, has_side_effects=True, vmem_limit_bytes=63 * 2**20
        ),
    )(clip_len, *given)


def spread_kernel(width, shapes, weights, tail, *refs):
    outs, (low, rows) = refs[: len(shapes)], refs[len(shapes) : len(shapes) + 2]
    stages, (load_sem, store_sem) = refs[len(shapes) + 2 : -2], refs[-2:]
    total = weights.shape[0]
    piece = 512
    loads = [pltpu.make_async_copy(tail, rows, load_sem.at[0])] + [
        pltpu.make_async_copy(
            weights.at[pl.ds(first, piece)], low.at[pl.ds(first, piece)], load_sem.at[1 + index]
        )
        for index, first in enumerate(range(0, total, piece))
    ]
    held = [0]

    def need(end):
        while held[0] * piece < end:
            held[0] += 1
            loads[held[0]].wait()

    for load in loads:
        load.start()
    stores = [
        pltpu.make_async_copy(stage, out, store_sem.at[index])
        for index, (stage, out) in enumerate(zip(stages, outs))
    ]
    ada, qkv, down, up, co, ckv, cq, ao, bias, gain = range(10)
    loads[0].wait()
    first = 3 * width
    marks = [rows[first + 16 * part : first + 16 * (part + 1), :] for part in range(8)]
    for part in range(6):
        here = slice(part * width, (part + 1) * width)
        stages[ada][:, here] = dg(marks[7], marks[part], TN)
        stages[bias][here] = jnp.sum(marks[part].astype(f32), axis=0)
    stages[gain][...] = jnp.sum(marks[6].astype(f32), axis=0)
    stores[ada].start()
    stores[bias].start()
    stores[gain].start()
    for part in range(3):
        stages[qkv][:, part * width : (part + 1) * width] = rows[
            part * width : (part + 1) * width, :
        ].astype(f32)
    stores[qkv].start()
    first = 0
    for part in range(shapes[down][0] // width):
        here = slice(part * width, (part + 1) * width)
        need(first + 2 * width)
        stages[down][here, :] = low[first : first + width, :].astype(f32)
        first += width
        stages[up][:, here] = low[first : first + width, :].astype(f32)
        first += width
    stores[down].start()
    stores[up].start()
    for index in (co, ckv, cq, ao):
        length = shapes[index][0]
        for part in range(shapes[index][1] // width):
            here = slice(part * width, (part + 1) * width)
            need(first + length)
            stages[index][:, here] = low[first : first + length, :].astype(f32)
            first += length
        stores[index].start()
    need(total)
    for store in stores:
        store.wait()


def spread_weights(weights, tail, text_width, hidden_width):
    width = weights.shape[1]
    square = (width, width)
    shapes = [
        (width, 6 * width),
        (width, 3 * width),
        (hidden_width, width),
        (width, hidden_width),
        square,
        (text_width, 2 * width),
        square,
        square,
        (6 * width,),
        (width,),
    ]
    anywhere = pl.BlockSpec(memory_space=pl.ANY)
    return pl.pallas_call(
        functools.partial(spread_kernel, width, shapes),
        name="weight_gradients",
        out_shape=[jax.ShapeDtypeStruct(shape, f32) for shape in shapes],
        in_specs=[anywhere] * 2,
        out_specs=[anywhere] * len(shapes),
        scratch_shapes=[pltpu.VMEM(weights.shape, bf16), pltpu.VMEM(tail.shape, bf16)]
        + [pltpu.VMEM(shape, f32) for shape in shapes]
        + [pltpu.SemaphoreType.DMA((1 + weights.shape[0] // 512,)), pltpu.SemaphoreType.DMA((len(shapes),))],
        compiler_params=pltpu.CompilerParams(vmem_limit_bytes=62 * 2**20),
    )(weights, tail)


def spread_matrices(width):
    head_size = width // HEADS
    lane = np.arange(HEADS * LANES, dtype=np.int32)[None, :]
    head, inner = lane // LANES, lane % LANES
    row = np.arange(LANES, dtype=np.int32)[:, None]
    spread_q = (row < 3 * HEADS) & (head == row // 3) & (inner == head_size + 4 + row % 3)
    row = np.arange(width, dtype=np.int32)[:, None]
    spread_o = [(head == row // head_size) & (inner == row % head_size)]
    row = np.arange(LANES, dtype=np.int32)[:, None] - 3 * HEADS
    spread_o.append((row >= 0) & (head == row // 3) & (inner == head_size + row % 3))
    column = np.arange(LANES, dtype=np.int32)[None, :] - 3 * HEADS
    sum_heads = np.arange(width, dtype=np.int32)[:, None] // head_size == column // 3
    return (
        spread_q.astype(bf16),
        np.concatenate(spread_o, axis=0).astype(bf16),
        sum_heads.astype(bf16),
    )


def per_device(
    latents,
    time_embed,
    text_states,
    text_len,
    clip_len,
    cotangent,
    w_ada,
    b_ada,
    w_qkv,
    w_ao,
    gain_cross,
    w_cq,
    w_ckv,
    w_co,
    w_up,
    w_down,
):
    frames = latents.shape[1]
    width = latents.shape[2]
    clip_count = time_embed.shape[1]
    text_slots = text_states.shape[2]
    count = lax.axis_size("frame") // 2
    attention, stats, mod_rows, mod_all, mod_peer, pairs, queries = forward_attention(
        clip_len, latents[0], time_embed[0], w_ada, b_ada, w_qkv, count
    )
    text_rows = text_states[0].reshape(clip_count * text_slots, text_states.shape[3])
    mixed, grad_attention, grad_attn_out, sums, weights = middle_part(
        clip_len,
        text_len,
        latents[0],
        cotangent[0],
        attention,
        mod_rows,
        text_rows,
        gain_cross,
        w_ao,
        w_cq,
        w_ckv,
        w_co,
        w_up,
        w_down,
        count=count,
    )

    grad_latents, tail, weights = backward_attention(
        clip_len,
        latents[0],
        time_embed[0],
        mod_rows,
        grad_attn_out,
        sums,
        weights,
        grad_attention,
        attention,
        stats,
        mod_all,
        mod_peer,
        pairs,
        queries,
        w_qkv,
        *spread_matrices(width),
        count=count,
    )
    ada, qkv, down, up, co, ckv, cq, ao, bias, gain = spread_weights(
        weights, tail, text_rows.shape[1], w_up.shape[1]
    )
    grads = (ada, bias, qkv, ao, gain, cq, ckv, co, up, down)
    return (mixed[None], grad_latents[None]) + grads


def solution(mesh):
    placed = (
        P("batch", "frame", None),
        P("batch", None, None),
        P("batch", None, None, None),
        P("batch", None),
        P("batch", None),
        P("batch", "frame", None),
    ) + (P(),) * 10
    return jax.shard_map(
        per_device,
        mesh=mesh,
        in_specs=placed,
        out_specs=(P("batch", "frame", None), P("batch", "frame", None)) + (P(),) * 10,
        check_vma=False,
    )
```
